32 devices in a mesh: exp: 8 (over y, x, core), tp: 4 (over z).
Axes of the slice: x: 2, y: 2, z: 4, core: 2. Of those that a mesh axis runs over, the one named last changes fastest.
Arguments:
- tokens: bfloat16 [8192, 1024], P(('exp', 'tp')), may hold values from -6 to 6
- norm1_gain: float32 [1024], replicated, may hold values from 0.5 to 1.5
- w_query: bfloat16 [1024, 1024], P(None, 'tp'), may hold values from -0.1875 to 0.1875
- w_key_value: bfloat16 [1024, 8, 128], P(None, 'tp'), may hold values from -0.1875 to 0.1875
- w_out: bfloat16 [1024, 1024], P('tp'), may hold values from -2 to 2
- norm2_gain: float32 [1024], replicated, may hold values from 0.5 to 1.5
- w_router: bfloat16 [1024, 32], replicated, may hold values from -0.09375 to 0.09375
- w_gate_up: bfloat16 [32, 1024, 1024], P('exp'), may hold values from -0.1875 to 0.1875
- w_down: bfloat16 [32, 512, 1024], P('exp'), may hold values from -0.75 to 0.75
- routes: int32 [8192, 8], P(('exp', 'tp')), may hold values from 0 to 31, all different within a row; in each aligned block of 256 rows (0 to 255, 256 to 511, ...) at most 80 rows name the same one
- prefix: int32 [8], P('exp'), may hold values from 102 to 512
- cotangent: bfloat16 [8192, 1024], P(('exp', 'tp')), may hold values from -6 to 6
Outputs:
- layer_out: bfloat16 [8192, 1024], P(('exp', 'tp'))
- input_grad: float32 [8192, 1024], P(('exp', 'tp'))
- norm1_grad: float32 [1024], replicated
- query_grad: float32 [1024, 1024], P(None, 'tp')
- key_value_grad: float32 [1024, 8, 128], P(None, 'tp')
- out_grad: float32 [1024, 1024], P('tp')
- norm2_grad: float32 [1024], replicated
- router_grad: float32 [1024, 32], replicated
- gate_up_grad: float32 [32, 1024, 1024], P('exp')
- down_grad: float32 [32, 512, 1024], P('exp')
The draws below stay inside these ranges and needn't reach their ends.
Inputs may be any that keep to these rules, and one draw needn't show every extreme that they name: `routes`: each row names 8 different experts; in each aligned block of 256 rows (the rows of one device) no expert is named by more than 80 rows, a bound that some block reaches.
All inputs are finite; a program needn't handle non-finite values.
Results may differ from the reference program's by a relative error of at most 0.024.
Values may be sent and summed in bfloat16 or wider, within the bound.
A program may use at most 192 MiB of HBM per device.

```python
import math
import jax
import jax.numpy as jnp
import numpy as np
from jax import lax

D = 1024
H = 16
KVH = 8
HD = 64
FF = 512
EXPERTS = 32
TOP = 8
SEQ_LEN = 1024
SEQ_DEV = 1
SEQS = 8
TOK_GRP = 1024
TOKENS = 8192
ROWS_DEV = 256
CAP = 80
N_EXP = 8
N_TP = 4


def plant(entries, rng, smallest, high):
    index_at = [jax.random.randint(jax.random.fold_in(rng, axis), (), 0, length) for axis, length in enumerate(entries.shape)]
    longest = entries.shape.index(max(entries.shape))
    next_to = index_at[:longest] + [(index_at[longest] + 1) % entries.shape[longest]] + index_at[longest + 1:]
    return entries.at[tuple(index_at)].set(smallest).at[tuple(next_to)].set(high)


def block_levels(key, dims, cuts, low, high):
    loudness, own = 1.0, jax.random.fold_in(key, 6)
    for dim, blocks in cuts:
        steps = jnp.exp(jax.random.uniform(jax.random.fold_in(own, dim), (blocks,), jnp.float32, low / len(cuts), high / len(cuts)))
        loudness = loudness * jnp.repeat(steps, dims[dim] // blocks).reshape([-1 if axis == dim else 1 for axis in range(len(dims))])
    return loudness


def routed_block(own_key, own, number, rows, count, top, most, slope):
    order = jax.random.permutation(own_key, count)
    crowded, ordinary = portions_of(count, rows * top, most, slope, True), portions_of(count, rows * top, most, slope, False)
    places = jnp.arange(count)

    def named(sizes, turn):
        used = int((sizes > 0).sum())
        fixed = max(1, used // 4)
        passed = fixed + (places - fixed + turn * (used - fixed)) % max(1, count - fixed)
        return jnp.zeros((count,), jnp.int32).at[order[jnp.where(places < fixed, places, passed)]].set(jnp.asarray(sizes, jnp.int32))

    sizes = jnp.where(number % 4 == 0, named(crowded, number // 4), named(ordinary, number - number // 4 - 1))
    mixed = jax.random.permutation(jax.random.fold_in(own, 3), count)
    giver, sink = mixed[0:count // 2 * 2:2], mixed[1:count // 2 * 2:2]
    room = jnp.minimum(sizes[giver] - 1, most - sizes[sink]) // 2
    room = jnp.where((giver == order[0]) | (sink == order[0]) | (sizes[sink] == 0), 0, jnp.maximum(room, 0))
    passed = jax.random.randint(jax.random.fold_in(own, 4), (count // 2,), 0, 1 << 20) % (room + 1)
    sizes = sizes.at[giver].add(-passed).at[sink].add(passed)
    labels = jnp.searchsorted(jnp.cumsum(sizes), jnp.arange(rows * top), side="right").astype(jnp.int32)
    listing = labels.reshape(top, rows).T
    listing = listing[jax.random.permutation(jax.random.fold_in(own, 1), rows)]
    turn = jax.random.randint(jax.random.fold_in(own, 2), (rows, 1), 0, top)
    return jnp.take_along_axis(listing, (jnp.arange(top)[None, :] + turn) % top, axis=1)


def portions_of(count, total, reach, skew, full):
    portions = [(1 << 20) // math.isqrt(standing ** skew) + 1 for standing in range(1, count + 1)]
    largest = reach if full else min(reach, max(-(-total // count), total * portions[0] // sum(portions)))
    least = 1 if total - largest >= count - 1 else 0
    counts, spare = [largest] + [least] * (count - 1), total - largest - least * (count - 1)
    while spare > 0:
        candidates = [i for i in range(1, count) if counts[i] < largest] or [i for i in range(1, count) if counts[i] < reach]
        pool, budget = sum([portions[i] for i in candidates]), spare
        for i in candidates:
            addition = min(reach - counts[i], max(1, budget * portions[i] // pool), spare)
            counts[i] = counts[i] + addition
            spare = spare - addition
    return np.array(counts)


def centred(rng, dims, spread, bound, pieces=(), kind=jnp.bfloat16):
    level = block_levels(rng, dims, pieces, -0.22, 0.18) if pieces else 1.0
    array = jax.random.normal(rng, dims, jnp.float32) * spread * level
    return jnp.minimum(jnp.maximum(array, -bound), bound).astype(kind)


def setup_inputs(seed: int = 0) -> dict:
    key_list = jax.random.split(jax.random.key(seed), 13)
    tokens = centred(key_list[0], (TOKENS, D), 1.0, 6.0, ((0, 32),))
    norm1_gain = jnp.clip(1.0 + 0.1 * jax.random.normal(key_list[1], (D,), jnp.float32), 0.5, 1.5)
    w_query = centred(key_list[2], (D, H * HD), D ** -0.5, 0.1875, ((1, 4),))
    w_key_value = centred(key_list[3], (D, KVH, 2 * HD), D ** -0.5, 0.1875, ((1, 4),))
    w_out = centred(key_list[4], (H * HD, D), (H * HD * 8 // SEQ_LEN) ** -0.5, 2.0, ((0, 4),))
    norm2_gain = jnp.clip(1.0 + 0.1 * jax.random.normal(key_list[5], (D,), jnp.float32), 0.5, 1.5)
    w_router = centred(key_list[6], (D, EXPERTS), (4 * D) ** -0.5, 0.09375)
    w_gate_up = centred(key_list[7], (EXPERTS, D, 2 * FF), D ** -0.5, 0.1875, ((0, 8),))
    w_down = centred(key_list[8], (EXPERTS, FF, D), (FF // 8) ** -0.5, 0.75, ((0, 8),))
    routes_keys = jax.random.split(jax.random.fold_in(key_list[9], 1), TOKENS // ROWS_DEV)
    routes_turns = jax.random.permutation(jax.random.fold_in(key_list[9], 3), TOKENS // ROWS_DEV)
    routes = jax.vmap(lambda own, number: routed_block(jax.random.fold_in(key_list[9], 2), own, number, ROWS_DEV, EXPERTS, TOP, CAP, 2))(routes_keys, routes_turns).reshape((TOKENS, TOP))
    prefix = plant(jax.random.randint(key_list[10], (SEQS,), SEQ_LEN // 10, SEQ_LEN // 2 + 1), jax.random.fold_in(key_list[10], 1), SEQ_LEN // 10, (SEQ_LEN // 2 + 1) - 1).astype(jnp.int32)
    cotangent = centred(key_list[11], (TOKENS, D), 1.0, 6.0, ((0, 32),))
    return {"tokens": tokens, "norm1_gain": norm1_gain, "w_query": w_query, "w_key_value": w_key_value, "w_out": w_out, "norm2_gain": norm2_gain, "w_router": w_router, "w_gate_up": w_gate_up, "w_down": w_down, "routes": routes, "prefix": prefix, "cotangent": cotangent}


epsilon = 1e-06
masked_score = -1e+30
highest = lax.Precision.HIGHEST

@jax.custom_vjp
def low(v):
    return lax.optimization_barrier(v.astype(jnp.bfloat16)).astype(jnp.float32)

@jax.custom_vjp
def low_back(v):
    return v

def low_keep(v):
    return (low(v), None)

def low_pass(kept, grad):
    return (grad,)

def back_keep(v):
    return (v, None)

def back_low(kept, grad):
    return (low(grad),)
low.defvjp(low_keep, low_pass)
low_back.defvjp(back_keep, back_low)

def rms_scale(values, gain_vector):
    inverse = lax.rsqrt(lax.optimization_barrier(jnp.mean(values * values, axis=-1, keepdims=True)) + epsilon)
    return values * inverse * gain_vector

def sequence_attention(normed, prefix_len, w_query, w_key_value, w_out):
    length = normed.shape[0]
    head_groups = H // KVH
    queries = low(low_back(jnp.dot(normed, w_query, precision=highest)))
    queries = queries.reshape(length, KVH, head_groups, HD)
    key_value = low(low_back(jnp.einsum('td,dhf->thf', normed, w_key_value, precision=highest)))
    key_part = key_value[:, :, :HD]
    value_part = key_value[:, :, HD:]
    scores = jnp.einsum('qhgd,khd->hgqk', queries, key_part, precision=highest) * HD ** (-0.5)
    scores = low_back(scores)
    row_ids = jnp.arange(length, dtype=jnp.int32)[:, None]
    col_ids = jnp.arange(length, dtype=jnp.int32)[None, :]
    visible = (col_ids <= row_ids) | (col_ids < prefix_len)
    scores = jnp.where(visible, scores, masked_score)
    probs = jax.nn.softmax(scores, axis=-1)
    mixed = jnp.einsum('hgqk,khd->qhgd', low(probs), value_part, precision=highest)
    mixed = low(low_back(mixed.reshape(length, H * HD)))
    return jnp.dot(mixed, w_out, precision=highest)

def expert_mixture(normed_moe, gate_weights, route_group, gate_up, down_proj):
    assign_count = TOK_GRP * TOP
    slot_count = N_TP * CAP
    flat_routes = route_group.reshape(assign_count)
    onehot = (flat_routes[:, None] == jnp.arange(EXPERTS, dtype=jnp.int32)[None, :]).astype(jnp.int32)
    before = jnp.cumsum(onehot, axis=0) - onehot
    position = lax.optimization_barrier(jnp.sum(before * onehot, axis=1)).astype(jnp.int32)
    slot_index = (flat_routes * slot_count + position).astype(jnp.int32)
    sources = jnp.full((EXPERTS * slot_count,), TOK_GRP, jnp.int32)
    sources = sources.at[slot_index].set(jnp.arange(assign_count, dtype=jnp.int32) // TOP)
    padded = jnp.concatenate([normed_moe, jnp.zeros((1, D), jnp.float32)], axis=0)
    inputs = low_back(padded[sources].reshape(EXPERTS, slot_count, D))
    units = low_back(jnp.einsum('esd,edf->esf', inputs, gate_up, precision=highest))
    active = low(jax.nn.silu(units[:, :, :FF]) * units[:, :, FF:])
    outputs = low(low_back(jnp.einsum('esf,efd->esd', active, down_proj, precision=highest)))
    picked = outputs.reshape(EXPERTS * slot_count, D)[slot_index].reshape(TOK_GRP, TOP, D)
    return lax.optimization_barrier(jnp.sum(gate_weights[:, :, None] * picked, axis=1))

def group_layer(params, token_group, route_group, prefix_group):
    norm1_gain, w_query, w_key_value, w_out, norm2_gain, w_router, gate_up, down_proj = params
    normed = low(rms_scale(token_group, norm1_gain))
    seq_normed = normed.reshape(SEQ_DEV, SEQ_LEN, D)
    attend = jax.checkpoint(sequence_attention)

    def one_sequence(sequence_item):
        return attend(sequence_item[0], sequence_item[1], w_query, w_key_value, w_out)
    attended = lax.map(one_sequence, (seq_normed, prefix_group)).reshape(TOK_GRP, D)
    hidden = token_group + low_back(attended)
    normed_moe = low(rms_scale(hidden, norm2_gain))
    logits = low_back(jnp.dot(normed_moe, w_router, precision=highest))
    chosen = jnp.take_along_axis(logits, route_group, axis=1)
    gate_weights = jax.nn.softmax(chosen, axis=-1)
    mixture = expert_mixture(normed_moe, gate_weights, route_group, gate_up, down_proj)
    return hidden + mixture

def reference(tokens, norm1_gain, w_query, w_key_value, w_out, norm2_gain, w_router, w_gate_up, w_down, routes, prefix, cotangent):
    params = (norm1_gain, w_query.astype(jnp.float32), w_key_value.astype(jnp.float32), w_out.astype(jnp.float32), norm2_gain, w_router.astype(jnp.float32), w_gate_up.astype(jnp.float32), w_down.astype(jnp.float32))
    token_groups_routes = routes.reshape(N_EXP, TOK_GRP, TOP)
    prefix_groups = prefix.reshape(N_EXP, SEQ_DEV)
    group_step = jax.checkpoint(group_layer)

    def layer_forward(token_values, param_values):
        token_groups = token_values.reshape(N_EXP, TOK_GRP, D)

        def scan_step(carried, group_item):
            return (carried, group_step(param_values, group_item[0], group_item[1], group_item[2]))
        start = jnp.zeros((), jnp.float32)
        unused, layer_values = lax.scan(scan_step, start, (token_groups, token_groups_routes, prefix_groups))
        return layer_values.reshape(TOKENS, D)
    layer_values, pullback = jax.vjp(layer_forward, tokens.astype(jnp.float32), params)
    input_grad, param_grads = pullback(cotangent.astype(jnp.float32))
    return (layer_values.astype(jnp.bfloat16), input_grad, param_grads[0], param_grads[1], param_grads[2], param_grads[3], param_grads[4], param_grads[5], param_grads[6], param_grads[7])
```

```python
import functools

import jax
import jax.numpy as jnp
from jax import lax
from jax.experimental import pallas as pl
from jax.experimental.pallas import tpu as pltpu
from jax.sharding import PartitionSpec as P

D = 1024
H = 16
KVH = 8
HD = 64
FF = 512
LANES = 128
XW = D + LANES
GROUP = 4

EPS = 1e-06
MASKED = -1e30
MESH = pl.DeviceIdType.MESH
BF = jnp.bfloat16
F32 = jnp.float32
VMEM = pltpu.VMEM
MIB = 1 << 20


def mm(a, b):
    return jnp.dot(a, b, preferred_element_type=F32)


def mm_nt(a, b):
    return lax.dot_general(a, b, (((1,), (1,)), ((), ())), preferred_element_type=F32)


def mm_tn(a, b):
    return lax.dot_general(a, b, (((0,), (0,)), ((), ())), preferred_element_type=F32)


def row_scaling(values):
    inverse = lax.rsqrt(jnp.mean(values * values, axis=-1, keepdims=True) + EPS)
    return values * inverse, inverse


def norm_backward(gradient, scaled, inverse, gain):
    weighted = gradient * gain
    inner = jnp.mean(weighted * scaled, axis=-1, keepdims=True)
    return inverse * (weighted - scaled * inner)


def block(ref, index, rows):
    return ref.at[pl.ds(pl.multiple_of(index * rows, rows), rows)]


def line_order(n):
    orders = []
    for z in range(n):
        right = list(range(n - 1, z, -1))
        left = list(range(z))
        first, second = (right, left) if len(right) >= len(left) else (left, right)
        order = []
        while first or second:
            if len(first) >= len(second):
                order.append(first.pop(0))
            else:
                order.append(second.pop(0))
        orders.append(order + [z])
    return orders


def lookup(table, z, j):
    value = jnp.int32(table[0][0])
    for a, row in enumerate(table):
        for b, entry in enumerate(row):
            value = jnp.where((z == a) & (j == b), jnp.int32(entry), value)
    return value


def greet_line(e, z, n):
    barrier = pltpu.get_barrier_semaphore()

    @pl.when(z > 0)
    def _():
        pl.semaphore_signal(barrier, inc=1, device_id=(e, z - 1), device_id_type=MESH)

    @pl.when(z < n - 1)
    def _():
        pl.semaphore_signal(barrier, inc=1, device_id=(e, z + 1), device_id_type=MESH)

    neighbours = jnp.where(z > 0, 1, 0) + jnp.where(z < n - 1, 1, 0)
    pl.semaphore_wait(barrier, neighbours)


def line_gather(e, z, n, rows, held, right_sems, left_sems, work):
    def copy(step, way):
        send, recv = right_sems if way > 0 else left_sems
        there = block(held, z - way * step, rows)
        return pltpu.make_async_remote_copy(
            src_ref=there,
            dst_ref=there,
            send_sem=send.at[step],
            recv_sem=recv.at[step],
            device_id=(e, z + way),
            device_id_type=MESH,
        )

    def arrived(step, way):
        send, recv = right_sems if way > 0 else left_sems
        there = block(held, z - way * step, rows)
        return pltpu.make_async_remote_copy(
            src_ref=there,
            dst_ref=there,
            send_sem=send.at[step],
            recv_sem=recv.at[step - 1],
            device_id=(e, z + way),
            device_id_type=MESH,
        )

    from_here = {1: z < n - 1, -1: z > 0}
    for way in (1, -1):

        @pl.when(from_here[way])
        def _():
            copy(0, way).start()

    work(z)
    for step in range(1, n):
        has = {1: z >= step, -1: z + step < n}
        for way in (1, -1):

            @pl.when(has[way])
            def _():
                arrived(step, way).wait_recv()

            @pl.when(has[way] & from_here[way])
            def _():
                copy(step, way).start()

        def one(way, carry):
            @pl.when(jnp.where(way > 0, has[-1], has[1]))
            def _():
                work(jnp.where(way > 0, z + step, z - step))

            return carry

        lax.fori_loop(0, 2, one, 0)

    def drain():
        for step in range(n - 1):
            has = {1: z >= step, -1: z + step < n}
            for way in (1, -1):

                @pl.when(has[way] & from_here[way])
                def _():
                    copy(step, way).wait_send()

    return drain


def line_scatter(e, z, n, sent, landed, sems, part, between=None):
    send, recv = sems
    table = line_order(n)

    def copy(way, slot):
        return pltpu.make_async_remote_copy(
            src_ref=sent.at[way, slot],
            dst_ref=landed.at[way, slot],
            send_sem=send.at[way, slot],
            recv_sem=recv.at[way, slot],
            device_id=(e, jnp.where(way == 0, z + 1, z - 1)),
            device_id_type=MESH,
        )

    def one(j, carry):
        d = lookup(table, z, j)
        way = jnp.where(d > z, 0, 1)
        slot = jnp.where(d > z, n - 1 - d, d)
        value = part(d)
        upstream = jnp.where(d > z, z > 0, z < n - 1)

        @pl.when(upstream)
        def _():
            copy(way, slot).wait_recv()
            sent[way, slot] = (value + landed[way, slot].astype(F32)).astype(BF)

        @pl.when(jnp.logical_not(upstream))
        def _():
            sent[way, slot] = value.astype(BF)

        copy(way, slot).start()
        return carry

    lax.fori_loop(0, n - 1, one, 0)
    own = part(z)
    if between is not None:
        between()

    def finish(total_ref):
        total_ref[...] = own

        @pl.when(z > 0)
        def _():
            copy(0, n - 1 - z).wait_recv()
            total_ref[...] += landed[0, n - 1 - z].astype(F32)

        @pl.when(z < n - 1)
        def _():
            copy(1, z).wait_recv()
            total_ref[...] += landed[1, z].astype(F32)

        for slot in range(n):

            @pl.when(slot < n - 1 - z)
            def _():
                copy(0, slot).wait_send()

            @pl.when(slot < z)
            def _():
                copy(1, slot).wait_send()

    return finish


def visible_mask(d, rows, length, prefix):
    row_ids = d * rows + lax.broadcasted_iota(jnp.int32, (rows, length), 0)
    col_ids = lax.broadcasted_iota(jnp.int32, (rows, length), 1)
    return (col_ids <= row_ids) | (col_ids < prefix)


def halves(pair, low):
    pair = pair.astype(F32)
    zero = jnp.zeros_like(pair)
    return jnp.where(low, pair, zero), jnp.where(low, pltpu.roll(pair, HD, 1), zero)


def attention_forward_kernel(
    n,
    tokens,
    gain1,
    w_query,
    w_pair,
    w_out,
    gain2,
    w_router,
    routes,
    prefix,
    hidden,
    ext,
    held,
    queries,
    pairs,
    mixed,
    totals,
    sent,
    landed,
    ag_rs,
    ag_rr,
    ag_ls,
    ag_lr,
    rs_s,
    rs_r,
):
    e, z = lax.axis_index("exp"), lax.axis_index("tp")
    rows = tokens.shape[0]
    length = rows * n
    kv_local = pairs.shape[1] // LANES
    low = lax.broadcasted_iota(jnp.int32, (rows, LANES), 1) < HD
    greet_line(e, z, n)
    scaled, _ = row_scaling(tokens[...].astype(F32))
    held[pl.ds(pl.multiple_of(z * rows, rows), rows)] = (scaled * gain1[...]).astype(BF)

    def project(d):
        at = pl.ds(pl.multiple_of(d * rows, rows), rows)
        normed = held[at]
        queries[at] = mm(normed, w_query[...]).astype(BF)
        pairs[at] = mm(normed, w_pair[...]).astype(BF)

    drain = line_gather(e, z, n, rows, held, (ag_rs, ag_rr), (ag_ls, ag_lr), project)

    def part(d):
        at = pl.ds(pl.multiple_of(d * rows, rows), rows)
        seen = visible_mask(d, rows, length, prefix[0])
        lane = lax.broadcasted_iota(jnp.int32, (rows, LANES), 1)
        stats = jnp.zeros((rows, LANES), F32)
        for kv in range(kv_local):
            span = slice(kv * LANES, (kv + 1) * LANES)
            pair = pairs[:, span]
            outs = []
            for h, head in enumerate(halves(queries[at, span], low)):
                scores = mm_nt((head * HD**-0.5).astype(BF), pair)
                scores = jnp.where(seen, scores, MASKED)
                top = jnp.max(scores, axis=-1, keepdims=True)
                grown = jnp.exp(scores - top)
                total = jnp.sum(grown, axis=-1, keepdims=True)
                probs = (grown / total).astype(BF)
                outs.append(mm(probs, pair))
                stats = jnp.where(lane == 2 * kv + h, top + jnp.log(total), stats)
            both = jnp.where(low, pltpu.roll(outs[0], HD, 1), outs[1])
            mixed[at, span] = both.astype(BF)
        totals[at] = stats
        return mm(mixed[at], w_out[...])

    finish = line_scatter(e, z, n, sent, landed, (rs_s, rs_r), part)
    finish(hidden)
    hid = tokens[...].astype(F32) + hidden[...]
    hidden[...] = hid
    scaled2, _ = row_scaling(hid)
    normed2 = (scaled2 * gain2[...]).astype(BF)
    ext[:, :D] = normed2
    experts = w_router.shape[1]
    logits = mm(normed2, w_router[...])
    lane = lax.broadcasted_iota(jnp.int32, (rows, experts), 1)
    chosen = lane == routes[:, 0:1]
    for k in range(1, routes.shape[1]):
        chosen = chosen | (lane == routes[:, k : k + 1])
    logits = jnp.where(chosen, logits, MASKED)
    grown = jnp.exp(logits - jnp.max(logits, axis=-1, keepdims=True))
    grown = jnp.where(chosen, grown, 0.0)
    gates = grown / jnp.sum(grown, axis=-1, keepdims=True)
    high = gates.astype(BF)
    low_part = (gates - high.astype(F32)).astype(BF)
    mask = jnp.where(chosen, 1.0, 0.0).astype(BF)
    pad = jnp.zeros((rows, LANES - 3 * experts), BF)
    ext[:, D:] = jnp.concatenate([high, low_part, mask, pad], axis=1)
    drain()


def attention_forward(n, tokens, gain1, w_query, w_pair, w_out, gain2, w_router, routes, prefix):
    rows = tokens.shape[0]
    length = rows * n
    qw, pw = w_query.shape[1], w_pair.shape[1]
    v = pl.BlockSpec(memory_space=VMEM)
    sem = pltpu.SemaphoreType.DMA
    return pl.pallas_call(
        functools.partial(attention_forward_kernel, n),
        out_shape=(
            jax.ShapeDtypeStruct((rows, D), F32),
            jax.ShapeDtypeStruct((rows, XW), BF),
            jax.ShapeDtypeStruct((length, D), BF),
            jax.ShapeDtypeStruct((length, qw), BF),
            jax.ShapeDtypeStruct((length, pw), BF),
            jax.ShapeDtypeStruct((length, qw), BF),
            jax.ShapeDtypeStruct((length, LANES), F32),
        ),
        in_specs=[v] * 8 + [pl.BlockSpec(memory_space=pltpu.SMEM)],
        out_specs=[v] * 7,
        scratch_shapes=[
            pltpu.VMEM((2, n, rows, D), BF),
            pltpu.VMEM((2, n, rows, D), BF),
            sem((n,)),
            sem((n,)),
            sem((n,)),
            sem((n,)),
            sem((2, n)),
            sem((2, n)),
        ],
        compiler_params=pltpu.CompilerParams(
            collective_id=1, has_side_effects=True, vmem_limit_bytes=48 * MIB
        ),
        cost_estimate=pl.CostEstimate(
            flops=2 * length * D * 4 * qw, bytes_accessed=300 * MIB, transcendentals=0
        ),
    )(tokens, gain1, w_query, w_pair, w_out, gain2, w_router, routes, prefix)


def slot_rows(rows, top_k, experts):
    capacity = rows * top_k * 5 // (experts * 4)
    return -(-capacity // 16) * 16


def selection(extra, first, local_experts, slots):
    rows = extra.shape[0]
    pick = lax.broadcasted_iota(jnp.int32, (8, LANES), 1) == (
        64 + first + lax.broadcasted_iota(jnp.int32, (8, LANES), 0)
    )
    named = mm_nt(jnp.where(pick, 1.0, 0.0).astype(BF), extra)
    earlier = lax.broadcasted_iota(jnp.int32, (rows, rows), 0) < lax.broadcasted_iota(
        jnp.int32, (rows, rows), 1
    )
    place = mm(named.astype(BF), jnp.where(earlier, 1.0, 0.0).astype(BF))
    place = jnp.where(named > 0.5, place, -1.0).astype(jnp.int32)
    slot = lax.broadcasted_iota(jnp.int32, (slots, rows), 0)
    parts = [
        jnp.where(slot == place[k : k + 1, :], 1.0, 0.0) for k in range(local_experts)
    ]
    return jnp.concatenate(parts, axis=0).astype(BF)


def own_gate(extra, expert):
    lane = lax.broadcasted_iota(jnp.int32, extra.shape, 1)
    mine = (lane == expert) | (lane == 32 + expert)
    return jnp.sum(jnp.where(mine, extra.astype(F32), 0.0), axis=-1, keepdims=True)


def sigmoid(v):
    return 1.0 / (1.0 + jnp.exp(-v))


def own_experts_kernel(
    n_exp,
    local_experts,
    ext,
    cot,
    cot_all,
    w_gate_up,
    w_down,
    hidden,
    w_router,
    gain2,
    layer_out,
    dhidden,
    dhidden_low,
    router_part,
    norm2_part,
    xg,
    cg,
    wgu,
    wd,
    sel,
    xs,
    cs,
    core_in,
    chip_out,
    chip_in,
    mix_core_in,
    mix_out,
    mix_in,
    total,
    cot_sem,
    w_sem,
    ag_s,
    ag_r,
    fw_s,
    fw_r,
    core_s,
    core_r,
    chip_s,
    chip_r,
    mcore_s,
    mcore_r,
    mchip_s,
    mchip_r,
):
    e, z = lax.axis_index("exp"), lax.axis_index("tp")
    rows = ext.shape[0]
    chips = n_exp // 2
    chip, core = e // 2, lax.rem(e, 2)
    partner = 2 * chip + 1 - core
    slots = sel.shape[1] // local_experts
    first = e * local_experts
    experts = w_router.shape[1]

    loads = [
        pltpu.make_async_copy(w_gate_up, wgu, w_sem.at[0]),
        pltpu.make_async_copy(w_down, wd, w_sem.at[1]),
    ]
    for b in range(n_exp):
        loads.append(pltpu.make_async_copy(cot_all.at[b, z], cg.at[b], cot_sem.at[b]))
    for load in loads:
        load.start()

    def there(k):
        return 2 * (chip ^ k) + core

    barrier = pltpu.get_barrier_semaphore()
    pl.semaphore_signal(barrier, inc=1, device_id=(partner, z), device_id_type=MESH)
    for k in range(1, chips):
        pl.semaphore_signal(barrier, inc=1, device_id=(there(k), z), device_id_type=MESH)
    xg[e] = ext[...]
    pl.semaphore_wait(barrier, chips)

    def push(k):
        return pltpu.make_async_remote_copy(
            src_ref=xg.at[e],
            dst_ref=xg.at[e],
            send_sem=ag_s.at[k],
            recv_sem=ag_r.at[k],
            device_id=(there(k), z),
            device_id_type=MESH,
        )

    def forward(k):
        return pltpu.make_async_remote_copy(
            src_ref=xg.at[there(k)],
            dst_ref=xg.at[there(k)],
            send_sem=fw_s.at[k],
            recv_sem=fw_r.at[k],
            device_id=(partner, z),
            device_id_type=MESH,
        )

    def pushed(k):
        return pltpu.make_async_remote_copy(
            src_ref=xg.at[there(k)],
            dst_ref=xg.at[there(k)],
            send_sem=ag_s.at[k],
            recv_sem=ag_r.at[k],
            device_id=(there(k), z),
            device_id_type=MESH,
        )

    def forwarded(k):
        b = 2 * (chip ^ k) + 1 - core
        return pltpu.make_async_remote_copy(
            src_ref=xg.at[b],
            dst_ref=xg.at[b],
            send_sem=fw_s.at[k],
            recv_sem=fw_r.at[k],
            device_id=(partner, z),
            device_id_type=MESH,
        )

    for k in range(1, chips):
        push(k).start()
    forward(0).start()
    for load in loads[2:]:
        load.wait()

    def gather(b):
        s = selection(xg[b, :, D:], first, local_experts, slots)
        sel[b] = s
        xs[b] = mm(s, xg[b]).astype(BF)
        cs[b] = mm(s, cg[b]).astype(BF)

    gather(e)
    for k in range(1, chips):
        pushed(k).wait_recv()
        forward(k).start()
    lax.fori_loop(1, chips, lambda k, c: (gather(there(k)), c)[1], 0)
    for k in range(chips):
        forwarded(k).wait_recv()
    lax.fori_loop(0, chips, lambda k, c: (gather(2 * (chip ^ k) + 1 - core), c)[1], 0)
    for load in loads[:2]:
        load.wait()
    for k in range(1, chips):
        push(k).wait_send()
    for k in range(chips):
        forward(k).wait_send()

    groups = n_exp // GROUP

    def expert_step(step, carry):
        k = step // groups
        b0 = lax.rem(step, groups) * GROUP
        at = pl.ds(pl.multiple_of(k * slots, slots), slots)
        wide = jnp.concatenate([xs[b0 + i, at] for i in range(GROUP)], axis=0)
        gate_value = own_gate(wide[:, D:], first + k)
        units = mm(wide[:, :D], wgu[k])
        gate, up = units[:, :FF], units[:, FF:]
        sig = sigmoid(gate)
        silu = gate * sig
        active = (silu * up).astype(BF)
        made = mm(active, wd[k]).astype(BF).astype(F32)
        upstream = jnp.concatenate([cs[b0 + i, at] for i in range(GROUP)], axis=0).astype(F32)
        dgate_value = jnp.sum(upstream * made, axis=-1, keepdims=True)
        share = (gate_value * made).astype(BF)
        dmade = (gate_value * upstream).astype(BF)
        dactive = mm_nt(dmade, wd[k])
        dgate = dactive * up * sig * (1.0 + gate * (1.0 - sig))
        dunits = jnp.concatenate([dgate, dactive * silu], axis=1).astype(BF)
        dx = mm_nt(dunits, wgu[k]).astype(BF)
        lane = lax.broadcasted_iota(jnp.int32, (GROUP * slots, LANES), 1)
        high = dgate_value.astype(BF).astype(F32)
        packed = jnp.where(lane == first + k, high, 0.0)
        packed = jnp.where(lane == 32 + first + k, dgate_value - high, packed).astype(BF)
        for i in range(GROUP):
            here = slice(i * slots, (i + 1) * slots)
            xs[b0 + i, at, :D] = share[here]
            xs[b0 + i, at, D:] = packed[here]
            cs[b0 + i, at] = dx[here]
        return carry

    lax.fori_loop(0, local_experts * groups, expert_step, 0)

    def other(k):
        return 2 * (chip ^ k) + 1 - core

    def core_copy(k, src, dst, s, r):
        return pltpu.make_async_remote_copy(
            src_ref=src.at[other(k)],
            dst_ref=dst.at[k],
            send_sem=s.at[k],
            recv_sem=r.at[k],
            device_id=(partner, z),
            device_id_type=MESH,
        )

    def chip_copy(k, src, dst, s, r):
        return pltpu.make_async_remote_copy(
            src_ref=src.at[k],
            dst_ref=dst.at[k],
            send_sem=s.at[k],
            recv_sem=r.at[k],
            device_id=(there(k), z),
            device_id_type=MESH,
        )

    def grads_of(b):
        s = sel[b]
        return jnp.concatenate([mm_tn(s, cs[b]), mm_tn(s, xs[b, :, D:])], axis=1)

    def each(count, body):
        lax.fori_loop(0, count, lambda i, c: (body(i), c)[1], 0)

    def give_grads(i):
        k = chips - 1 - i
        xg[other(k)] = grads_of(other(k)).astype(BF)
        core_copy(k, xg, core_in, core_s, core_r).start()

    def pass_grads(i):
        k = chips - 1 - i
        mine = grads_of(there(k))
        core_copy(k, xg, core_in, core_s, core_r).wait_recv()
        chip_out[k] = (mine + core_in[k].astype(F32)).astype(BF)
        chip_copy(k, chip_out, chip_in, chip_s, chip_r).start()

    def give_mix(i):
        k = chips - 1 - i
        cg[other(k)] = mm_tn(sel[other(k)], xs[other(k), :, :D]).astype(BF)
        core_copy(k, cg, mix_core_in, mcore_s, mcore_r).start()

    def pass_mix(i):
        k = chips - 1 - i
        mine = mm_tn(sel[there(k)], xs[there(k), :, :D])
        core_copy(k, cg, mix_core_in, mcore_s, mcore_r).wait_recv()
        mix_out[k] = (mine + mix_core_in[k].astype(F32)).astype(BF)
        chip_copy(k, mix_out, mix_in, mchip_s, mchip_r).start()

    each(chips, give_grads)
    each(chips - 1, pass_grads)
    each(chips, give_mix)
    each(chips - 1, pass_mix)
    total[...] = grads_of(e)
    core_copy(0, xg, core_in, core_s, core_r).wait_recv()
    total[...] += core_in[0].astype(F32)

    def take_grads(i):
        k = chips - 1 - i
        chip_copy(k, chip_out, chip_in, chip_s, chip_r).wait_recv()
        total[...] += chip_in[k].astype(F32)

    each(chips - 1, take_grads)
    extra = ext[:, D:].astype(F32)
    gates = extra[:, :experts] + extra[:, experts : 2 * experts]
    dgates = total[:, D : D + experts] + total[:, D + experts : D + 2 * experts]
    dlogits = gates * (dgates - jnp.sum(gates * dgates, axis=-1, keepdims=True))
    dlogits = dlogits.astype(BF)
    normed2 = ext[:, :D]
    router_part[...] = mm_tn(dlogits, normed2)
    dnormed2 = total[:, :D] + mm_nt(dlogits, w_router[...])
    scaled2, inverse2 = row_scaling(hidden[...])
    norm2_part[...] = jnp.broadcast_to(
        jnp.sum(dnormed2 * scaled2, axis=0, keepdims=True), norm2_part.shape
    )
    back = cot[...].astype(F32) + norm_backward(dnormed2, scaled2, inverse2, gain2[...])
    dhidden[...] = back
    dhidden_low[...] = back.astype(BF)

    total[:, :D] = hidden[...] + mm_tn(sel[e], xs[e, :, :D])
    core_copy(0, cg, mix_core_in, mcore_s, mcore_r).wait_recv()
    total[:, :D] += mix_core_in[0].astype(F32)

    def take_mix(i):
        k = chips - 1 - i
        chip_copy(k, mix_out, mix_in, mchip_s, mchip_r).wait_recv()
        total[:, :D] += mix_in[k].astype(F32)

    each(chips - 1, take_mix)
    layer_out[...] = total[:, :D].astype(BF)

    def sent_to_core(k):
        core_copy(k, xg, core_in, core_s, core_r).wait_send()
        core_copy(k, cg, mix_core_in, mcore_s, mcore_r).wait_send()

    def sent_to_chip(i):
        chip_copy(i + 1, chip_out, chip_in, chip_s, chip_r).wait_send()
        chip_copy(i + 1, mix_out, mix_in, mchip_s, mchip_r).wait_send()

    each(chips, sent_to_core)
    each(chips - 1, sent_to_chip)


def own_experts(n_exp, ext, cot, cot_all, w_gate_up, w_down, hidden, w_router, gain2, slots):
    rows = ext.shape[0]
    local_experts = w_gate_up.shape[0]
    experts = w_router.shape[1]
    chips = n_exp // 2
    v = pl.BlockSpec(memory_space=VMEM)
    hbm = pl.BlockSpec(memory_space=pl.ANY)
    sem = pltpu.SemaphoreType.DMA
    taken = n_exp * local_experts * slots
    return pl.pallas_call(
        functools.partial(own_experts_kernel, n_exp, local_experts),
        out_shape=(
            jax.ShapeDtypeStruct((rows, D), BF),
            jax.ShapeDtypeStruct((rows, D), F32),
            jax.ShapeDtypeStruct((rows, D), BF),
            jax.ShapeDtypeStruct((experts, D), F32),
            jax.ShapeDtypeStruct((8, D), F32),
        ),
        in_specs=[v, v, hbm, hbm, hbm, v, v, v],
        out_specs=[v] * 5,
        scratch_shapes=[
            pltpu.VMEM((n_exp, rows, XW), BF),
            pltpu.VMEM((n_exp, rows, D), BF),
            pltpu.VMEM(w_gate_up.shape, BF),
            pltpu.VMEM(w_down.shape, BF),
            pltpu.VMEM((n_exp, local_experts * slots, rows), BF),
            pltpu.VMEM((n_exp, local_experts * slots, XW), BF),
            pltpu.VMEM((n_exp, local_experts * slots, D), BF),
            pltpu.VMEM((chips, rows, XW), BF),
            pltpu.VMEM((chips, rows, XW), BF),
            pltpu.VMEM((chips, rows, XW), BF),
            pltpu.VMEM((chips, rows, D), BF),
            pltpu.VMEM((chips, rows, D), BF),
            pltpu.VMEM((chips, rows, D), BF),
            pltpu.VMEM((rows, XW), F32),
            sem((n_exp,)),
            sem((2,)),
        ]
        + [sem((chips,))] * 12,
        compiler_params=pltpu.CompilerParams(
            collective_id=2, has_side_effects=True, vmem_limit_bytes=62 * MIB
        ),
        cost_estimate=pl.CostEstimate(
            flops=2 * taken * 6 * D * FF, bytes_accessed=300 * MIB, transcendentals=0
        ),
    )(ext, cot, cot_all, w_gate_up, w_down, hidden, w_router, gain2)


def expert_grads_kernel(
    blocks,
    groups,
    local_experts,
    ext_all,
    cot_all,
    w_gate_up,
    w_down,
    gate_up_grad,
    down_grad,
    xbuf,
    cbuf,
    kept_x,
    kept_dy,
    kept_active,
    kept_dunits,
    sems,
):
    first = lax.axis_index("exp") * local_experts
    k, g = pl.program_id(0), pl.program_id(1)
    slots = kept_x.shape[0] // blocks
    chunks = blocks // GROUP
    size = GROUP * slots

    def load(c, slot):
        at = pl.ds(g * blocks + c * GROUP, GROUP)
        return (
            pltpu.make_async_copy(ext_all.at[at], xbuf.at[slot], sems.at[0, slot]),
            pltpu.make_async_copy(cot_all.at[at], cbuf.at[slot], sems.at[1, slot]),
        )

    for copy in load(0, 0):
        copy.start()

    def chunk(c, carry):
        slot = lax.rem(c, 2)

        @pl.when(c + 1 < chunks)
        def _():
            for copy in load(c + 1, 1 - slot):
                copy.start()

        for copy in load(c, slot):
            copy.wait()
        wide, upstream = [], []
        for i in range(GROUP):
            s = selection(xbuf[slot, i, :, D:], first + k, 1, slots)
            wide.append(mm(s, xbuf[slot, i]))
            upstream.append(mm(s, cbuf[slot, i]))
        wide = jnp.concatenate(wide, axis=0)
        upstream = jnp.concatenate(upstream, axis=0)
        gate_value = own_gate(wide[:, D:], first + k)
        x = wide[:, :D].astype(BF)
        units = mm(x, w_gate_up[0])
        gate, up = units[:, :FF], units[:, FF:]
        sig = sigmoid(gate)
        silu = gate * sig
        dmade = (gate_value * upstream).astype(BF)
        dactive = mm_nt(dmade, w_down[0])
        dgate = dactive * up * sig * (1.0 + gate * (1.0 - sig))
        at = pl.ds(pl.multiple_of(c * size, size), size)
        kept_x[at] = x
        kept_dy[at] = dmade
        kept_active[at] = (silu * up).astype(BF)
        kept_dunits[at, :FF] = dgate.astype(BF)
        kept_dunits[at, FF:] = (dactive * silu).astype(BF)
        return carry

    lax.fori_loop(0, chunks, chunk, 0)

    def add(out, at, value):
        if groups == 1:
            out[0, at] = value
        else:

            @pl.when(g == 0)
            def _():
                out[0, at] = value

            @pl.when(g > 0)
            def _():
                out[0, at] += value

    tile = 256

    def up_tile(m, carry):
        at = pl.ds(pl.multiple_of(m * tile, tile), tile)
        add(gate_up_grad, at, mm_tn(kept_x[:, at], kept_dunits[...]))
        return carry

    lax.fori_loop(0, D // tile, up_tile, 0)

    def down_tile(m, carry):
        at = pl.ds(pl.multiple_of(m * tile, tile), tile)
        add(down_grad, at, mm_tn(kept_active[:, at], kept_dy[...]))
        return carry

    lax.fori_loop(0, FF // tile, down_tile, 0)


def expert_grads(ext_all, cot_all, w_gate_up, w_down, slots):
    total, rows = ext_all.shape[:2]
    local_experts = w_gate_up.shape[0]
    blocks = min(total, 32)
    groups = total // blocks
    kept = blocks * slots
    hbm = pl.BlockSpec(memory_space=pl.ANY)
    return pl.pallas_call(
        functools.partial(expert_grads_kernel, blocks, groups, local_experts),
        grid=(local_experts, groups),
        out_shape=(
            jax.ShapeDtypeStruct((local_experts, D, 2 * FF), F32),
            jax.ShapeDtypeStruct((local_experts, FF, D), F32),
        ),
        in_specs=[
            hbm,
            hbm,
            pl.BlockSpec((1, D, 2 * FF), lambda k, g: (k, 0, 0)),
            pl.BlockSpec((1, FF, D), lambda k, g: (k, 0, 0)),
        ],
        out_specs=[
            pl.BlockSpec((1, D, 2 * FF), lambda k, g: (k, 0, 0)),
            pl.BlockSpec((1, FF, D), lambda k, g: (k, 0, 0)),
        ],
        scratch_shapes=[
            pltpu.VMEM((2, GROUP, rows, XW), BF),
            pltpu.VMEM((2, GROUP, rows, D), BF),
            pltpu.VMEM((kept, D), BF),
            pltpu.VMEM((kept, D), BF),
            pltpu.VMEM((kept, FF), BF),
            pltpu.VMEM((kept, 2 * FF), BF),
            pltpu.SemaphoreType.DMA((2, 2)),
        ],
        compiler_params=pltpu.CompilerParams(vmem_limit_bytes=60 * MIB),
        cost_estimate=pl.CostEstimate(
            flops=2 * total * slots * local_experts * 6 * D * FF,
            bytes_accessed=200 * MIB,
            transcendentals=0,
        ),
    )(ext_all, cot_all, w_gate_up, w_down)


def attention_backward_kernel(
    n,
    dhidden_low,
    dhidden,
    tokens,
    gain1,
    held,
    queries,
    pairs,
    mixed,
    totals,
    w_query,
    w_pair,
    w_out,
    prefix,
    input_grad,
    query_grad,
    pair_grad,
    out_grad,
    norm1_part,
    dfull,
    dqueries,
    dpairs,
    dpairs_low,
    sent,
    landed,
    ag_rs,
    ag_rr,
    ag_ls,
    ag_lr,
    rs_s,
    rs_r,
):
    e, z = lax.axis_index("exp"), lax.axis_index("tp")
    rows = tokens.shape[0]
    length = rows * n
    kv_local = pairs.shape[1] // LANES
    low = lax.broadcasted_iota(jnp.int32, (rows, LANES), 1) < HD
    scale = HD**-0.5
    greet_line(e, z, n)
    dfull[pl.ds(pl.multiple_of(z * rows, rows), rows)] = dhidden_low[...]
    dpairs[...] = jnp.zeros_like(dpairs)

    def work(d):
        at = pl.ds(pl.multiple_of(d * rows, rows), rows)
        seen = visible_mask(d, rows, length, prefix[0])
        dmixed = mm_nt(dfull[at], w_out[...]).astype(BF)
        stats = totals[at]
        for kv in range(kv_local):
            span = slice(kv * LANES, (kv + 1) * LANES)
            pair = pairs[:, span]
            outs = []
            added = jnp.zeros((length, LANES), F32)
            heads = halves(queries[at, span], low)
            grads = halves(dmixed[:, span], low)
            for h in range(2):
                head = (heads[h] * scale).astype(BF)
                grad = pltpu.roll(grads[h], HD, 1).astype(BF)
                column = 2 * kv + h
                scores = mm_nt(head, pair)
                probs = jnp.where(seen, jnp.exp(scores - stats[:, column : column + 1]), 0.0)
                dprobs = mm_nt(grad, pair)
                inner = jnp.sum(probs * dprobs, axis=-1, keepdims=True)
                dscores = (probs * (dprobs - inner)).astype(BF)
                outs.append(mm(dscores, pair) * scale)
                added += mm_tn(dscores, head) + mm_tn(probs.astype(BF), grad)
            both = jnp.where(low, outs[0], pltpu.roll(outs[1], HD, 1))
            dqueries[at, span] = both.astype(BF)
            dpairs[:, span] += added

    drain = line_gather(e, z, n, rows, dfull, (ag_rs, ag_rr), (ag_ls, ag_lr), work)
    dpairs_low[...] = dpairs[...].astype(BF)

    def part(d):
        at = pl.ds(pl.multiple_of(d * rows, rows), rows)
        return mm_nt(dqueries[at], w_query[...]) + mm_nt(dpairs_low[at], w_pair[...])

    def weights():
        query_grad[...] = mm_tn(held[...], dqueries[...]).astype(BF)
        pair_grad[...] = mm_tn(held[...], dpairs_low[...]).astype(BF)
        out_grad[...] = mm_tn(mixed[...], dfull[...]).astype(BF)

    finish = line_scatter(e, z, n, sent, landed, (rs_s, rs_r), part, weights)
    finish(input_grad)
    dnormed1 = input_grad[...]
    scaled, inverse = row_scaling(tokens[...].astype(F32))
    norm1_part[...] = jnp.broadcast_to(
        jnp.sum(dnormed1 * scaled, axis=0, keepdims=True), norm1_part.shape
    )
    input_grad[...] = dhidden[...] + norm_backward(dnormed1, scaled, inverse, gain1[...])
    drain()


def attention_backward(
    n,
    dhidden_low,
    dhidden,
    tokens,
    gain1,
    held,
    queries,
    pairs,
    mixed,
    totals,
    w_query,
    w_pair,
    w_out,
    prefix,
):
    rows = tokens.shape[0]
    length = rows * n
    qw, pw = w_query.shape[1], w_pair.shape[1]
    v = pl.BlockSpec(memory_space=VMEM)
    sem = pltpu.SemaphoreType.DMA
    return pl.pallas_call(
        functools.partial(attention_backward_kernel, n),
        out_shape=(
            jax.ShapeDtypeStruct((rows, D), F32),
            jax.ShapeDtypeStruct((D, qw), BF),
            jax.ShapeDtypeStruct((D, pw), BF),
            jax.ShapeDtypeStruct((qw, D), BF),
            jax.ShapeDtypeStruct((8, D), F32),
        ),
        in_specs=[v] * 12 + [pl.BlockSpec(memory_space=pltpu.SMEM)],
        out_specs=[v] * 5,
        scratch_shapes=[
            pltpu.VMEM((length, D), BF),
            pltpu.VMEM((length, qw), BF),
            pltpu.VMEM((length, pw), F32),
            pltpu.VMEM((length, pw), BF),
            pltpu.VMEM((2, n, rows, D), BF),
            pltpu.VMEM((2, n, rows, D), BF),
            sem((n,)),
            sem((n,)),
            sem((n,)),
            sem((n,)),
            sem((2, n)),
            sem((2, n)),
        ],
        compiler_params=pltpu.CompilerParams(
            collective_id=3, has_side_effects=True, vmem_limit_bytes=56 * MIB
        ),
        cost_estimate=pl.CostEstimate(
            flops=2 * length * D * 8 * qw, bytes_accessed=300 * MIB, transcendentals=0
        ),
    )(
        dhidden_low,
        dhidden,
        tokens,
        gain1,
        held,
        queries,
        pairs,
        mixed,
        totals,
        w_query,
        w_pair,
        w_out,
        prefix,
    )


def local(
    n_exp,
    n_tp,
    tokens,
    norm1_gain,
    w_query,
    w_key_value,
    w_out,
    norm2_gain,
    w_router,
    w_gate_up,
    w_down,
    routes,
    prefix,
    cotangent,
):
    rows = tokens.shape[0]
    experts = w_router.shape[1]
    slots = slot_rows(rows, routes.shape[1], experts)
    w_pair = w_key_value.reshape(D, -1)
    gain1, gain2 = norm1_gain.reshape(1, D), norm2_gain.reshape(1, D)
    cot_all = lax.all_gather(cotangent, ("exp", "tp"), axis=0, tiled=True)
    cot_all = cot_all.reshape(n_exp * n_tp, rows, D)
    hidden, ext, held, queries, pairs, mixed, totals = attention_forward(
        n_tp, tokens, gain1, w_query, w_pair, w_out, gain2, w_router, routes, prefix
    )
    ext_all = lax.all_gather(ext, ("exp", "tp"), axis=0, tiled=True)
    ext_all = ext_all.reshape(n_exp * n_tp, rows, XW)
    layer_out, dhidden, dhidden_low, router_part, norm2_part = own_experts(
        n_exp,
        ext,
        cotangent,
        cot_all.reshape(n_exp, n_tp, rows, D),
        w_gate_up,
        w_down,
        hidden,
        w_router,
        gain2,
        slots,
    )
    input_grad, query_grad, pair_grad, out_grad, norm1_part = attention_backward(
        n_tp,
        dhidden_low,
        dhidden,
        tokens,
        gain1,
        held,
        queries,
        pairs,
        mixed,
        totals,
        w_query,
        w_pair,
        w_out,
        prefix,
    )
    gate_up_grad, down_grad = expert_grads(ext_all, cot_all, w_gate_up, w_down, slots)
    query_grad, pair_grad, out_grad = (
        lax.psum(query_grad, "exp").astype(F32),
        lax.psum(pair_grad, "exp").astype(F32),
        lax.psum(out_grad, "exp").astype(F32),
    )
    small = jnp.concatenate([router_part, norm1_part[:1], norm2_part[:1]], axis=0)
    small = lax.psum(small, ("exp", "tp"))
    return (
        layer_out,
        input_grad,
        small[experts],
        query_grad,
        pair_grad.reshape(w_key_value.shape),
        out_grad,
        small[experts + 1],
        small[:experts].T,
        gate_up_grad,
        down_grad,
    )


def solution(mesh):
    return jax.shard_map(
        functools.partial(local, mesh.shape["exp"], mesh.shape["tp"]),
        mesh=mesh,
        in_specs=(
            P(("exp", "tp"), None),
            P(),
            P(None, "tp"),
            P(None, "tp", None),
            P("tp", None),
            P(),
            P(),
            P("exp", None, None),
            P("exp", None, None),
            P(("exp", "tp"), None),
            P("exp"),
            P(("exp", "tp"), None),
        ),
        out_specs=(
            P(("exp", "tp"), None),
            P(("exp", "tp"), None),
            P(),
            P(None, "tp"),
            P(None, "tp", None),
            P("tp", None),
            P(),
            P(),
            P("exp", None, None),
            P("exp", None, None),
        ),
        check_vma=False,
    )
```

```python
import functools

import jax
import jax.numpy as jnp
from jax import lax
from jax.experimental import pallas as pl
from jax.experimental.pallas import tpu as pltpu
from jax.sharding import PartitionSpec as P

D = 1024
H = 16
KVH = 8
HD = 64
FF = 512
LANES = 128
XW = D + LANES
RW = XW + D
GROUP = 4

EPS = 1e-06
MASKED = -1e30
MESH = pl.DeviceIdType.MESH
BF = jnp.bfloat16
F32 = jnp.float32
VMEM = pltpu.VMEM
MIB = 1 << 20


def mm(a, b):
    return jnp.dot(a, b, preferred_element_type=F32)


def mm_nt(a, b):
    return lax.dot_general(a, b, (((1,), (1,)), ((), ())), preferred_element_type=F32)


def mm_tn(a, b):
    return lax.dot_general(a, b, (((0,), (0,)), ((), ())), preferred_element_type=F32)


def row_scaling(values):
    inverse = lax.rsqrt(jnp.mean(values * values, axis=-1, keepdims=True) + EPS)
    return values * inverse, inverse


def norm_backward(gradient, scaled, inverse, gain):
    weighted = gradient * gain
    inner = jnp.mean(weighted * scaled, axis=-1, keepdims=True)
    return inverse * (weighted - scaled * inner)


def block(ref, index, rows):
    return ref.at[pl.ds(pl.multiple_of(index * rows, rows), rows)]


def line_order(n):
    orders = []
    for z in range(n):
        right = list(range(n - 1, z, -1))
        left = list(range(z))
        first, second = (right, left) if len(right) >= len(left) else (left, right)
        order = []
        while first or second:
            if len(first) >= len(second):
                order.append(first.pop(0))
            else:
                order.append(second.pop(0))
        orders.append(order + [z])
    return orders


def lookup(table, z, j):
    value = jnp.int32(table[0][0])
    for a, row in enumerate(table):
        for b, entry in enumerate(row):
            value = jnp.where((z == a) & (j == b), jnp.int32(entry), value)
    return value


def greet(e, z, n, n_exp, line, plane):
    barrier = pltpu.get_barrier_semaphore()
    peers = jnp.int32(0)
    if line:

        @pl.when(z > 0)
        def _():
            pl.semaphore_signal(barrier, inc=1, device_id=(e, z - 1), device_id_type=MESH)

        @pl.when(z < n - 1)
        def _():
            pl.semaphore_signal(barrier, inc=1, device_id=(e, z + 1), device_id_type=MESH)

        peers += jnp.where(z > 0, 1, 0) + jnp.where(z < n - 1, 1, 0)
    if plane:
        chip, core = e // 2, lax.rem(e, 2)
        pl.semaphore_signal(barrier, inc=1, device_id=(e + 1 - 2 * core, z), device_id_type=MESH)

        def one(k, carry):
            there = 2 * (chip ^ k) + core
            pl.semaphore_signal(barrier, inc=1, device_id=(there, z), device_id_type=MESH)
            return carry

        lax.fori_loop(1, n_exp // 2, one, 0)
        peers += n_exp // 2
    return barrier, peers


def each(count, body, start=0):
    lax.fori_loop(start, count, lambda i, c: (body(i), c)[1], 0)


class PlaneGather:
    def __init__(self, e, z, n_exp, own, view, sems):
        self.e, self.z, self.own, self.view = e, z, own, view
        self.chip, self.core, self.chips = e // 2, lax.rem(e, 2), n_exp // 2
        self.push_s, self.push_r, self.pass_s, self.pass_r = sems

    def mine(self, k):
        return 2 * (self.chip ^ k) + self.core

    def other(self, k):
        return 2 * (self.chip ^ k) + 1 - self.core

    def push(self, k):
        return pltpu.make_async_remote_copy(
            src_ref=self.own,
            dst_ref=self.view(self.e),
            send_sem=self.push_s(k),
            recv_sem=self.push_r(k),
            device_id=(self.mine(k), self.z),
            device_id_type=MESH,
        )

    def pushed(self, k):
        there = self.view(self.mine(k))
        return pltpu.make_async_remote_copy(
            src_ref=there,
            dst_ref=there,
            send_sem=self.push_s(k),
            recv_sem=self.push_r(k),
            device_id=(self.mine(k), self.z),
            device_id_type=MESH,
        )

    def hand(self, k, first=False):
        there = self.view(self.mine(k))
        return pltpu.make_async_remote_copy(
            src_ref=self.own if first else there,
            dst_ref=there,
            send_sem=self.pass_s(k),
            recv_sem=self.pass_r(k),
            device_id=(self.other(0), self.z),
            device_id_type=MESH,
        )

    def handed(self, k):
        there = self.view(self.other(k))
        return pltpu.make_async_remote_copy(
            src_ref=there,
            dst_ref=there,
            send_sem=self.pass_s(k),
            recv_sem=self.pass_r(k),
            device_id=(self.other(0), self.z),
            device_id_type=MESH,
        )

    def begin(self):
        each(self.chips, lambda k: self.push(k).start(), 1)
        self.hand(0, True).start()

    def relay(self):
        def one(k):
            self.pushed(k).wait_recv()
            self.hand(k).start()

        each(self.chips, one, 1)

    def arrive(self):
        each(self.chips, lambda k: self.handed(k).wait_recv())

    def drain(self):
        self.hand(0, True).wait_send()

        def one(k):
            self.push(k).wait_send()
            self.hand(k).wait_send()

        each(self.chips, one, 1)


class LineGather:
    def __init__(self, e, z, n, rows, held, right_sems, left_sems):
        self.e, self.z, self.n, self.rows, self.held = e, z, n, rows, held
        self.sems = {1: right_sems, -1: left_sems}
        self.onward = {1: z < n - 1, -1: z > 0}

    def has(self, step, way):
        return self.z >= step if way > 0 else self.z + step < self.n

    def copy(self, step, way, landed=False):
        send, recv = self.sems[way]
        there = block(self.held, self.z - way * step, self.rows)
        return pltpu.make_async_remote_copy(
            src_ref=there,
            dst_ref=there,
            send_sem=send.at[step],
            recv_sem=recv.at[step - 1 if landed else step],
            device_id=(self.e, self.z + way),
            device_id_type=MESH,
        )

    def begin(self):
        for way in (1, -1):

            @pl.when(self.onward[way])
            def _():
                self.copy(0, way).start()

    def step(self, step):
        for way in (1, -1):

            @pl.when(self.has(step, way))
            def _():
                self.copy(step, way, True).wait_recv()

            @pl.when(self.has(step, way) & self.onward[way])
            def _():
                self.copy(step, way).start()

    def work(self, step, body):
        def one(way, carry):
            d = jnp.where(way > 0, self.z - step, self.z + step)

            @pl.when((d >= 0) & (d < self.n) & ((step > 0) | (way > 0)))
            def _():
                body(d)

            return carry

        lax.fori_loop(0, 2, one, 0)

    def drain(self):
        for step in range(self.n - 1):
            for way in (1, -1):

                @pl.when(self.has(step, way) & self.onward[way])
                def _():
                    self.copy(step, way).wait_send()


class LineScatter:
    def __init__(self, e, z, n, sent, landed, sems, part):
        self.e, self.z, self.n, self.sent, self.landed, self.part = e, z, n, sent, landed, part
        self.send, self.recv = sems
        self.table = line_order(n)

    def outgoing(self, d):
        right = d > self.z
        place = jnp.where(right | (d < self.z - 1), d, self.n)
        return pltpu.make_async_remote_copy(
            src_ref=self.sent.at[d],
            dst_ref=self.landed.at[place],
            send_sem=self.send.at[d],
            recv_sem=self.recv.at[place],
            device_id=(self.e, jnp.where(right, self.z + 1, self.z - 1)),
            device_id_type=MESH,
        )

    def incoming(self, place):
        return pltpu.make_async_remote_copy(
            src_ref=self.landed.at[place],
            dst_ref=self.landed.at[place],
            send_sem=self.send.at[0],
            recv_sem=self.recv.at[place],
            device_id=(self.e, jnp.where(self.z > 0, self.z - 1, self.z + 1)),
            device_id_type=MESH,
        )

    def step(self, j):
        d = lookup(self.table, self.z, j)
        value = self.part(d)
        upstream = jnp.where(d > self.z, self.z > 0, self.z < self.n - 1)

        @pl.when(upstream)
        def _():
            self.incoming(d).wait_recv()
            self.sent[d] = (value + self.landed[d].astype(F32)).astype(BF)

        @pl.when(jnp.logical_not(upstream))
        def _():
            self.sent[d] = value.astype(BF)

        self.outgoing(d).start()

    def finish(self, total):
        total[...] = self.part(self.z)

        @pl.when(self.z > 0)
        def _():
            self.incoming(self.z).wait_recv()
            total[...] += self.landed[self.z].astype(F32)

        @pl.when(self.z < self.n - 1)
        def _():
            self.incoming(self.n).wait_recv()
            total[...] += self.landed[self.n].astype(F32)

    def drain(self):
        for d in range(self.n):

            @pl.when(self.z != d)
            def _():
                self.outgoing(d).wait_send()


def visible_mask(d, rows, length, prefix):
    row_ids = d * rows + lax.broadcasted_iota(jnp.int32, (rows, length), 0)
    col_ids = lax.broadcasted_iota(jnp.int32, (rows, length), 1)
    return (col_ids <= row_ids) | (col_ids < prefix)


def halves(pair, low):
    pair = pair.astype(F32)
    zero = jnp.zeros_like(pair)
    return jnp.where(low, pair, zero), jnp.where(low, pltpu.roll(pair, HD, 1), zero)


def attention_forward_kernel(
    n,
    n_exp,
    tokens,
    gain1,
    w_query,
    w_pair,
    w_out,
    gain2,
    w_router,
    routes,
    prefix,
    cot,
    hidden,
    ext,
    cot_plane,
    held,
    queries,
    pairs,
    mixed,
    totals,
    sent,
    landed,
    ag_rs,
    ag_rr,
    ag_ls,
    ag_lr,
    rs_s,
    rs_r,
    push_s,
    push_r,
    pass_s,
    pass_r,
    local_sem,
):
    e, z = lax.axis_index("exp"), lax.axis_index("tp")
    rows = tokens.shape[0]
    length = rows * n
    kv_local = pairs.shape[1] // LANES
    low = lax.broadcasted_iota(jnp.int32, (rows, LANES), 1) < HD
    barrier, peers = greet(e, z, n, n_exp, True, True)
    scaled, _ = row_scaling(tokens[...].astype(F32))
    held[pl.ds(pl.multiple_of(z * rows, rows), rows)] = (scaled * gain1[...]).astype(BF)

    def project(d):
        at = pl.ds(pl.multiple_of(d * rows, rows), rows)
        normed = held[at]
        queries[at] = mm(normed, w_query[...]).astype(BF)
        pairs[at] = mm(normed, w_pair[...]).astype(BF)

    pl.semaphore_wait(barrier, peers)
    line = LineGather(e, z, n, rows, held, (ag_rs, ag_rr), (ag_ls, ag_lr))
    line.begin()
    plane = PlaneGather(
        e,
        z,
        n_exp,
        cot,
        lambda b: cot_plane.at[b],
        [lambda k, s=s: s.at[k] for s in (push_s, push_r, pass_s, pass_r)],
    )
    plane.begin()
    keep = pltpu.make_async_copy(cot, cot_plane.at[e], local_sem)
    keep.start()
    line.work(0, project)

    def gather_step(step):
        line.step(step)
        line.work(step, project)

    each(n, gather_step, 1)

    def part(d):
        at = pl.ds(pl.multiple_of(d * rows, rows), rows)
        seen = visible_mask(d, rows, length, prefix[0])
        lane = lax.broadcasted_iota(jnp.int32, (rows, LANES), 1)
        stats = jnp.zeros((rows, LANES), F32)
        for kv in range(kv_local):
            span = slice(kv * LANES, (kv + 1) * LANES)
            pair = pairs[:, span]
            outs = []
            for h, head in enumerate(halves(queries[at, span], low)):
                scores = mm_nt((head * HD**-0.5).astype(BF), pair)
                scores = jnp.where(seen, scores, MASKED)
                top = jnp.max(scores, axis=-1, keepdims=True)
                grown = jnp.exp(scores - top)
                total = jnp.sum(grown, axis=-1, keepdims=True)
                probs = (grown / total).astype(BF)
                outs.append(mm(probs, pair))
                stats = jnp.where(lane == 2 * kv + h, top + jnp.log(total), stats)
            both = jnp.where(low, pltpu.roll(outs[0], HD, 1), outs[1])
            mixed[at, span] = both.astype(BF)
        totals[at] = stats
        return mm(mixed[at], w_out[...])

    scatter = LineScatter(e, z, n, sent, landed, (rs_s, rs_r), part)
    each(n - 1, scatter.step)
    plane.relay()
    scatter.finish(hidden)
    hid = tokens[...].astype(F32) + hidden[...]
    hidden[...] = hid
    scaled2, _ = row_scaling(hid)
    normed2 = (scaled2 * gain2[...]).astype(BF)
    ext[:, :D] = normed2
    experts = w_router.shape[1]
    logits = mm(normed2, w_router[...])
    lane = lax.broadcasted_iota(jnp.int32, (rows, experts), 1)
    chosen = lane == routes[:, 0:1]
    for k in range(1, routes.shape[1]):
        chosen = chosen | (lane == routes[:, k : k + 1])
    logits = jnp.where(chosen, logits, MASKED)
    grown = jnp.exp(logits - jnp.max(logits, axis=-1, keepdims=True))
    grown = jnp.where(chosen, grown, 0.0)
    gates = grown / jnp.sum(grown, axis=-1, keepdims=True)
    high = gates.astype(BF)
    low_part = (gates - high.astype(F32)).astype(BF)
    mask = jnp.where(chosen, 1.0, 0.0).astype(BF)
    pad = jnp.zeros((rows, LANES - 3 * experts), BF)
    ext[:, D:] = jnp.concatenate([high, low_part, mask, pad], axis=1)
    keep.wait()
    plane.arrive()
    plane.drain()
    line.drain()
    scatter.drain()


def attention_forward(
    n, n_exp, tokens, gain1, w_query, w_pair, w_out, gain2, w_router, routes, prefix, cot
):
    rows = tokens.shape[0]
    length = rows * n
    qw, pw = w_query.shape[1], w_pair.shape[1]
    v = pl.BlockSpec(memory_space=VMEM)
    sem = pltpu.SemaphoreType.DMA
    return pl.pallas_call(
        functools.partial(attention_forward_kernel, n, n_exp),
        out_shape=(
            jax.ShapeDtypeStruct((rows, D), F32),
            jax.ShapeDtypeStruct((rows, XW), BF),
            jax.ShapeDtypeStruct((n_exp, rows, D), BF),
            jax.ShapeDtypeStruct((length, D), BF),
            jax.ShapeDtypeStruct((length, qw), BF),
            jax.ShapeDtypeStruct((length, pw), BF),
            jax.ShapeDtypeStruct((length, qw), BF),
            jax.ShapeDtypeStruct((length, LANES), F32),
        ),
        in_specs=[v] * 8 + [pl.BlockSpec(memory_space=pltpu.SMEM), v],
        out_specs=[v, v, pl.BlockSpec(memory_space=pl.ANY)] + [v] * 5,
        scratch_shapes=[
            pltpu.VMEM((n, rows, D), BF),
            pltpu.VMEM((n + 1, rows, D), BF),
            sem((n,)),
            sem((n,)),
            sem((n,)),
            sem((n,)),
            sem((n,)),
            sem((n + 1,)),
        ]
        + [sem((n_exp // 2,))] * 4
        + [sem],
        compiler_params=pltpu.CompilerParams(
            collective_id=1, has_side_effects=True, vmem_limit_bytes=48 * MIB
        ),
        cost_estimate=pl.CostEstimate(
            flops=2 * length * D * 4 * qw, bytes_accessed=300 * MIB, transcendentals=0
        ),
    )(tokens, gain1, w_query, w_pair, w_out, gain2, w_router, routes, prefix, cot)


def slot_rows(rows, top_k, experts):
    capacity = rows * top_k * 5 // (experts * 4)
    return -(-capacity // 16) * 16


def selection(extra, first, local_experts, slots):
    rows = extra.shape[0]
    pick = lax.broadcasted_iota(jnp.int32, (8, LANES), 1) == (
        64 + first + lax.broadcasted_iota(jnp.int32, (8, LANES), 0)
    )
    named = mm_nt(jnp.where(pick, 1.0, 0.0).astype(BF), extra)
    earlier = lax.broadcasted_iota(jnp.int32, (rows, rows), 0) < lax.broadcasted_iota(
        jnp.int32, (rows, rows), 1
    )
    place = mm(named.astype(BF), jnp.where(earlier, 1.0, 0.0).astype(BF))
    place = jnp.where(named > 0.5, place, -1.0).astype(jnp.int32)
    slot = lax.broadcasted_iota(jnp.int32, (slots, rows), 0)
    parts = [
        jnp.where(slot == place[k : k + 1, :], 1.0, 0.0) for k in range(local_experts)
    ]
    return jnp.concatenate(parts, axis=0).astype(BF)


def own_gate(extra, expert):
    lane = lax.broadcasted_iota(jnp.int32, extra.shape, 1)
    mine = (lane == expert) | (lane == 32 + expert)
    return jnp.sum(jnp.where(mine, extra.astype(F32), 0.0), axis=-1, keepdims=True)


def sigmoid(v):
    return 1.0 / (1.0 + jnp.exp(-v))


def own_experts_kernel(
    n,
    n_exp,
    local_experts,
    ext,
    cot,
    cot_plane,
    w_gate_up,
    w_down,
    hidden,
    w_router,
    gain2,
    layer_out,
    dhidden,
    dhidden_low,
    router_part,
    norm2_part,
    all_rows,
    xg,
    cg,
    wgu,
    wd,
    sel,
    xs,
    cs,
    core_in,
    chip_out,
    chip_in,
    mix_core_in,
    mix_out,
    mix_in,
    total,
    joined,
    cot_sem,
    w_sem,
    out_sem,
    column_s,
    column_r,
    ag_s,
    ag_r,
    fw_s,
    fw_r,
    core_s,
    core_r,
    chip_s,
    chip_r,
    mcore_s,
    mcore_r,
    mchip_s,
    mchip_r,
):
    e, z = lax.axis_index("exp"), lax.axis_index("tp")
    rows = ext.shape[0]
    chips = n_exp // 2
    chip, core = e // 2, lax.rem(e, 2)
    partner = 2 * chip + 1 - core
    slots = sel.shape[1] // local_experts
    first = e * local_experts
    experts = w_router.shape[1]

    loads = [
        pltpu.make_async_copy(w_gate_up, wgu, w_sem.at[0]),
        pltpu.make_async_copy(w_down, wd, w_sem.at[1]),
    ]
    for b in range(n_exp):
        loads.append(pltpu.make_async_copy(cot_plane.at[b], cg.at[b], cot_sem.at[b]))
    for load in loads:
        load.start()

    barrier, peers = greet(e, z, n, n_exp, False, True)
    for k in range(1, n):
        pl.semaphore_signal(barrier, inc=1, device_id=(e, z ^ k), device_id_type=MESH)
    xg[e] = ext[...]
    joined[:, :XW] = ext[...]
    joined[:, XW:] = cot[...]
    pl.semaphore_wait(barrier, peers + n - 1)
    plane = PlaneGather(
        e,
        z,
        n_exp,
        xg.at[e],
        lambda b: xg.at[b],
        [lambda k, s=s: s.at[k] for s in (ag_s, ag_r, fw_s, fw_r)],
    )
    there, other = plane.mine, plane.other
    plane.begin()

    def up_column(k, landed=False):
        return pltpu.make_async_remote_copy(
            src_ref=joined,
            dst_ref=all_rows.at[(z ^ k) if landed else z, e],
            send_sem=column_s.at[k],
            recv_sem=column_r.at[k],
            device_id=(e, z ^ k),
            device_id_type=MESH,
        )

    for k in range(1, n):
        up_column(k).start()
    for load in loads[2:]:
        load.wait()

    def gather(b):
        s = selection(xg[b, :, D:], first, local_experts, slots)
        sel[b] = s
        xs[b] = mm(s, xg[b]).astype(BF)
        cs[b] = mm(s, cg[b]).astype(BF)

    def save(b):
        return (
            pltpu.make_async_copy(xg.at[b], all_rows.at[z, b, :, pl.ds(0, XW)], out_sem.at[0, b]),
            pltpu.make_async_copy(cg.at[b], all_rows.at[z, b, :, pl.ds(XW, D)], out_sem.at[1, b]),
        )

    gather(e)
    plane.relay()
    each(chips, lambda k: gather(there(k)), 1)
    plane.arrive()
    each(chips, lambda k: gather(other(k)))

    def start_save(b):
        for copy in save(b):
            copy.start()

    def end_save(b):
        for copy in save(b):
            copy.wait()

    each(n_exp, start_save)
    for load in loads[:2]:
        load.wait()

    groups = n_exp // GROUP

    def expert_step(step, carry):
        k = step // groups
        b0 = lax.rem(step, groups) * GROUP
        at = pl.ds(pl.multiple_of(k * slots, slots), slots)
        wide = jnp.concatenate([xs[b0 + i, at] for i in range(GROUP)], axis=0)
        gate_value = own_gate(wide[:, D:], first + k)
        units = mm(wide[:, :D], wgu[k])
        gate, up = units[:, :FF], units[:, FF:]
        sig = sigmoid(gate)
        silu = gate * sig
        active = (silu * up).astype(BF)
        made = mm(active, wd[k]).astype(BF).astype(F32)
        upstream = jnp.concatenate([cs[b0 + i, at] for i in range(GROUP)], axis=0).astype(F32)
        dgate_value = jnp.sum(upstream * made, axis=-1, keepdims=True)
        share = (gate_value * made).astype(BF)
        dmade = (gate_value * upstream).astype(BF)
        dactive = mm_nt(dmade, wd[k])
        dgate = dactive * up * sig * (1.0 + gate * (1.0 - sig))
        dunits = jnp.concatenate([dgate, dactive * silu], axis=1).astype(BF)
        dx = mm_nt(dunits, wgu[k]).astype(BF)
        lane = lax.broadcasted_iota(jnp.int32, (GROUP * slots, LANES), 1)
        high = dgate_value.astype(BF).astype(F32)
        packed = jnp.where(lane == first + k, high, 0.0)
        packed = jnp.where(lane == 32 + first + k, dgate_value - high, packed).astype(BF)
        for i in range(GROUP):
            here = slice(i * slots, (i + 1) * slots)
            xs[b0 + i, at, :D] = share[here]
            xs[b0 + i, at, D:] = packed[here]
            cs[b0 + i, at] = dx[here]
        return carry

    lax.fori_loop(0, local_experts * groups, expert_step, 0)

    each(n_exp, end_save)
    plane.drain()

    def core_copy(k, src, dst, s, r):
        return pltpu.make_async_remote_copy(
            src_ref=src.at[other(k)],
            dst_ref=dst.at[k],
            send_sem=s.at[k],
            recv_sem=r.at[k],
            device_id=(partner, z),
            device_id_type=MESH,
        )

    def chip_copy(k, src, dst, s, r):
        return pltpu.make_async_remote_copy(
            src_ref=src.at[k],
            dst_ref=dst.at[k],
            send_sem=s.at[k],
            recv_sem=r.at[k],
            device_id=(there(k), z),
            device_id_type=MESH,
        )

    def grads_of(b):
        s = sel[b]
        return jnp.concatenate([mm_tn(s, cs[b]), mm_tn(s, xs[b, :, D:])], axis=1)

    def give_grads(i):
        k = chips - 1 - i
        xg[other(k)] = grads_of(other(k)).astype(BF)
        core_copy(k, xg, core_in, core_s, core_r).start()

    def pass_grads(i):
        k = chips - 1 - i
        mine = grads_of(there(k))
        core_copy(k, xg, core_in, core_s, core_r).wait_recv()
        chip_out[k] = (mine + core_in[k].astype(F32)).astype(BF)
        chip_copy(k, chip_out, chip_in, chip_s, chip_r).start()

    def give_mix(i):
        k = chips - 1 - i
        cg[other(k)] = mm_tn(sel[other(k)], xs[other(k), :, :D]).astype(BF)
        core_copy(k, cg, mix_core_in, mcore_s, mcore_r).start()

    def pass_mix(i):
        k = chips - 1 - i
        mine = mm_tn(sel[there(k)], xs[there(k), :, :D])
        core_copy(k, cg, mix_core_in, mcore_s, mcore_r).wait_recv()
        mix_out[k] = (mine + mix_core_in[k].astype(F32)).astype(BF)
        chip_copy(k, mix_out, mix_in, mchip_s, mchip_r).start()

    each(chips, give_grads)
    each(chips - 1, pass_grads)
    each(chips, give_mix)
    each(chips - 1, pass_mix)
    total[...] = grads_of(e)
    core_copy(0, xg, core_in, core_s, core_r).wait_recv()
    total[...] += core_in[0].astype(F32)

    def take_grads(i):
        k = chips - 1 - i
        chip_copy(k, chip_out, chip_in, chip_s, chip_r).wait_recv()
        total[...] += chip_in[k].astype(F32)

    each(chips - 1, take_grads)
    extra = ext[:, D:].astype(F32)
    gates = extra[:, :experts] + extra[:, experts : 2 * experts]
    dgates = total[:, D : D + experts] + total[:, D + experts : D + 2 * experts]
    dlogits = gates * (dgates - jnp.sum(gates * dgates, axis=-1, keepdims=True))
    dlogits = dlogits.astype(BF)
    normed2 = ext[:, :D]
    router_part[...] = mm_tn(dlogits, normed2)
    dnormed2 = total[:, :D] + mm_nt(dlogits, w_router[...])
    scaled2, inverse2 = row_scaling(hidden[...])
    norm2_part[...] = jnp.broadcast_to(
        jnp.sum(dnormed2 * scaled2, axis=0, keepdims=True), norm2_part.shape
    )
    back = cot[...].astype(F32) + norm_backward(dnormed2, scaled2, inverse2, gain2[...])
    dhidden[...] = back
    dhidden_low[...] = back.astype(BF)

    total[:, :D] = hidden[...] + mm_tn(sel[e], xs[e, :, :D])
    core_copy(0, cg, mix_core_in, mcore_s, mcore_r).wait_recv()
    total[:, :D] += mix_core_in[0].astype(F32)

    def take_mix(i):
        k = chips - 1 - i
        chip_copy(k, mix_out, mix_in, mchip_s, mchip_r).wait_recv()
        total[:, :D] += mix_in[k].astype(F32)

    each(chips - 1, take_mix)
    layer_out[...] = total[:, :D].astype(BF)

    def sent_to_core(k):
        core_copy(k, xg, core_in, core_s, core_r).wait_send()
        core_copy(k, cg, mix_core_in, mcore_s, mcore_r).wait_send()

    def sent_to_chip(i):
        chip_copy(i + 1, chip_out, chip_in, chip_s, chip_r).wait_send()
        chip_copy(i + 1, mix_out, mix_in, mchip_s, mchip_r).wait_send()

    each(chips, sent_to_core)
    each(chips - 1, sent_to_chip)
    for k in range(1, n):
        up_column(k, True).wait_recv()
        up_column(k).wait_send()


def own_experts(n, n_exp, ext, cot, cot_plane, w_gate_up, w_down, hidden, w_router, gain2, slots):
    rows = ext.shape[0]
    local_experts = w_gate_up.shape[0]
    experts = w_router.shape[1]
    chips = n_exp // 2
    v = pl.BlockSpec(memory_space=VMEM)
    hbm = pl.BlockSpec(memory_space=pl.ANY)
    sem = pltpu.SemaphoreType.DMA
    taken = n_exp * local_experts * slots
    return pl.pallas_call(
        functools.partial(own_experts_kernel, n, n_exp, local_experts),
        out_shape=(
            jax.ShapeDtypeStruct((rows, D), BF),
            jax.ShapeDtypeStruct((rows, D), F32),
            jax.ShapeDtypeStruct((rows, D), BF),
            jax.ShapeDtypeStruct((experts, D), F32),
            jax.ShapeDtypeStruct((8, D), F32),
            jax.ShapeDtypeStruct((n, n_exp, rows, RW), BF),
        ),
        in_specs=[v, v, hbm, hbm, hbm, v, v, v],
        out_specs=[v] * 5 + [hbm],
        scratch_shapes=[
            pltpu.VMEM((n_exp, rows, XW), BF),
            pltpu.VMEM((n_exp, rows, D), BF),
            pltpu.VMEM(w_gate_up.shape, BF),
            pltpu.VMEM(w_down.shape, BF),
            pltpu.VMEM((n_exp, local_experts * slots, rows), BF),
            pltpu.VMEM((n_exp, local_experts * slots, XW), BF),
            pltpu.VMEM((n_exp, local_experts * slots, D), BF),
            pltpu.VMEM((chips, rows, XW), BF),
            pltpu.VMEM((chips, rows, XW), BF),
            pltpu.VMEM((chips, rows, XW), BF),
            pltpu.VMEM((chips, rows, D), BF),
            pltpu.VMEM((chips, rows, D), BF),
            pltpu.VMEM((chips, rows, D), BF),
            pltpu.VMEM((rows, XW), F32),
            pltpu.VMEM((rows, RW), BF),
            sem((n_exp,)),
            sem((2,)),
            sem((2, n_exp)),
            sem((n,)),
            sem((n,)),
        ]
        + [sem((chips,))] * 12,
        compiler_params=pltpu.CompilerParams(
            collective_id=2, has_side_effects=True, vmem_limit_bytes=62 * MIB
        ),
        cost_estimate=pl.CostEstimate(
            flops=2 * taken * 6 * D * FF, bytes_accessed=300 * MIB, transcendentals=0
        ),
    )(ext, cot, cot_plane, w_gate_up, w_down, hidden, w_router, gain2)


def expert_middle(x, gate_value, upstream, w_gate_up, w_down):
    units = mm(x, w_gate_up)
    gate, up = units[:, :FF], units[:, FF:]
    sig = sigmoid(gate)
    silu = gate * sig
    dmade = (gate_value * upstream.astype(F32)).astype(BF)
    dactive = mm_nt(dmade, w_down)
    dgate = dactive * up * sig * (1.0 + gate * (1.0 - sig))
    return dmade, (silu * up).astype(BF), dgate.astype(BF), (dactive * silu).astype(BF)


def expert_grads_kernel(
    blocks,
    groups,
    early,
    local_experts,
    rows_all,
    *refs,
):
    first = lax.axis_index("exp") * local_experts + early
    k, g = pl.program_id(0), pl.program_id(1)
    refs = list(refs)
    w_gate_up, w_down = refs.pop(0), refs.pop(0)
    done = (refs.pop(0), refs.pop(0)) if early else None
    gate_up_grad, down_grad, rbuf, kept_x, kept_dy, kept_active, kept_dunits = refs[:7]
    acc_up, acc_down, sems, out_sems, copy_sems = refs[7:]
    slots = kept_x.shape[0] // blocks
    chunks = blocks // GROUP
    size = GROUP * slots
    last = local_experts - early - 1

    def brought():
        return (
            pltpu.make_async_copy(done[0], acc_up.at[pl.ds(0, early)], copy_sems.at[0]),
            pltpu.make_async_copy(done[1], acc_down.at[pl.ds(0, early)], copy_sems.at[1]),
        )

    def taken():
        return (
            pltpu.make_async_copy(
                acc_up.at[pl.ds(0, early)], gate_up_grad.at[pl.ds(0, early)], copy_sems.at[0]
            ),
            pltpu.make_async_copy(
                acc_down.at[pl.ds(0, early)], down_grad.at[pl.ds(0, early)], copy_sems.at[1]
            ),
        )

    opening = (k == 0) & (g == 0)
    if early:

        @pl.when(opening)
        def _():
            for copy in brought():
                copy.start()

    def load(c, slot):
        at = pl.ds(g * blocks + c * GROUP, GROUP)
        return pltpu.make_async_copy(rows_all.at[at], rbuf.at[slot], sems.at[slot])

    load(0, 0).start()

    def chunk(c, carry):
        slot = lax.rem(c, 2)

        @pl.when(c + 1 < chunks)
        def _():
            load(c + 1, 1 - slot).start()

        load(c, slot).wait()
        if early:

            @pl.when(opening & (c == 2))
            def _():
                for copy in brought():
                    copy.wait()
                for copy in taken():
                    copy.start()

        wide = []
        for i in range(GROUP):
            s = selection(rbuf[slot, i, :, D:XW], first + k, 1, slots)
            wide.append(mm(s, rbuf[slot, i]))
        wide = jnp.concatenate(wide, axis=0)
        x = wide[:, :D].astype(BF)
        made = expert_middle(
            x, own_gate(wide[:, D:XW], first + k), wide[:, XW:], w_gate_up[0], w_down[0]
        )
        at = pl.ds(pl.multiple_of(c * size, size), size)
        kept_x[at] = x
        kept_dy[at] = made[0]
        kept_active[at] = made[1]
        kept_dunits[at, :FF] = made[2]
        kept_dunits[at, FF:] = made[3]
        return carry

    lax.fori_loop(0, chunks, chunk, 0)
    bank = lax.rem(k, 2)
    if early:

        @pl.when(opening)
        def _():
            for copy in taken():
                copy.wait()

    def store(kk):
        b = lax.rem(kk, 2)
        return (
            pltpu.make_async_copy(acc_up.at[b], gate_up_grad.at[early + kk], out_sems.at[0, b]),
            pltpu.make_async_copy(acc_down.at[b], down_grad.at[early + kk], out_sems.at[1, b]),
        )

    @pl.when((g == 0) & (k >= 2))
    def _():
        for copy in store(k - 2):
            copy.wait()

    def add(out, at, value):
        if groups == 1:
            out[bank, at] = value
        else:

            @pl.when(g == 0)
            def _():
                out[bank, at] = value

            @pl.when(g > 0)
            def _():
                out[bank, at] += value

    tile = 256

    def up_tile(m, carry):
        at = pl.ds(pl.multiple_of(m * tile, tile), tile)
        add(acc_up, at, mm_tn(kept_x[:, at], kept_dunits[...]))
        return carry

    lax.fori_loop(0, D // tile, up_tile, 0)

    def down_tile(m, carry):
        at = pl.ds(pl.multiple_of(m * tile, tile), tile)
        add(acc_down, at, mm_tn(kept_active[:, at], kept_dy[...]))
        return carry

    lax.fori_loop(0, FF // tile, down_tile, 0)

    @pl.when(g == groups - 1)
    def _():
        for copy in store(k):
            copy.start()

    @pl.when((g == groups - 1) & (k == last))
    def _():
        for copy in store(k):
            copy.wait()
        if last > 0:
            for copy in store(k - 1):
                copy.wait()


def expert_grads(rows_all, w_gate_up, w_down, done, slots):
    total, rows = rows_all.shape[:2]
    local_experts = w_gate_up.shape[0]
    early = done[0].shape[0] if done else 0
    assert early <= 2
    blocks = min(total, 32)
    groups = total // blocks
    kept = blocks * slots
    hbm = pl.BlockSpec(memory_space=pl.ANY)
    sem = pltpu.SemaphoreType.DMA
    return pl.pallas_call(
        functools.partial(expert_grads_kernel, blocks, groups, early, local_experts),
        grid=(local_experts - early, groups),
        out_shape=(
            jax.ShapeDtypeStruct((local_experts, D, 2 * FF), F32),
            jax.ShapeDtypeStruct((local_experts, FF, D), F32),
        ),
        in_specs=[
            hbm,
            pl.BlockSpec((1, D, 2 * FF), lambda k, g: (k + early, 0, 0)),
            pl.BlockSpec((1, FF, D), lambda k, g: (k + early, 0, 0)),
        ]
        + [hbm] * len(done),
        out_specs=[hbm, hbm],
        scratch_shapes=[
            pltpu.VMEM((2, GROUP, rows, RW), BF),
            pltpu.VMEM((kept, D), BF),
            pltpu.VMEM((kept, D), BF),
            pltpu.VMEM((kept, FF), BF),
            pltpu.VMEM((kept, 2 * FF), BF),
            pltpu.VMEM((2, D, 2 * FF), F32),
            pltpu.VMEM((2, FF, D), F32),
            sem((2,)),
            sem((2, 2)),
            sem((2,)),
        ],
        compiler_params=pltpu.CompilerParams(vmem_limit_bytes=60 * MIB),
        cost_estimate=pl.CostEstimate(
            flops=2 * total * slots * local_experts * 6 * D * FF,
            bytes_accessed=300 * MIB,
            transcendentals=0,
        ),
    )(rows_all, w_gate_up, w_down, *done)


def backward_kernel(n, n_exp, early, local_experts, *refs):
    refs = list(refs)

    def take(count):
        got = refs[:count]
        del refs[:count]
        return got

    dhidden_low, dhidden, tokens, gain1, held, queries, pairs, mixed, totals = take(9)
    w_query, w_pair, w_out, prefix, _ = take(5)
    if early:
        w_gate_up, w_down = take(2)
    input_grad, query_grad, pair_grad, out_grad, norm1, all_rows = take(6)
    if early:
        gate_up_grad, down_grad = take(2)
    dfull, dqueries, dpairs, dpairs_low, sent, landed, line_norms, plane_norms = take(8)
    ag_rs, ag_rr, ag_ls, ag_lr, rs_s, rs_r, push_s, push_r, pass_s, pass_r = take(10)
    nz_s, nz_r, np_s, np_r = take(4)
    if early:
        tokens_in, wgu, wd, acc_up, acc_down, kept_x, kept_c, kept_active, kept_dunits = take(9)
        load_s, w_sem, out_sem = take(3)

    e, z = lax.axis_index("exp"), lax.axis_index("tp")
    rows = tokens.shape[0]
    length = rows * n
    kv_local = pairs.shape[1] // LANES
    low = lax.broadcasted_iota(jnp.int32, (rows, LANES), 1) < HD
    scale = HD**-0.5
    first = e * local_experts

    if early:
        weights = [
            pltpu.make_async_copy(w_gate_up.at[pl.ds(0, early)], wgu, w_sem.at[0]),
            pltpu.make_async_copy(w_down.at[pl.ds(0, early)], wd, w_sem.at[1]),
        ]
        for copy in weights:
            copy.start()

    barrier = pltpu.get_barrier_semaphore()

    def greet_plane(k):
        pl.semaphore_signal(barrier, inc=1, device_id=(e ^ k, z), device_id_type=MESH)

    def greet_line(k):
        pl.semaphore_signal(barrier, inc=1, device_id=(e, z ^ k), device_id_type=MESH)

    each(n_exp, greet_plane, 1)
    each(n, greet_line, 1)
    dfull[pl.ds(pl.multiple_of(z * rows, rows), rows)] = dhidden_low[...]
    dpairs[...] = jnp.zeros_like(dpairs)
    pl.semaphore_wait(barrier, n_exp + n - 2)

    line = LineGather(e, z, n, rows, dfull, (ag_rs, ag_rr), (ag_ls, ag_lr))
    line.begin()

    def plane(i):
        return PlaneGather(
            e,
            z,
            n_exp,
            all_rows.at[z ^ i, e],
            lambda b: all_rows.at[z ^ i, b],
            [lambda k, s=s: s.at[i, k] for s in (push_s, push_r, pass_s, pass_r)],
        )

    plane(1).begin()

    def attend(d):
        at = pl.ds(pl.multiple_of(d * rows, rows), rows)
        seen = visible_mask(d, rows, length, prefix[0])
        dmixed = mm_nt(dfull[at], w_out[...]).astype(BF)
        stats = totals[at]
        for kv in range(kv_local):
            span = slice(kv * LANES, (kv + 1) * LANES)
            pair = pairs[:, span]
            outs = []
            added = jnp.zeros((length, LANES), F32)
            heads = halves(queries[at, span], low)
            grads = halves(dmixed[:, span], low)
            for h in range(2):
                head = (heads[h] * scale).astype(BF)
                grad = pltpu.roll(grads[h], HD, 1).astype(BF)
                stat = 2 * kv + h
                scores = mm_nt(head, pair)
                probs = jnp.where(seen, jnp.exp(scores - stats[:, stat : stat + 1]), 0.0)
                dprobs = mm_nt(grad, pair)
                inner = jnp.sum(probs * dprobs, axis=-1, keepdims=True)
                dscores = (probs * (dprobs - inner)).astype(BF)
                outs.append(mm(dscores, pair) * scale)
                added += mm_tn(dscores, head) + mm_tn(probs.astype(BF), grad)
            both = jnp.where(low, outs[0], pltpu.roll(outs[1], HD, 1))
            dqueries[at, span] = both.astype(BF)
            dpairs[:, span] += added

    def part(d):
        at = pl.ds(pl.multiple_of(d * rows, rows), rows)
        return mm_nt(dqueries[at], w_query[...]) + mm_nt(dpairs_low[at], w_pair[...])

    scatter = LineScatter(e, z, n, sent, landed, (rs_s, rs_r), part)

    def line_norm(k, landed=False):
        return pltpu.make_async_remote_copy(
            src_ref=line_norms.at[z],
            dst_ref=line_norms.at[(z ^ k) if landed else z],
            send_sem=nz_s.at[k],
            recv_sem=nz_r.at[k],
            device_id=(e, z ^ k),
            device_id_type=MESH,
        )

    def plane_norm(k, landed=False):
        return pltpu.make_async_remote_copy(
            src_ref=plane_norms.at[e],
            dst_ref=plane_norms.at[(e ^ k) if landed else e],
            send_sem=np_s.at[k],
            recv_sem=np_r.at[k],
            device_id=(e ^ k, z),
            device_id_type=MESH,
        )

    def event(t):
        @pl.when((t > 0) & (t < n))
        def _():
            line.step(t)

        @pl.when(t < n)
        def _():
            line.work(t, attend)

        @pl.when(t == n)
        def _():
            dpairs_low[...] = dpairs[...].astype(BF)

        @pl.when((t >= n) & (t < 2 * n - 1))
        def _():
            scatter.step(t - n)

        @pl.when(t == 2 * n - 1)
        def _():
            query_grad[...] = mm_tn(held[...], dqueries[...]).astype(BF)
            pair_grad[...] = mm_tn(held[...], dpairs_low[...]).astype(BF)
            out_grad[...] = mm_tn(mixed[...], dfull[...]).astype(BF)

        @pl.when(t == 2 * n)
        def _():
            scatter.finish(input_grad)
            dnormed1 = input_grad[...]
            scaled, inverse = row_scaling(tokens[...].astype(F32))
            total = jnp.sum(dnormed1 * scaled, axis=0, keepdims=True)
            line_norms[z] = jnp.concatenate(
                [total[:, k * LANES : (k + 1) * LANES] for k in range(D // LANES)], axis=0
            )
            each(n, lambda k: line_norm(k).start(), 1)
            back = dhidden[...] + norm_backward(dnormed1, scaled, inverse, gain1[...])
            input_grad[...] = back

        @pl.when(t == 2 * n + 1)
        def _():
            each(n, lambda k: line_norm(k, True).wait_recv(), 1)
            total = line_norms[0]
            for k in range(1, n):
                total = total + line_norms[k]
            plane_norms[e] = total
            each(n_exp, lambda k: plane_norm(k).start(), 1)

    events = 2 * n + 2
    steps = n * (1 + early) if early else 0

    def relay(i):
        each(n_exp // 2, lambda k: plane(i).pushed(k).wait_recv(), 1)

        @pl.when(i + 1 < n)
        def _():
            plane(i + 1).begin()

        each(n_exp // 2, lambda k: plane(i).hand(k).start(), 1)

    if early:
        slots = kept_x.shape[1] // n_exp
        acc_up[...] = jnp.zeros_like(acc_up)
        acc_down[...] = jnp.zeros_like(acc_down)
        for copy in weights:
            copy.wait()

        def one_plane(i, carry):
            @pl.when(i > 0)
            def _():
                plane(i).arrive()

            def load(b):
                return pltpu.make_async_copy(
                    all_rows.at[z ^ i, b], tokens_in.at[b], load_s.at[b]
                )

            each(n_exp, lambda b: load(b).start())

            def pick(b):
                load(b).wait()
                s = selection(tokens_in[b, :, D:XW], first, early, slots)
                got = mm(s, tokens_in[b]).astype(BF)
                at = pl.ds(pl.multiple_of(b * slots, slots), slots)
                for k in range(early):
                    here = got[k * slots : (k + 1) * slots]
                    kept_x[k, at] = here[:, :XW]
                    kept_c[k, at] = here[:, XW:]

            each(n_exp, pick)
            event(i * (1 + early))

            def expert(k):
                gate_value = own_gate(kept_x[k, :, D:], first + k)
                x = kept_x[k, :, :D]
                made = expert_middle(x, gate_value, kept_c[k], wgu[k], wd[k])
                kept_c[k] = made[0]
                kept_active[...] = made[1]
                kept_dunits[:, :FF] = made[2]
                kept_dunits[:, FF:] = made[3]
                acc_up[k] += mm_tn(kept_x[k, :, :D], kept_dunits[...])
                acc_down[k] += mm_tn(kept_active[...], kept_c[k])
                event(i * (1 + early) + 1 + k)

            each(early, expert)

            @pl.when(i + 1 < n)
            def _():
                relay(i + 1)

            return carry

        lax.fori_loop(0, n, one_plane, 0)
        stores = [
            pltpu.make_async_copy(acc_up, gate_up_grad, out_sem.at[0]),
            pltpu.make_async_copy(acc_down, down_grad, out_sem.at[1]),
        ]
        for copy in stores:
            copy.start()
    each(max(events, steps), event, steps)
    if early:
        for copy in stores:
            copy.wait()
    else:

        def one_relay(i):
            relay(i)

        each(n, one_relay, 1)
        each(n, lambda i: plane(i).arrive(), 1)
    each(n_exp, lambda k: plane_norm(k, True).wait_recv(), 1)
    total = plane_norms[0]
    for k in range(1, n_exp):
        total = total + plane_norms[k]
    norm1[...] = total
    each(n, lambda i: plane(i).drain(), 1)
    each(n, lambda k: line_norm(k).wait_send(), 1)
    each(n_exp, lambda k: plane_norm(k).wait_send(), 1)
    line.drain()
    scatter.drain()


def backward(n, n_exp, slots, whole, prefix, all_rows, weights):
    tokens, held = whole[2], whole[4]
    rows = tokens.shape[0]
    length = rows * n
    qw, pw = whole[9].shape[1], whole[10].shape[1]
    local_experts = weights[0].shape[0]
    early = local_experts // 2
    v = pl.BlockSpec(memory_space=VMEM)
    hbm = pl.BlockSpec(memory_space=pl.ANY)
    sem = pltpu.SemaphoreType.DMA
    chips = n_exp // 2
    outs = [
        (jax.ShapeDtypeStruct((rows, D), F32), v),
        (jax.ShapeDtypeStruct((D, qw), BF), v),
        (jax.ShapeDtypeStruct((D, pw), BF), v),
        (jax.ShapeDtypeStruct((qw, D), BF), v),
        (jax.ShapeDtypeStruct((D // LANES, LANES), F32), v),
        (jax.ShapeDtypeStruct((n, n_exp, rows, RW), BF), hbm),
    ]
    scratch = [
        pltpu.VMEM((length, D), BF),
        pltpu.VMEM((length, qw), BF),
        pltpu.VMEM((length, pw), F32),
        pltpu.VMEM((length, pw), BF),
        pltpu.VMEM((n, rows, D), BF),
        pltpu.VMEM((n + 1, rows, D), BF),
        pltpu.VMEM((n, D // LANES, LANES), F32),
        pltpu.VMEM((n_exp, D // LANES, LANES), F32),
        sem((n,)),
        sem((n,)),
        sem((n,)),
        sem((n,)),
        sem((n,)),
        sem((n + 1,)),
    ]
    scratch += [sem((n, chips))] * 4
    scratch += [sem((n,)), sem((n,)), sem((n_exp,)), sem((n_exp,))]
    if early:
        kept = n_exp * slots
        outs += [
            (jax.ShapeDtypeStruct((early, D, 2 * FF), F32), hbm),
            (jax.ShapeDtypeStruct((early, FF, D), F32), hbm),
        ]
        scratch += [
            pltpu.VMEM((n_exp, rows, RW), BF),
            pltpu.VMEM((early, D, 2 * FF), BF),
            pltpu.VMEM((early, FF, D), BF),
            pltpu.VMEM((early, D, 2 * FF), F32),
            pltpu.VMEM((early, FF, D), F32),
            pltpu.VMEM((early, kept, XW), BF),
            pltpu.VMEM((early, kept, D), BF),
            pltpu.VMEM((kept, FF), BF),
            pltpu.VMEM((kept, 2 * FF), BF),
            sem((n_exp,)),
            sem((2,)),
            sem((2,)),
        ]
    return pl.pallas_call(
        functools.partial(backward_kernel, n, n_exp, early, local_experts),
        out_shape=tuple(shape for shape, _ in outs),
        in_specs=[v] * len(whole)
        + [pl.BlockSpec(memory_space=pltpu.SMEM)]
        + [hbm] * (1 + (2 if early else 0)),
        out_specs=tuple(spec for _, spec in outs),
        input_output_aliases={len(whole) + 1: 5},
        scratch_shapes=scratch,
        compiler_params=pltpu.CompilerParams(
            collective_id=3, has_side_effects=True, vmem_limit_bytes=62 * MIB
        ),
        cost_estimate=pl.CostEstimate(
            flops=2 * length * D * 8 * qw, bytes_accessed=300 * MIB, transcendentals=0
        ),
    )(*whole, prefix, all_rows, *(weights if early else ()))


def local(
    n_exp,
    n_tp,
    tokens,
    norm1_gain,
    w_query,
    w_key_value,
    w_out,
    norm2_gain,
    w_router,
    w_gate_up,
    w_down,
    routes,
    prefix,
    cotangent,
):
    rows = tokens.shape[0]
    experts = w_router.shape[1]
    slots = slot_rows(rows, routes.shape[1], experts)
    w_pair = w_key_value.reshape(D, -1)
    gain1, gain2 = norm1_gain.reshape(1, D), norm2_gain.reshape(1, D)
    hidden, ext, cot_plane, held, queries, pairs, mixed, totals = attention_forward(
        n_tp,
        n_exp,
        tokens,
        gain1,
        w_query,
        w_pair,
        w_out,
        gain2,
        w_router,
        routes,
        prefix,
        cotangent,
    )
    layer_out, dhidden, dhidden_low, router_part, norm2_part, all_rows = own_experts(
        n_tp,
        n_exp,
        ext,
        cotangent,
        cot_plane,
        w_gate_up,
        w_down,
        hidden,
        w_router,
        gain2,
        slots,
    )
    small = jnp.concatenate([router_part, norm2_part], axis=0)
    small = lax.psum(small, ("exp", "tp"))
    whole = (dhidden_low, dhidden, tokens, gain1, held, queries, pairs, mixed, totals)
    whole += (w_query, w_pair, w_out)
    made = backward(n_tp, n_exp, slots, whole, prefix, all_rows, (w_gate_up, w_down))
    input_grad, query_grad, pair_grad, out_grad, norm1, all_rows = made[:6]
    gate_up_grad, down_grad = expert_grads(
        all_rows.reshape(n_exp * n_tp, rows, RW), w_gate_up, w_down, made[6:], slots
    )
    query_grad, pair_grad, out_grad = (
        lax.psum(query_grad, "exp").astype(F32),
        lax.psum(pair_grad, "exp").astype(F32),
        lax.psum(out_grad, "exp").astype(F32),
    )
    return (
        layer_out,
        input_grad,
        norm1.reshape(D),
        query_grad,
        pair_grad.reshape(w_key_value.shape),
        out_grad,
        small[experts],
        small[:experts].T,
        gate_up_grad,
        down_grad,
    )


def solution(mesh):
    return jax.shard_map(
        functools.partial(local, mesh.shape["exp"], mesh.shape["tp"]),
        mesh=mesh,
        in_specs=(
            P(("exp", "tp"), None),
            P(),
            P(None, "tp"),
            P(None, "tp", None),
            P("tp", None),
            P(),
            P(),
            P("exp", None, None),
            P("exp", None, None),
            P(("exp", "tp"), None),
            P("exp"),
            P(("exp", "tp"), None),
        ),
        out_specs=(
            P(("exp", "tp"), None),
            P(("exp", "tp"), None),
            P(),
            P(None, "tp"),
            P(None, "tp", None),
            P("tp", None),
            P(),
            P(),
            P("exp", None, None),
            P("exp", None, None),
        ),
        check_vma=False,
    )
```

```python
import functools

import jax
import jax.numpy as jnp
from jax import lax
from jax.experimental import pallas as pl
from jax.experimental.pallas import tpu as pltpu
from jax.sharding import PartitionSpec as P

D = 1024
H = 16
KVH = 8
HD = 64
FF = 512
LANES = 128
XW = D + LANES
RW = XW + D
GROUP = 4

EPS = 1e-06
MASKED = -1e30
MESH = pl.DeviceIdType.MESH
BF = jnp.bfloat16
F32 = jnp.float32
VMEM = pltpu.VMEM
MIB = 1 << 20


def mm(a, b):
    return jnp.dot(a, b, preferred_element_type=F32)


def mm_nt(a, b):
    return lax.dot_general(a, b, (((1,), (1,)), ((), ())), preferred_element_type=F32)


def mm_tn(a, b):
    return lax.dot_general(a, b, (((0,), (0,)), ((), ())), preferred_element_type=F32)


def row_scaling(values):
    inverse = lax.rsqrt(jnp.mean(values * values, axis=-1, keepdims=True) + EPS)
    return values * inverse, inverse


def norm_backward(gradient, scaled, inverse, gain):
    weighted = gradient * gain
    inner = jnp.mean(weighted * scaled, axis=-1, keepdims=True)
    return inverse * (weighted - scaled * inner)


def block(ref, index, rows):
    return ref.at[pl.ds(pl.multiple_of(index * rows, rows), rows)]


def line_order(n):
    orders = []
    for z in range(n):
        right = list(range(n - 1, z, -1))
        left = list(range(z))
        first, second = (right, left) if len(right) >= len(left) else (left, right)
        order = []
        while first or second:
            if len(first) >= len(second):
                order.append(first.pop(0))
            else:
                order.append(second.pop(0))
        orders.append(order + [z])
    return orders


def lookup(table, z, j):
    value = jnp.int32(table[0][0])
    for a, row in enumerate(table):
        for b, entry in enumerate(row):
            value = jnp.where((z == a) & (j == b), jnp.int32(entry), value)
    return value


def greet(e, z, n, n_exp, line, plane):
    barrier = pltpu.get_barrier_semaphore()
    peers = jnp.int32(0)
    if line:

        @pl.when(z > 0)
        def _():
            pl.semaphore_signal(barrier, inc=1, device_id=(e, z - 1), device_id_type=MESH)

        @pl.when(z < n - 1)
        def _():
            pl.semaphore_signal(barrier, inc=1, device_id=(e, z + 1), device_id_type=MESH)

        peers += jnp.where(z > 0, 1, 0) + jnp.where(z < n - 1, 1, 0)
    if plane:
        chip, core = e // 2, lax.rem(e, 2)
        pl.semaphore_signal(barrier, inc=1, device_id=(e + 1 - 2 * core, z), device_id_type=MESH)

        def one(k, carry):
            there = 2 * (chip ^ k) + core
            pl.semaphore_signal(barrier, inc=1, device_id=(there, z), device_id_type=MESH)
            return carry

        lax.fori_loop(1, n_exp // 2, one, 0)
        peers += n_exp // 2
    return barrier, peers


def each(count, body, start=0):
    lax.fori_loop(start, count, lambda i, c: (body(i), c)[1], 0)


class PlaneGather:
    def __init__(self, e, z, n_exp, own, view, sems):
        self.e, self.z, self.own, self.view = e, z, own, view
        self.chip, self.core, self.chips = e // 2, lax.rem(e, 2), n_exp // 2
        self.push_s, self.push_r, self.pass_s, self.pass_r = sems
        self.square = self.chips == 4
        self.pushes = 3 if self.square else self.chips

    def mine(self, k):
        return 2 * (self.chip ^ k) + self.core

    def other(self, k):
        return 2 * (self.chip ^ k) + 1 - self.core

    def copy(self, src, dst, sems, at, device):
        return pltpu.make_async_remote_copy(
            src_ref=src,
            dst_ref=dst,
            send_sem=sems[0](at),
            recv_sem=sems[1](at),
            device_id=(device, self.z),
            device_id_type=MESH,
        )

    def push(self, k, landed=False):
        src = self.view(self.mine(k)) if landed else self.own
        dst = src if landed else self.view(self.e)
        return self.copy(src, dst, (self.push_s, self.push_r), k, self.mine(k))

    def hand(self, k, first=False, landed=False):
        there = self.view(self.other(k) if landed else self.mine(k))
        src = self.own if first else there
        return self.copy(src, there, (self.pass_s, self.pass_r), k, self.other(0))

    def across(self, half, landed=False):
        whole = self.view(self.mine(3 if landed else 1 + half))
        rows = whole.shape[0] // 2
        there = whole.at[pl.ds(half * rows, rows)]
        sems = (self.push_s, self.push_r)
        return self.copy(there, there, sems, 3 * half, self.mine(2 - half))

    def begin(self):
        each(self.pushes, lambda k: self.push(k).start(), 1)
        self.hand(0, True).start()

    def turn(self):
        def one(k):
            self.push(k, True).wait_recv()
            self.hand(k).start()

        if self.square:
            for half in range(2):
                self.push(1 + half, True).wait_recv()
                self.across(half).start()
                self.hand(1 + half).start()
        else:
            each(self.chips, one, 1)

    def turn_across(self):
        if self.square:
            for half in range(2):
                self.across(half, True).wait_recv()
            self.hand(3).start()

    def arrive(self, k):
        self.hand(k, landed=True).wait_recv()

    def drain(self):
        self.hand(0, True).wait_send()
        each(self.pushes, lambda k: self.push(k).wait_send(), 1)
        each(self.chips, lambda k: self.hand(k).wait_send(), 1)
        if self.square:
            for half in range(2):
                self.across(half).wait_send()


class LineGather:
    def __init__(self, e, z, n, rows, held, right_sems, left_sems):
        self.e, self.z, self.n, self.rows, self.held = e, z, n, rows, held
        self.sems = {1: right_sems, -1: left_sems}
        self.onward = {1: z < n - 1, -1: z > 0}

    def has(self, step, way):
        return self.z >= step if way > 0 else self.z + step < self.n

    def copy(self, step, way, landed=False):
        send, recv = self.sems[way]
        there = block(self.held, self.z - way * step, self.rows)
        return pltpu.make_async_remote_copy(
            src_ref=there,
            dst_ref=there,
            send_sem=send.at[step],
            recv_sem=recv.at[step - 1 if landed else step],
            device_id=(self.e, self.z + way),
            device_id_type=MESH,
        )

    def begin(self):
        for way in (1, -1):

            @pl.when(self.onward[way])
            def _():
                self.copy(0, way).start()

    def step(self, step):
        for way in (1, -1):

            @pl.when(self.has(step, way))
            def _():
                self.copy(step, way, True).wait_recv()

            @pl.when(self.has(step, way) & self.onward[way])
            def _():
                self.copy(step, way).start()

    def work(self, step, body):
        def one(way, carry):
            d = jnp.where(way > 0, self.z - step, self.z + step)

            @pl.when((d >= 0) & (d < self.n) & ((step > 0) | (way > 0)))
            def _():
                body(d)

            return carry

        lax.fori_loop(0, 2, one, 0)

    def drain(self):
        for step in range(self.n - 1):
            for way in (1, -1):

                @pl.when(self.has(step, way) & self.onward[way])
                def _():
                    self.copy(step, way).wait_send()


class LineScatter:
    def __init__(self, e, z, n, sent, landed, sems, part):
        self.e, self.z, self.n, self.sent, self.landed, self.part = e, z, n, sent, landed, part
        self.send, self.recv = sems
        self.table = line_order(n)

    def outgoing(self, d):
        right = d > self.z
        place = jnp.where(right | (d < self.z - 1), d, self.n)
        return pltpu.make_async_remote_copy(
            src_ref=self.sent.at[d],
            dst_ref=self.landed.at[place],
            send_sem=self.send.at[d],
            recv_sem=self.recv.at[place],
            device_id=(self.e, jnp.where(right, self.z + 1, self.z - 1)),
            device_id_type=MESH,
        )

    def incoming(self, place):
        return pltpu.make_async_remote_copy(
            src_ref=self.landed.at[place],
            dst_ref=self.landed.at[place],
            send_sem=self.send.at[0],
            recv_sem=self.recv.at[place],
            device_id=(self.e, jnp.where(self.z > 0, self.z - 1, self.z + 1)),
            device_id_type=MESH,
        )

    def step(self, j):
        d = lookup(self.table, self.z, j)
        value = self.part(d)
        upstream = jnp.where(d > self.z, self.z > 0, self.z < self.n - 1)

        @pl.when(upstream)
        def _():
            self.incoming(d).wait_recv()
            self.sent[d] = (value + self.landed[d].astype(F32)).astype(BF)

        @pl.when(jnp.logical_not(upstream))
        def _():
            self.sent[d] = value.astype(BF)

        self.outgoing(d).start()

    def finish(self, total):
        total[...] = self.part(self.z)

        @pl.when(self.z > 0)
        def _():
            self.incoming(self.z).wait_recv()
            total[...] += self.landed[self.z].astype(F32)

        @pl.when(self.z < self.n - 1)
        def _():
            self.incoming(self.n).wait_recv()
            total[...] += self.landed[self.n].astype(F32)

    def drain(self):
        for d in range(self.n):

            @pl.when(self.z != d)
            def _():
                self.outgoing(d).wait_send()


def visible_mask(d, rows, length, prefix):
    row_ids = d * rows + lax.broadcasted_iota(jnp.int32, (rows, length), 0)
    col_ids = lax.broadcasted_iota(jnp.int32, (rows, length), 1)
    return (col_ids <= row_ids) | (col_ids < prefix)


def halves(pair, low):
    pair = pair.astype(F32)
    zero = jnp.zeros_like(pair)
    return jnp.where(low, pair, zero), jnp.where(low, pltpu.roll(pair, HD, 1), zero)


def attention_forward_kernel(
    n,
    n_exp,
    tokens,
    gain1,
    w_query,
    w_pair,
    w_out,
    gain2,
    w_router,
    routes,
    prefix,
    cot,
    hidden,
    ext,
    cot_plane,
    held,
    queries,
    pairs,
    mixed,
    totals,
    sent,
    landed,
    ag_rs,
    ag_rr,
    ag_ls,
    ag_lr,
    rs_s,
    rs_r,
    push_s,
    push_r,
    pass_s,
    pass_r,
    local_sem,
):
    e, z = lax.axis_index("exp"), lax.axis_index("tp")
    rows = tokens.shape[0]
    length = rows * n
    kv_local = pairs.shape[1] // LANES
    low = lax.broadcasted_iota(jnp.int32, (rows, LANES), 1) < HD
    barrier, peers = greet(e, z, n, n_exp, True, True)
    scaled, _ = row_scaling(tokens[...].astype(F32))
    held[pl.ds(pl.multiple_of(z * rows, rows), rows)] = (scaled * gain1[...]).astype(BF)

    def project(d):
        at = pl.ds(pl.multiple_of(d * rows, rows), rows)
        normed = held[at]
        queries[at] = mm(normed, w_query[...]).astype(BF)
        pairs[at] = mm(normed, w_pair[...]).astype(BF)

    pl.semaphore_wait(barrier, peers)
    line = LineGather(e, z, n, rows, held, (ag_rs, ag_rr), (ag_ls, ag_lr))
    line.begin()
    plane = PlaneGather(
        e,
        z,
        n_exp,
        cot,
        lambda b: cot_plane.at[b],
        [lambda k, s=s: s.at[k] for s in (push_s, push_r, pass_s, pass_r)],
    )
    plane.begin()
    keep = pltpu.make_async_copy(cot, cot_plane.at[e], local_sem)
    keep.start()
    line.work(0, project)

    def gather_step(step):
        line.step(step)
        line.work(step, project)

    each(n, gather_step, 1)

    def part(d):
        at = pl.ds(pl.multiple_of(d * rows, rows), rows)
        seen = visible_mask(d, rows, length, prefix[0])
        lane = lax.broadcasted_iota(jnp.int32, (rows, LANES), 1)
        stats = jnp.zeros((rows, LANES), F32)
        for kv in range(kv_local):
            span = slice(kv * LANES, (kv + 1) * LANES)
            pair = pairs[:, span]
            outs = []
            for h, head in enumerate(halves(queries[at, span], low)):
                scores = mm_nt((head * HD**-0.5).astype(BF), pair)
                scores = jnp.where(seen, scores, MASKED)
                top = jnp.max(scores, axis=-1, keepdims=True)
                grown = jnp.exp(scores - top)
                total = jnp.sum(grown, axis=-1, keepdims=True)
                probs = (grown / total).astype(BF)
                outs.append(mm(probs, pair))
                stats = jnp.where(lane == 2 * kv + h, top + jnp.log(total), stats)
            both = jnp.where(low, pltpu.roll(outs[0], HD, 1), outs[1])
            mixed[at, span] = both.astype(BF)
        totals[at] = stats
        return mm(mixed[at], w_out[...])

    scatter = LineScatter(e, z, n, sent, landed, (rs_s, rs_r), part)
    each(n - 1, scatter.step)
    plane.turn()
    plane.turn_across()
    scatter.finish(hidden)
    hid = tokens[...].astype(F32) + hidden[...]
    hidden[...] = hid
    scaled2, _ = row_scaling(hid)
    normed2 = (scaled2 * gain2[...]).astype(BF)
    ext[:, :D] = normed2
    experts = w_router.shape[1]
    logits = mm(normed2, w_router[...])
    lane = lax.broadcasted_iota(jnp.int32, (rows, experts), 1)
    chosen = lane == routes[:, 0:1]
    for k in range(1, routes.shape[1]):
        chosen = chosen | (lane == routes[:, k : k + 1])
    logits = jnp.where(chosen, logits, MASKED)
    grown = jnp.exp(logits - jnp.max(logits, axis=-1, keepdims=True))
    grown = jnp.where(chosen, grown, 0.0)
    gates = grown / jnp.sum(grown, axis=-1, keepdims=True)
    high = gates.astype(BF)
    low_part = (gates - high.astype(F32)).astype(BF)
    mask = jnp.where(chosen, 1.0, 0.0).astype(BF)
    pad = jnp.zeros((rows, LANES - 3 * experts), BF)
    ext[:, D:] = jnp.concatenate([high, low_part, mask, pad], axis=1)
    keep.wait()
    each(n_exp // 2, plane.arrive)
    plane.drain()
    line.drain()
    scatter.drain()


def attention_forward(
    n, n_exp, tokens, gain1, w_query, w_pair, w_out, gain2, w_router, routes, prefix, cot
):
    rows = tokens.shape[0]
    length = rows * n
    qw, pw = w_query.shape[1], w_pair.shape[1]
    v = pl.BlockSpec(memory_space=VMEM)
    sem = pltpu.SemaphoreType.DMA
    return pl.pallas_call(
        functools.partial(attention_forward_kernel, n, n_exp),
        out_shape=(
            jax.ShapeDtypeStruct((rows, D), F32),
            jax.ShapeDtypeStruct((rows, XW), BF),
            jax.ShapeDtypeStruct((n_exp, rows, D), BF),
            jax.ShapeDtypeStruct((length, D), BF),
            jax.ShapeDtypeStruct((length, qw), BF),
            jax.ShapeDtypeStruct((length, pw), BF),
            jax.ShapeDtypeStruct((length, qw), BF),
            jax.ShapeDtypeStruct((length, LANES), F32),
        ),
        in_specs=[v] * 8 + [pl.BlockSpec(memory_space=pltpu.SMEM), v],
        out_specs=[v, v, pl.BlockSpec(memory_space=pl.ANY)] + [v] * 5,
        scratch_shapes=[
            pltpu.VMEM((n, rows, D), BF),
            pltpu.VMEM((n + 1, rows, D), BF),
            sem((n,)),
            sem((n,)),
            sem((n,)),
            sem((n,)),
            sem((n,)),
            sem((n + 1,)),
        ]
        + [sem((n_exp // 2,))] * 4
        + [sem],
        compiler_params=pltpu.CompilerParams(
            collective_id=1, has_side_effects=True, vmem_limit_bytes=48 * MIB
        ),
        cost_estimate=pl.CostEstimate(
            flops=2 * length * D * 4 * qw, bytes_accessed=300 * MIB, transcendentals=0
        ),
    )(tokens, gain1, w_query, w_pair, w_out, gain2, w_router, routes, prefix, cot)


def slot_rows(rows, top_k, experts):
    capacity = rows * top_k * 5 // (experts * 4)
    return -(-capacity // 16) * 16


def selection(extra, first, local_experts, slots):
    rows = extra.shape[0]
    pick = lax.broadcasted_iota(jnp.int32, (8, LANES), 1) == (
        64 + first + lax.broadcasted_iota(jnp.int32, (8, LANES), 0)
    )
    named = mm_nt(jnp.where(pick, 1.0, 0.0).astype(BF), extra)
    earlier = lax.broadcasted_iota(jnp.int32, (rows, rows), 0) < lax.broadcasted_iota(
        jnp.int32, (rows, rows), 1
    )
    place = mm(named.astype(BF), jnp.where(earlier, 1.0, 0.0).astype(BF))
    place = jnp.where(named > 0.5, place, -1.0).astype(jnp.int32)
    slot = lax.broadcasted_iota(jnp.int32, (slots, rows), 0)
    parts = [
        jnp.where(slot == place[k : k + 1, :], 1.0, 0.0) for k in range(local_experts)
    ]
    return jnp.concatenate(parts, axis=0).astype(BF)


def own_gate(extra, expert):
    lane = lax.broadcasted_iota(jnp.int32, extra.shape, 1)
    mine = (lane == expert) | (lane == 32 + expert)
    return jnp.sum(jnp.where(mine, extra.astype(F32), 0.0), axis=-1, keepdims=True)


def sigmoid(v):
    return 1.0 / (1.0 + jnp.exp(-v))


def own_experts_kernel(
    n,
    n_exp,
    local_experts,
    ext,
    cot,
    cot_plane,
    w_gate_up,
    w_down,
    hidden,
    w_router,
    gain2,
    layer_out,
    dhidden,
    dhidden_low,
    router_part,
    norm2_part,
    all_rows,
    xg,
    cg,
    wgu,
    wd,
    sel,
    xs,
    cs,
    core_in,
    chip_out,
    chip_in,
    mix_core_in,
    mix_out,
    mix_in,
    total,
    joined,
    cot_sem,
    w_sem,
    out_sem,
    column_s,
    column_r,
    ag_s,
    ag_r,
    fw_s,
    fw_r,
    core_s,
    core_r,
    chip_s,
    chip_r,
    mcore_s,
    mcore_r,
    mchip_s,
    mchip_r,
):
    e, z = lax.axis_index("exp"), lax.axis_index("tp")
    rows = ext.shape[0]
    chips = n_exp // 2
    chip, core = e // 2, lax.rem(e, 2)
    partner = 2 * chip + 1 - core
    slots = sel.shape[1] // local_experts
    first = e * local_experts
    experts = w_router.shape[1]

    loads = [
        pltpu.make_async_copy(w_gate_up, wgu, w_sem.at[0]),
        pltpu.make_async_copy(w_down, wd, w_sem.at[1]),
    ]
    for b in range(n_exp):
        loads.append(pltpu.make_async_copy(cot_plane.at[b], cg.at[b], cot_sem.at[b]))
    for load in loads:
        load.start()

    barrier, peers = greet(e, z, n, n_exp, False, True)
    for k in range(1, n):
        pl.semaphore_signal(barrier, inc=1, device_id=(e, z ^ k), device_id_type=MESH)
    xg[e] = ext[...]
    joined[:, :XW] = ext[...]
    joined[:, XW:] = cot[...]
    pl.semaphore_wait(barrier, peers + n - 1)
    plane = PlaneGather(
        e,
        z,
        n_exp,
        xg.at[e],
        lambda b: xg.at[b],
        [lambda k, s=s: s.at[k] for s in (ag_s, ag_r, fw_s, fw_r)],
    )
    there, other = plane.mine, plane.other

    def place(p):
        if chips != 4:
            return p
        return jnp.where(p == 0, 0, jnp.where(p == 1, 3, p - 1))

    pair = GROUP // 2
    each(pair, lambda p: plane.push(place(p)).start(), 1)
    plane.hand(0, True).start()

    def up_column(k, landed=False):
        return pltpu.make_async_remote_copy(
            src_ref=joined,
            dst_ref=all_rows.at[(z ^ k) if landed else z, e],
            send_sem=column_s.at[k],
            recv_sem=column_r.at[k],
            device_id=(e, z ^ k),
            device_id_type=MESH,
        )

    for k in range(1, n):
        up_column(k).start()
    for load in loads[2:]:
        load.wait()

    def gather(b):
        s = selection(xg[b, :, D:], first, local_experts, slots)
        sel[b] = s
        xs[b] = mm(s, xg[b]).astype(BF)
        cs[b] = mm(s, cg[b]).astype(BF)

    def save(b):
        return (
            pltpu.make_async_copy(xg.at[b], all_rows.at[z, b, :, pl.ds(0, XW)], out_sem.at[0, b]),
            pltpu.make_async_copy(cg.at[b], all_rows.at[z, b, :, pl.ds(XW, D)], out_sem.at[1, b]),
        )

    def save(b):
        return (
            pltpu.make_async_copy(
                xg.at[b], all_rows.at[z, b, :, pl.ds(0, XW)], out_sem.at[0, b]
            ),
            pltpu.make_async_copy(
                cg.at[b], all_rows.at[z, b, :, pl.ds(XW, D)], out_sem.at[1, b]
            ),
        )

    def members(g):
        return [f(place(pair * g + i)) for i in range(pair) for f in (there, other)]

    def expert_step(g, k):
        blocks = members(g)
        at = pl.ds(pl.multiple_of(k * slots, slots), slots)
        wide = jnp.concatenate([xs[b, at] for b in blocks], axis=0)
        gate_value = own_gate(wide[:, D:], first + k)
        units = mm(wide[:, :D], wgu[k])
        gate, up = units[:, :FF], units[:, FF:]
        sig = sigmoid(gate)
        silu = gate * sig
        active = (silu * up).astype(BF)
        made = mm(active, wd[k]).astype(BF).astype(F32)
        upstream = jnp.concatenate([cs[b, at] for b in blocks], axis=0).astype(F32)
        dgate_value = jnp.sum(upstream * made, axis=-1, keepdims=True)
        share = (gate_value * made).astype(BF)
        dmade = (gate_value * upstream).astype(BF)
        dactive = mm_nt(dmade, wd[k])
        dgate = dactive * up * sig * (1.0 + gate * (1.0 - sig))
        dunits = jnp.concatenate([dgate, dactive * silu], axis=1).astype(BF)
        dx = mm_nt(dunits, wgu[k]).astype(BF)
        lane = lax.broadcasted_iota(jnp.int32, (GROUP * slots, LANES), 1)
        high = dgate_value.astype(BF).astype(F32)
        packed = jnp.where(lane == first + k, high, 0.0)
        packed = jnp.where(lane == 32 + first + k, dgate_value - high, packed).astype(BF)
        for i, b in enumerate(blocks):
            here = slice(i * slots, (i + 1) * slots)
            xs[b, at, :D] = share[here]
            xs[b, at, D:] = packed[here]
            cs[b, at] = dx[here]

    def core_copy(k, src, dst, s, r):
        return pltpu.make_async_remote_copy(
            src_ref=src.at[other(k)],
            dst_ref=dst.at[k],
            send_sem=s.at[k],
            recv_sem=r.at[k],
            device_id=(partner, z),
            device_id_type=MESH,
        )

    def chip_copy(k, src, dst, s, r):
        return pltpu.make_async_remote_copy(
            src_ref=src.at[k],
            dst_ref=dst.at[k],
            send_sem=s.at[k],
            recv_sem=r.at[k],
            device_id=(there(k), z),
            device_id_type=MESH,
        )

    def grads_of(b):
        s = sel[b]
        return jnp.concatenate([mm_tn(s, cs[b]), mm_tn(s, xs[b, :, D:])], axis=1)

    def mix_of(b):
        return mm_tn(sel[b], xs[b, :, :D])

    def pass_on(g, of, kept, came, out, into, sems):
        core_sems, chip_sems = sems

        def give(i):
            k = place(pair * g + i)
            kept[other(k)] = of(other(k)).astype(BF)
            core_copy(k, kept, came, *core_sems).start()

        def send(i):
            k = place(pair * g + i)

            @pl.when(k > 0)
            def _():
                mine = of(there(k))
                core_copy(k, kept, came, *core_sems).wait_recv()
                out[k] = (mine + came[k].astype(F32)).astype(BF)
                chip_copy(k, out, into, *chip_sems).start()

        each(pair, give)
        each(pair, send)

    def group_step(g):
        @pl.when(g == 0)
        def _():
            gather(e)

        def turn(i):
            k = place(pair * g + i)

            @pl.when(k > 0)
            def _():
                plane.push(k, True).wait_recv()
                plane.hand(k).start()

        each(pair, turn)

        @pl.when(g == 0)
        def _():
            each(chips, lambda p: plane.push(place(p)).start(), pair)

        def pick(i):
            k = place(pair * g + i)

            @pl.when(k > 0)
            def _():
                gather(there(k))

        def pick_other(i):
            k = place(pair * g + i)
            plane.arrive(k)
            gather(other(k))

        each(pair, pick)
        each(pair, pick_other)

        def start_save(i):
            for b in (there(place(pair * g + i)), other(place(pair * g + i))):
                for copy in save(b):
                    copy.start()

        def end_save(i):
            for b in (there(place(pair * g + i)), other(place(pair * g + i))):
                for copy in save(b):
                    copy.wait()

        each(pair, start_save)

        @pl.when(g == 0)
        def _():
            for load in loads[:2]:
                load.wait()

        each(local_experts, lambda k: expert_step(g, k))
        each(pair, end_save)
        grad_sems = ((core_s, core_r), (chip_s, chip_r))
        mix_sems = ((mcore_s, mcore_r), (mchip_s, mchip_r))
        pass_on(g, grads_of, xg, core_in, chip_out, chip_in, grad_sems)
        pass_on(g, mix_of, cg, mix_core_in, mix_out, mix_in, mix_sems)

    each(n_exp // GROUP, group_step)
    plane.hand(0, True).wait_send()
    each(chips, lambda k: plane.push(k).wait_send(), 1)
    each(chips, lambda k: plane.hand(k).wait_send(), 1)
    total[...] = grads_of(e)
    core_copy(0, xg, core_in, core_s, core_r).wait_recv()
    total[...] += core_in[0].astype(F32)

    def take_grads(i):
        k = chips - 1 - i
        chip_copy(k, chip_out, chip_in, chip_s, chip_r).wait_recv()
        total[...] += chip_in[k].astype(F32)

    each(chips - 1, take_grads)
    extra = ext[:, D:].astype(F32)
    gates = extra[:, :experts] + extra[:, experts : 2 * experts]
    dgates = total[:, D : D + experts] + total[:, D + experts : D + 2 * experts]
    dlogits = gates * (dgates - jnp.sum(gates * dgates, axis=-1, keepdims=True))
    dlogits = dlogits.astype(BF)
    normed2 = ext[:, :D]
    router_part[...] = mm_tn(dlogits, normed2)
    dnormed2 = total[:, :D] + mm_nt(dlogits, w_router[...])
    scaled2, inverse2 = row_scaling(hidden[...])
    norm2_part[...] = jnp.broadcast_to(
        jnp.sum(dnormed2 * scaled2, axis=0, keepdims=True), norm2_part.shape
    )
    back = cot[...].astype(F32) + norm_backward(dnormed2, scaled2, inverse2, gain2[...])
    dhidden[...] = back
    dhidden_low[...] = back.astype(BF)

    total[:, :D] = hidden[...] + mix_of(e)
    core_copy(0, cg, mix_core_in, mcore_s, mcore_r).wait_recv()
    total[:, :D] += mix_core_in[0].astype(F32)

    def take_mix(i):
        k = chips - 1 - i
        chip_copy(k, mix_out, mix_in, mchip_s, mchip_r).wait_recv()
        total[:, :D] += mix_in[k].astype(F32)

    each(chips - 1, take_mix)
    layer_out[...] = total[:, :D].astype(BF)

    def sent_to_core(k):
        core_copy(k, xg, core_in, core_s, core_r).wait_send()
        core_copy(k, cg, mix_core_in, mcore_s, mcore_r).wait_send()

    def sent_to_chip(i):
        chip_copy(i + 1, chip_out, chip_in, chip_s, chip_r).wait_send()
        chip_copy(i + 1, mix_out, mix_in, mchip_s, mchip_r).wait_send()

    each(chips, sent_to_core)
    each(chips - 1, sent_to_chip)
    for k in range(1, n):
        up_column(k, True).wait_recv()
        up_column(k).wait_send()


def own_experts(n, n_exp, ext, cot, cot_plane, w_gate_up, w_down, hidden, w_router, gain2, slots):
    rows = ext.shape[0]
    local_experts = w_gate_up.shape[0]
    experts = w_router.shape[1]
    chips = n_exp // 2
    v = pl.BlockSpec(memory_space=VMEM)
    hbm = pl.BlockSpec(memory_space=pl.ANY)
    sem = pltpu.SemaphoreType.DMA
    taken = n_exp * local_experts * slots
    return pl.pallas_call(
        functools.partial(own_experts_kernel, n, n_exp, local_experts),
        out_shape=(
            jax.ShapeDtypeStruct((rows, D), BF),
            jax.ShapeDtypeStruct((rows, D), F32),
            jax.ShapeDtypeStruct((rows, D), BF),
            jax.ShapeDtypeStruct((experts, D), F32),
            jax.ShapeDtypeStruct((8, D), F32),
            jax.ShapeDtypeStruct((n, n_exp, rows, RW), BF),
        ),
        in_specs=[v, v, hbm, hbm, hbm, v, v, v],
        out_specs=[v] * 5 + [hbm],
        scratch_shapes=[
            pltpu.VMEM((n_exp, rows, XW), BF),
            pltpu.VMEM((n_exp, rows, D), BF),
            pltpu.VMEM(w_gate_up.shape, BF),
            pltpu.VMEM(w_down.shape, BF),
            pltpu.VMEM((n_exp, local_experts * slots, rows), BF),
            pltpu.VMEM((n_exp, local_experts * slots, XW), BF),
            pltpu.VMEM((n_exp, local_experts * slots, D), BF),
            pltpu.VMEM((chips, rows, XW), BF),
            pltpu.VMEM((chips, rows, XW), BF),
            pltpu.VMEM((chips, rows, XW), BF),
            pltpu.VMEM((chips, rows, D), BF),
            pltpu.VMEM((chips, rows, D), BF),
            pltpu.VMEM((chips, rows, D), BF),
            pltpu.VMEM((rows, XW), F32),
            pltpu.VMEM((rows, RW), BF),
            sem((n_exp,)),
            sem((2,)),
            sem((2, n_exp)),
            sem((n,)),
            sem((n,)),
        ]
        + [sem((chips,))] * 12,
        compiler_params=pltpu.CompilerParams(
            collective_id=2, has_side_effects=True, vmem_limit_bytes=63 * MIB
        ),
        cost_estimate=pl.CostEstimate(
            flops=2 * taken * 6 * D * FF, bytes_accessed=300 * MIB, transcendentals=0
        ),
    )(ext, cot, cot_plane, w_gate_up, w_down, hidden, w_router, gain2)


def expert_middle(x, gate_value, upstream, w_gate_up, w_down):
    units = mm(x, w_gate_up)
    gate, up = units[:, :FF], units[:, FF:]
    sig = sigmoid(gate)
    silu = gate * sig
    dmade = (gate_value * upstream.astype(F32)).astype(BF)
    dactive = mm_nt(dmade, w_down)
    dgate = dactive * up * sig * (1.0 + gate * (1.0 - sig))
    return dmade, (silu * up).astype(BF), dgate.astype(BF), (dactive * silu).astype(BF)


def expert_grads_kernel(
    blocks,
    groups,
    early,
    local_experts,
    rows_all,
    *refs,
):
    first = lax.axis_index("exp") * local_experts + early
    k, g = pl.program_id(0), pl.program_id(1)
    refs = list(refs)
    w_gate_up, w_down = refs.pop(0), refs.pop(0)
    done = (refs.pop(0), refs.pop(0)) if early else None
    gate_up_grad, down_grad, rbuf, kept_x, kept_dy, kept_active, kept_dunits = refs[:7]
    acc_up, acc_down, sems, out_sems, copy_sems = refs[7:]
    slots = kept_x.shape[0] // blocks
    chunks = blocks // GROUP
    size = GROUP * slots
    last = local_experts - early - 1

    def brought():
        return (
            pltpu.make_async_copy(done[0], acc_up.at[pl.ds(0, early)], copy_sems.at[0]),
            pltpu.make_async_copy(done[1], acc_down.at[pl.ds(0, early)], copy_sems.at[1]),
        )

    def taken():
        return (
            pltpu.make_async_copy(
                acc_up.at[pl.ds(0, early)], gate_up_grad.at[pl.ds(0, early)], copy_sems.at[0]
            ),
            pltpu.make_async_copy(
                acc_down.at[pl.ds(0, early)], down_grad.at[pl.ds(0, early)], copy_sems.at[1]
            ),
        )

    opening = (k == 0) & (g == 0)
    if early:

        @pl.when(opening)
        def _():
            for copy in brought():
                copy.start()

    def load(c, slot):
        at = pl.ds(g * blocks + c * GROUP, GROUP)
        return pltpu.make_async_copy(rows_all.at[at], rbuf.at[slot], sems.at[slot])

    load(0, 0).start()

    def chunk(c, carry):
        slot = lax.rem(c, 2)

        @pl.when(c + 1 < chunks)
        def _():
            load(c + 1, 1 - slot).start()

        load(c, slot).wait()
        if early:

            @pl.when(opening & (c == 2))
            def _():
                for copy in brought():
                    copy.wait()
                for copy in taken():
                    copy.start()

        wide = []
        for i in range(GROUP):
            s = selection(rbuf[slot, i, :, D:XW], first + k, 1, slots)
            wide.append(mm(s, rbuf[slot, i]))
        wide = jnp.concatenate(wide, axis=0)
        x = wide[:, :D].astype(BF)
        made = expert_middle(
            x, own_gate(wide[:, D:XW], first + k), wide[:, XW:], w_gate_up[0], w_down[0]
        )
        at = pl.ds(pl.multiple_of(c * size, size), size)
        kept_x[at] = x
        kept_dy[at] = made[0]
        kept_active[at] = made[1]
        kept_dunits[at, :FF] = made[2]
        kept_dunits[at, FF:] = made[3]
        return carry

    lax.fori_loop(0, chunks, chunk, 0)
    bank = lax.rem(k, 2)
    if early:

        @pl.when(opening)
        def _():
            for copy in taken():
                copy.wait()

    def store(kk):
        b = lax.rem(kk, 2)
        return (
            pltpu.make_async_copy(acc_up.at[b], gate_up_grad.at[early + kk], out_sems.at[0, b]),
            pltpu.make_async_copy(acc_down.at[b], down_grad.at[early + kk], out_sems.at[1, b]),
        )

    @pl.when((g == 0) & (k >= 2))
    def _():
        for copy in store(k - 2):
            copy.wait()

    def add(out, at, value):
        if groups == 1:
            out[bank, at] = value
        else:

            @pl.when(g == 0)
            def _():
                out[bank, at] = value

            @pl.when(g > 0)
            def _():
                out[bank, at] += value

    tile = 256

    def up_tile(m, carry):
        at = pl.ds(pl.multiple_of(m * tile, tile), tile)
        add(acc_up, at, mm_tn(kept_x[:, at], kept_dunits[...]))
        return carry

    lax.fori_loop(0, D // tile, up_tile, 0)

    def down_tile(m, carry):
        at = pl.ds(pl.multiple_of(m * tile, tile), tile)
        add(acc_down, at, mm_tn(kept_active[:, at], kept_dy[...]))
        return carry

    lax.fori_loop(0, FF // tile, down_tile, 0)

    @pl.when(g == groups - 1)
    def _():
        for copy in store(k):
            copy.start()

    @pl.when((g == groups - 1) & (k == last))
    def _():
        for copy in store(k):
            copy.wait()
        if last > 0:
            for copy in store(k - 1):
                copy.wait()


def expert_grads(rows_all, w_gate_up, w_down, done, slots):
    total, rows = rows_all.shape[:2]
    local_experts = w_gate_up.shape[0]
    early = done[0].shape[0] if done else 0
    assert early <= 2
    blocks = min(total, 32)
    groups = total // blocks
    kept = blocks * slots
    hbm = pl.BlockSpec(memory_space=pl.ANY)
    sem = pltpu.SemaphoreType.DMA
    return pl.pallas_call(
        functools.partial(expert_grads_kernel, blocks, groups, early, local_experts),
        grid=(local_experts - early, groups),
        out_shape=(
            jax.ShapeDtypeStruct((local_experts, D, 2 * FF), F32),
            jax.ShapeDtypeStruct((local_experts, FF, D), F32),
        ),
        in_specs=[
            hbm,
            pl.BlockSpec((1, D, 2 * FF), lambda k, g: (k + early, 0, 0)),
            pl.BlockSpec((1, FF, D), lambda k, g: (k + early, 0, 0)),
        ]
        + [hbm] * len(done),
        out_specs=[hbm, hbm],
        scratch_shapes=[
            pltpu.VMEM((2, GROUP, rows, RW), BF),
            pltpu.VMEM((kept, D), BF),
            pltpu.VMEM((kept, D), BF),
            pltpu.VMEM((kept, FF), BF),
            pltpu.VMEM((kept, 2 * FF), BF),
            pltpu.VMEM((2, D, 2 * FF), F32),
            pltpu.VMEM((2, FF, D), F32),
            sem((2,)),
            sem((2, 2)),
            sem((2,)),
        ],
        compiler_params=pltpu.CompilerParams(vmem_limit_bytes=60 * MIB),
        cost_estimate=pl.CostEstimate(
            flops=2 * total * slots * local_experts * 6 * D * FF,
            bytes_accessed=300 * MIB,
            transcendentals=0,
        ),
    )(rows_all, w_gate_up, w_down, *done)


def backward_kernel(n, n_exp, early, local_experts, *refs):
    refs = list(refs)

    def take(count):
        got = refs[:count]
        del refs[:count]
        return got

    dhidden_low, dhidden, tokens, gain1, held, queries, pairs, mixed, totals = take(9)
    w_query, w_pair, w_out, prefix, _ = take(5)
    if early:
        w_gate_up, w_down = take(2)
    input_grad, query_grad, pair_grad, out_grad, norm1, all_rows = take(6)
    if early:
        gate_up_grad, down_grad = take(2)
    dfull, dqueries, dpairs, dpairs_low, sent, landed, line_norms, plane_norms = take(8)
    ag_rs, ag_rr, ag_ls, ag_lr, rs_s, rs_r, push_s, push_r, pass_s, pass_r = take(10)
    nz_s, nz_r, np_s, np_r = take(4)
    if early:
        tokens_in, wgu, wd, acc_up, acc_down, kept_x, kept_c, kept_active, kept_dunits = take(9)
        load_s, w_sem, out_sem = take(3)

    e, z = lax.axis_index("exp"), lax.axis_index("tp")
    rows = tokens.shape[0]
    length = rows * n
    kv_local = pairs.shape[1] // LANES
    low = lax.broadcasted_iota(jnp.int32, (rows, LANES), 1) < HD
    scale = HD**-0.5
    first = e * local_experts

    if early:
        weights = [
            pltpu.make_async_copy(w_gate_up.at[pl.ds(0, early)], wgu, w_sem.at[0]),
            pltpu.make_async_copy(w_down.at[pl.ds(0, early)], wd, w_sem.at[1]),
        ]
        for copy in weights:
            copy.start()

    barrier = pltpu.get_barrier_semaphore()

    def greet_plane(k):
        pl.semaphore_signal(barrier, inc=1, device_id=(e ^ k, z), device_id_type=MESH)

    def greet_line(k):
        pl.semaphore_signal(barrier, inc=1, device_id=(e, z ^ k), device_id_type=MESH)

    each(n_exp, greet_plane, 1)
    each(n, greet_line, 1)
    dfull[pl.ds(pl.multiple_of(z * rows, rows), rows)] = dhidden_low[...]
    dpairs[...] = jnp.zeros_like(dpairs)
    pl.semaphore_wait(barrier, n_exp + n - 2)

    line = LineGather(e, z, n, rows, dfull, (ag_rs, ag_rr), (ag_ls, ag_lr))
    line.begin()

    def plane(i):
        return PlaneGather(
            e,
            z,
            n_exp,
            all_rows.at[z ^ i, e],
            lambda b: all_rows.at[z ^ i, b],
            [lambda k, s=s: s.at[i, k] for s in (push_s, push_r, pass_s, pass_r)],
        )

    plane(1).begin()

    def attend(d):
        at = pl.ds(pl.multiple_of(d * rows, rows), rows)
        seen = visible_mask(d, rows, length, prefix[0])
        dmixed = mm_nt(dfull[at], w_out[...]).astype(BF)
        stats = totals[at]
        for kv in range(kv_local):
            span = slice(kv * LANES, (kv + 1) * LANES)
            pair = pairs[:, span]
            outs = []
            added = jnp.zeros((length, LANES), F32)
            heads = halves(queries[at, span], low)
            grads = halves(dmixed[:, span], low)
            for h in range(2):
                head = (heads[h] * scale).astype(BF)
                grad = pltpu.roll(grads[h], HD, 1).astype(BF)
                stat = 2 * kv + h
                scores = mm_nt(head, pair)
                probs = jnp.where(seen, jnp.exp(scores - stats[:, stat : stat + 1]), 0.0)
                dprobs = mm_nt(grad, pair)
                inner = jnp.sum(probs * dprobs, axis=-1, keepdims=True)
                dscores = (probs * (dprobs - inner)).astype(BF)
                outs.append(mm(dscores, pair) * scale)
                added += mm_tn(dscores, head) + mm_tn(probs.astype(BF), grad)
            both = jnp.where(low, outs[0], pltpu.roll(outs[1], HD, 1))
            dqueries[at, span] = both.astype(BF)
            dpairs[:, span] += added

    def part(d):
        at = pl.ds(pl.multiple_of(d * rows, rows), rows)
        return mm_nt(dqueries[at], w_query[...]) + mm_nt(dpairs_low[at], w_pair[...])

    scatter = LineScatter(e, z, n, sent, landed, (rs_s, rs_r), part)

    def line_norm(k, landed=False):
        return pltpu.make_async_remote_copy(
            src_ref=line_norms.at[z],
            dst_ref=line_norms.at[(z ^ k) if landed else z],
            send_sem=nz_s.at[k],
            recv_sem=nz_r.at[k],
            device_id=(e, z ^ k),
            device_id_type=MESH,
        )

    def plane_norm(k, landed=False):
        return pltpu.make_async_remote_copy(
            src_ref=plane_norms.at[e],
            dst_ref=plane_norms.at[(e ^ k) if landed else e],
            send_sem=np_s.at[k],
            recv_sem=np_r.at[k],
            device_id=(e ^ k, z),
            device_id_type=MESH,
        )

    def event(t):
        @pl.when((t > 0) & (t < n))
        def _():
            line.step(t)

        @pl.when(t < n)
        def _():
            line.work(t, attend)

        @pl.when(t == n)
        def _():
            dpairs_low[...] = dpairs[...].astype(BF)

        @pl.when((t >= n) & (t < 2 * n - 1))
        def _():
            scatter.step(t - n)

        @pl.when(t == 2 * n - 1)
        def _():
            query_grad[...] = mm_tn(held[...], dqueries[...]).astype(BF)
            pair_grad[...] = mm_tn(held[...], dpairs_low[...]).astype(BF)
            out_grad[...] = mm_tn(mixed[...], dfull[...]).astype(BF)

        @pl.when(t == 2 * n)
        def _():
            scatter.finish(input_grad)
            dnormed1 = input_grad[...]
            scaled, inverse = row_scaling(tokens[...].astype(F32))
            total = jnp.sum(dnormed1 * scaled, axis=0, keepdims=True)
            line_norms[z] = jnp.concatenate(
                [total[:, k * LANES : (k + 1) * LANES] for k in range(D // LANES)], axis=0
            )
            each(n, lambda k: line_norm(k).start(), 1)
            back = dhidden[...] + norm_backward(dnormed1, scaled, inverse, gain1[...])
            input_grad[...] = back

        @pl.when(t == 2 * n + 1)
        def _():
            each(n, lambda k: line_norm(k, True).wait_recv(), 1)
            total = line_norms[0]
            for k in range(1, n):
                total = total + line_norms[k]
            plane_norms[e] = total
            each(n_exp, lambda k: plane_norm(k).start(), 1)

    events = 2 * n + 2
    steps = n * (1 + early) if early else 0

    def turn(i):
        plane(i).turn()

        @pl.when(i + 1 < n)
        def _():
            plane(i + 1).begin()

    if early:
        slots = kept_x.shape[1] // n_exp
        acc_up[...] = jnp.zeros_like(acc_up)
        acc_down[...] = jnp.zeros_like(acc_down)
        for copy in weights:
            copy.wait()

        def one_plane(i, carry):
            @pl.when(i > 0)
            def _():
                each(n_exp // 2, plane(i).arrive)

            def load(b):
                return pltpu.make_async_copy(
                    all_rows.at[z ^ i, b], tokens_in.at[b], load_s.at[b]
                )

            each(n_exp, lambda b: load(b).start())

            def pick(b):
                load(b).wait()
                s = selection(tokens_in[b, :, D:XW], first, early, slots)
                got = mm(s, tokens_in[b]).astype(BF)
                at = pl.ds(pl.multiple_of(b * slots, slots), slots)
                for k in range(early):
                    here = got[k * slots : (k + 1) * slots]
                    kept_x[k, at] = here[:, :XW]
                    kept_c[k, at] = here[:, XW:]

            each(n_exp, pick)
            event(i * (1 + early))

            def expert(k):
                gate_value = own_gate(kept_x[k, :, D:], first + k)
                x = kept_x[k, :, :D]
                made = expert_middle(x, gate_value, kept_c[k], wgu[k], wd[k])
                kept_c[k] = made[0]
                kept_active[...] = made[1]
                kept_dunits[:, :FF] = made[2]
                kept_dunits[:, FF:] = made[3]
                acc_up[k] += mm_tn(kept_x[k, :, :D], kept_dunits[...])
                acc_down[k] += mm_tn(kept_active[...], kept_c[k])
                event(i * (1 + early) + 1 + k)

                @pl.when((k == 0) & (i + 1 < n))
                def _():
                    turn(i + 1)

            each(early, expert)

            @pl.when(i + 1 < n)
            def _():
                plane(i + 1).turn_across()

            return carry

        lax.fori_loop(0, n, one_plane, 0)
        stores = [
            pltpu.make_async_copy(acc_up, gate_up_grad, out_sem.at[0]),
            pltpu.make_async_copy(acc_down, down_grad, out_sem.at[1]),
        ]
        for copy in stores:
            copy.start()
    each(max(events, steps), event, steps)
    if early:
        for copy in stores:
            copy.wait()
    else:

        def one_plane(i):
            turn(i)
            plane(i).turn_across()

        each(n, one_plane, 1)
        each(n, lambda i: each(n_exp // 2, plane(i).arrive), 1)
    each(n_exp, lambda k: plane_norm(k, True).wait_recv(), 1)
    total = plane_norms[0]
    for k in range(1, n_exp):
        total = total + plane_norms[k]
    norm1[...] = total
    each(n, lambda i: plane(i).drain(), 1)
    each(n, lambda k: line_norm(k).wait_send(), 1)
    each(n_exp, lambda k: plane_norm(k).wait_send(), 1)
    line.drain()
    scatter.drain()


def backward(n, n_exp, slots, whole, prefix, all_rows, weights):
    tokens, held = whole[2], whole[4]
    rows = tokens.shape[0]
    length = rows * n
    qw, pw = whole[9].shape[1], whole[10].shape[1]
    local_experts = weights[0].shape[0]
    early = local_experts // 2
    v = pl.BlockSpec(memory_space=VMEM)
    hbm = pl.BlockSpec(memory_space=pl.ANY)
    sem = pltpu.SemaphoreType.DMA
    chips = n_exp // 2
    outs = [
        (jax.ShapeDtypeStruct((rows, D), F32), v),
        (jax.ShapeDtypeStruct((D, qw), BF), v),
        (jax.ShapeDtypeStruct((D, pw), BF), v),
        (jax.ShapeDtypeStruct((qw, D), BF), v),
        (jax.ShapeDtypeStruct((D // LANES, LANES), F32), v),
        (jax.ShapeDtypeStruct((n, n_exp, rows, RW), BF), hbm),
    ]
    scratch = [
        pltpu.VMEM((length, D), BF),
        pltpu.VMEM((length, qw), BF),
        pltpu.VMEM((length, pw), F32),
        pltpu.VMEM((length, pw), BF),
        pltpu.VMEM((n, rows, D), BF),
        pltpu.VMEM((n + 1, rows, D), BF),
        pltpu.VMEM((n, D // LANES, LANES), F32),
        pltpu.VMEM((n_exp, D // LANES, LANES), F32),
        sem((n,)),
        sem((n,)),
        sem((n,)),
        sem((n,)),
        sem((n,)),
        sem((n + 1,)),
    ]
    scratch += [sem((n, chips))] * 4
    scratch += [sem((n,)), sem((n,)), sem((n_exp,)), sem((n_exp,))]
    if early:
        kept = n_exp * slots
        outs += [
            (jax.ShapeDtypeStruct((early, D, 2 * FF), F32), hbm),
            (jax.ShapeDtypeStruct((early, FF, D), F32), hbm),
        ]
        scratch += [
            pltpu.VMEM((n_exp, rows, RW), BF),
            pltpu.VMEM((early, D, 2 * FF), BF),
            pltpu.VMEM((early, FF, D), BF),
            pltpu.VMEM((early, D, 2 * FF), F32),
            pltpu.VMEM((early, FF, D), F32),
            pltpu.VMEM((early, kept, XW), BF),
            pltpu.VMEM((early, kept, D), BF),
            pltpu.VMEM((kept, FF), BF),
            pltpu.VMEM((kept, 2 * FF), BF),
            sem((n_exp,)),
            sem((2,)),
            sem((2,)),
        ]
    return pl.pallas_call(
        functools.partial(backward_kernel, n, n_exp, early, local_experts),
        out_shape=tuple(shape for shape, _ in outs),
        in_specs=[v] * len(whole)
        + [pl.BlockSpec(memory_space=pltpu.SMEM)]
        + [hbm] * (1 + (2 if early else 0)),
        out_specs=tuple(spec for _, spec in outs),
        input_output_aliases={len(whole) + 1: 5},
        scratch_shapes=scratch,
        compiler_params=pltpu.CompilerParams(
            collective_id=3, has_side_effects=True, vmem_limit_bytes=62 * MIB
        ),
        cost_estimate=pl.CostEstimate(
            flops=2 * length * D * 8 * qw, bytes_accessed=300 * MIB, transcendentals=0
        ),
    )(*whole, prefix, all_rows, *(weights if early else ()))


def local(
    n_exp,
    n_tp,
    tokens,
    norm1_gain,
    w_query,
    w_key_value,
    w_out,
    norm2_gain,
    w_router,
    w_gate_up,
    w_down,
    routes,
    prefix,
    cotangent,
):
    rows = tokens.shape[0]
    experts = w_router.shape[1]
    slots = slot_rows(rows, routes.shape[1], experts)
    w_pair = w_key_value.reshape(D, -1)
    gain1, gain2 = norm1_gain.reshape(1, D), norm2_gain.reshape(1, D)
    hidden, ext, cot_plane, held, queries, pairs, mixed, totals = attention_forward(
        n_tp,
        n_exp,
        tokens,
        gain1,
        w_query,
        w_pair,
        w_out,
        gain2,
        w_router,
        routes,
        prefix,
        cotangent,
    )
    layer_out, dhidden, dhidden_low, router_part, norm2_part, all_rows = own_experts(
        n_tp,
        n_exp,
        ext,
        cotangent,
        cot_plane,
        w_gate_up,
        w_down,
        hidden,
        w_router,
        gain2,
        slots,
    )
    small = jnp.concatenate([router_part, norm2_part], axis=0)
    small = lax.psum(small, ("exp", "tp"))
    whole = (dhidden_low, dhidden, tokens, gain1, held, queries, pairs, mixed, totals)
    whole += (w_query, w_pair, w_out)
    made = backward(n_tp, n_exp, slots, whole, prefix, all_rows, (w_gate_up, w_down))
    input_grad, query_grad, pair_grad, out_grad, norm1, all_rows = made[:6]
    gate_up_grad, down_grad = expert_grads(
        all_rows.reshape(n_exp * n_tp, rows, RW), w_gate_up, w_down, made[6:], slots
    )
    query_grad, pair_grad, out_grad = (
        lax.psum(query_grad, "exp").astype(F32),
        lax.psum(pair_grad, "exp").astype(F32),
        lax.psum(out_grad, "exp").astype(F32),
    )
    return (
        layer_out,
        input_grad,
        norm1.reshape(D),
        query_grad,
        pair_grad.reshape(w_key_value.shape),
        out_grad,
        small[experts],
        small[:experts].T,
        gate_up_grad,
        down_grad,
    )


def solution(mesh):
    return jax.shard_map(
        functools.partial(local, mesh.shape["exp"], mesh.shape["tp"]),
        mesh=mesh,
        in_specs=(
            P(("exp", "tp"), None),
            P(),
            P(None, "tp"),
            P(None, "tp", None),
            P("tp", None),
            P(),
            P(),
            P("exp", None, None),
            P("exp", None, None),
            P(("exp", "tp"), None),
            P("exp"),
            P(("exp", "tp"), None),
        ),
        out_specs=(
            P(("exp", "tp"), None),
            P(("exp", "tp"), None),
            P(),
            P(None, "tp"),
            P(None, "tp", None),
            P("tp", None),
            P(),
            P(),
            P("exp", None, None),
            P("exp", None, None),
        ),
        check_vma=False,
    )
```

```python
import functools

import jax
import jax.numpy as jnp
from jax import lax
from jax.experimental import pallas as pl
from jax.experimental.pallas import tpu as pltpu
from jax.sharding import PartitionSpec as P

D = 1024
H = 16
KVH = 8
HD = 64
FF = 512
LANES = 128
XW = D + LANES
RW = XW + D
GROUP = 4

EPS = 1e-06
MASKED = -1e30
MESH = pl.DeviceIdType.MESH
BF = jnp.bfloat16
F32 = jnp.float32
VMEM = pltpu.VMEM
MIB = 1 << 20


def mm(a, b):
    return jnp.dot(a, b, preferred_element_type=F32)


def mm_nt(a, b):
    return lax.dot_general(a, b, (((1,), (1,)), ((), ())), preferred_element_type=F32)


def mm_tn(a, b):
    return lax.dot_general(a, b, (((0,), (0,)), ((), ())), preferred_element_type=F32)


def row_scaling(values):
    inverse = lax.rsqrt(jnp.mean(values * values, axis=-1, keepdims=True) + EPS)
    return values * inverse, inverse


def norm_backward(gradient, scaled, inverse, gain):
    weighted = gradient * gain
    inner = jnp.mean(weighted * scaled, axis=-1, keepdims=True)
    return inverse * (weighted - scaled * inner)


def block(ref, index, rows):
    return ref.at[pl.ds(pl.multiple_of(index * rows, rows), rows)]


def line_order(n):
    orders = []
    for z in range(n):
        right = list(range(n - 1, z, -1))
        left = list(range(z))
        first, second = (right, left) if len(right) >= len(left) else (left, right)
        order = []
        while first or second:
            if len(first) >= len(second):
                order.append(first.pop(0))
            else:
                order.append(second.pop(0))
        orders.append(order + [z])
    return orders


def lookup(table, z, j):
    value = jnp.int32(table[0][0])
    for a, row in enumerate(table):
        for b, entry in enumerate(row):
            value = jnp.where((z == a) & (j == b), jnp.int32(entry), value)
    return value


def greet(e, z, n, n_exp, line, plane):
    barrier = pltpu.get_barrier_semaphore()
    peers = jnp.int32(0)
    if line:

        @pl.when(z > 0)
        def _():
            pl.semaphore_signal(barrier, inc=1, device_id=(e, z - 1), device_id_type=MESH)

        @pl.when(z < n - 1)
        def _():
            pl.semaphore_signal(barrier, inc=1, device_id=(e, z + 1), device_id_type=MESH)

        peers += jnp.where(z > 0, 1, 0) + jnp.where(z < n - 1, 1, 0)
    if plane:
        chip, core = e // 2, lax.rem(e, 2)
        pl.semaphore_signal(barrier, inc=1, device_id=(e + 1 - 2 * core, z), device_id_type=MESH)

        def one(k, carry):
            there = 2 * (chip ^ k) + core
            pl.semaphore_signal(barrier, inc=1, device_id=(there, z), device_id_type=MESH)
            return carry

        lax.fori_loop(1, n_exp // 2, one, 0)
        peers += n_exp // 2
    return barrier, peers


def each(count, body, start=0):
    lax.fori_loop(start, count, lambda i, c: (body(i), c)[1], 0)


class PlaneGather:
    def __init__(self, e, z, n_exp, own, view, sems):
        self.e, self.z, self.own, self.view = e, z, own, view
        self.chip, self.core, self.chips = e // 2, lax.rem(e, 2), n_exp // 2
        self.push_s, self.push_r, self.pass_s, self.pass_r = sems
        self.square = self.chips == 4
        self.pushes = 3 if self.square else self.chips

    def mine(self, k):
        return 2 * (self.chip ^ k) + self.core

    def other(self, k):
        return 2 * (self.chip ^ k) + 1 - self.core

    def copy(self, src, dst, sems, at, device):
        return pltpu.make_async_remote_copy(
            src_ref=src,
            dst_ref=dst,
            send_sem=sems[0](at),
            recv_sem=sems[1](at),
            device_id=(device, self.z),
            device_id_type=MESH,
        )

    def push(self, k, landed=False):
        src = self.view(self.mine(k)) if landed else self.own
        dst = src if landed else self.view(self.e)
        return self.copy(src, dst, (self.push_s, self.push_r), k, self.mine(k))

    def hand(self, k, first=False, landed=False):
        there = self.view(self.other(k) if landed else self.mine(k))
        src = self.own if first else there
        return self.copy(src, there, (self.pass_s, self.pass_r), k, self.other(0))

    def across(self, half, landed=False):
        whole = self.view(self.mine(3 if landed else 1 + half))
        rows = whole.shape[0] // 2
        there = whole.at[pl.ds(half * rows, rows)]
        sems = (self.push_s, self.push_r)
        return self.copy(there, there, sems, 3 * half, self.mine(2 - half))

    def begin(self):
        each(self.pushes, lambda k: self.push(k).start(), 1)
        self.hand(0, True).start()

    def turn(self):
        def one(k):
            self.push(k, True).wait_recv()
            self.hand(k).start()

        if self.square:
            for half in range(2):
                self.push(1 + half, True).wait_recv()
                self.across(half).start()
                self.hand(1 + half).start()
        else:
            each(self.chips, one, 1)

    def turn_across(self):
        if self.square:
            for half in range(2):
                self.across(half, True).wait_recv()
            self.hand(3).start()

    def arrive(self, k):
        self.hand(k, landed=True).wait_recv()

    def drain(self):
        self.hand(0, True).wait_send()
        each(self.pushes, lambda k: self.push(k).wait_send(), 1)
        each(self.chips, lambda k: self.hand(k).wait_send(), 1)
        if self.square:
            for half in range(2):
                self.across(half).wait_send()


class LineGather:
    def __init__(self, e, z, n, rows, held, right_sems, left_sems):
        self.e, self.z, self.n, self.rows, self.held = e, z, n, rows, held
        self.sems = {1: right_sems, -1: left_sems}
        self.onward = {1: z < n - 1, -1: z > 0}

    def has(self, step, way):
        return self.z >= step if way > 0 else self.z + step < self.n

    def copy(self, step, way, landed=False):
        send, recv = self.sems[way]
        there = block(self.held, self.z - way * step, self.rows)
        return pltpu.make_async_remote_copy(
            src_ref=there,
            dst_ref=there,
            send_sem=send.at[step],
            recv_sem=recv.at[step - 1 if landed else step],
            device_id=(self.e, self.z + way),
            device_id_type=MESH,
        )

    def begin(self):
        for way in (1, -1):

            @pl.when(self.onward[way])
            def _():
                self.copy(0, way).start()

    def step(self, step):
        for way in (1, -1):

            @pl.when(self.has(step, way))
            def _():
                self.copy(step, way, True).wait_recv()

            @pl.when(self.has(step, way) & self.onward[way])
            def _():
                self.copy(step, way).start()

    def work(self, step, body):
        def one(way, carry):
            d = jnp.where(way > 0, self.z - step, self.z + step)

            @pl.when((d >= 0) & (d < self.n) & ((step > 0) | (way > 0)))
            def _():
                body(d)

            return carry

        lax.fori_loop(0, 2, one, 0)

    def drain(self):
        for step in range(self.n - 1):
            for way in (1, -1):

                @pl.when(self.has(step, way) & self.onward[way])
                def _():
                    self.copy(step, way).wait_send()


class LineScatter:
    def __init__(self, e, z, n, sent, landed, sems, part):
        self.e, self.z, self.n, self.sent, self.landed, self.part = e, z, n, sent, landed, part
        self.send, self.recv = sems
        self.table = line_order(n)

    def outgoing(self, d):
        right = d > self.z
        place = jnp.where(right | (d < self.z - 1), d, self.n)
        return pltpu.make_async_remote_copy(
            src_ref=self.sent.at[d],
            dst_ref=self.landed.at[place],
            send_sem=self.send.at[d],
            recv_sem=self.recv.at[place],
            device_id=(self.e, jnp.where(right, self.z + 1, self.z - 1)),
            device_id_type=MESH,
        )

    def incoming(self, place):
        return pltpu.make_async_remote_copy(
            src_ref=self.landed.at[place],
            dst_ref=self.landed.at[place],
            send_sem=self.send.at[0],
            recv_sem=self.recv.at[place],
            device_id=(self.e, jnp.where(self.z > 0, self.z - 1, self.z + 1)),
            device_id_type=MESH,
        )

    def step(self, j):
        d = lookup(self.table, self.z, j)
        value = self.part(d)
        upstream = jnp.where(d > self.z, self.z > 0, self.z < self.n - 1)

        @pl.when(upstream)
        def _():
            self.incoming(d).wait_recv()
            self.sent[d] = (value + self.landed[d].astype(F32)).astype(BF)

        @pl.when(jnp.logical_not(upstream))
        def _():
            self.sent[d] = value.astype(BF)

        self.outgoing(d).start()

    def finish(self, total):
        total[...] = self.part(self.z)

        @pl.when(self.z > 0)
        def _():
            self.incoming(self.z).wait_recv()
            total[...] += self.landed[self.z].astype(F32)

        @pl.when(self.z < self.n - 1)
        def _():
            self.incoming(self.n).wait_recv()
            total[...] += self.landed[self.n].astype(F32)

    def drain(self):
        for d in range(self.n):

            @pl.when(self.z != d)
            def _():
                self.outgoing(d).wait_send()


def visible_mask(d, rows, length, prefix):
    row_ids = d * rows + lax.broadcasted_iota(jnp.int32, (rows, length), 0)
    col_ids = lax.broadcasted_iota(jnp.int32, (rows, length), 1)
    return (col_ids <= row_ids) | (col_ids < prefix)


def halves(pair, low):
    pair = pair.astype(F32)
    zero = jnp.zeros_like(pair)
    return jnp.where(low, pair, zero), jnp.where(low, pltpu.roll(pair, HD, 1), zero)


def attention_forward_kernel(n, n_exp, *refs):
    tokens_in, w_query_in, w_pair, w_out_in, cot, gain1, gain2, w_router, routes, prefix = refs[:10]
    hidden_out, ext_out, cot_plane, held_out, queries_out, pairs_out, mixed_out, totals_out = refs[
        10:18
    ]
    tokens, w_query, w_out, hidden, ext, held, queries, pairs, mixed, totals = refs[18:28]
    sent, landed, ag_rs, ag_rr, ag_ls, ag_lr, rs_s, rs_r = refs[28:36]
    push_s, push_r, pass_s, pass_r, local_sem, in_sem, out_sem = refs[36:]
    e, z = lax.axis_index("exp"), lax.axis_index("tp")
    rows = tokens.shape[0]
    length = rows * n
    kv_local = pairs.shape[1] // LANES
    low = lax.broadcasted_iota(jnp.int32, (rows, LANES), 1) < HD
    ins = [
        pltpu.make_async_copy(a, b, in_sem.at[i])
        for i, (a, b) in enumerate(
            ((tokens_in, tokens), (w_query_in, w_query), (w_out_in, w_out))
        )
    ]
    outs = [
        pltpu.make_async_copy(a, b, out_sem.at[i])
        for i, (a, b) in enumerate(
            (
                (held, held_out),
                (queries, queries_out),
                (pairs, pairs_out),
                (mixed, mixed_out),
                (totals, totals_out),
                (hidden, hidden_out),
                (ext, ext_out),
            )
        )
    ]
    for copy in ins:
        copy.start()
    barrier, peers = greet(e, z, n, n_exp, True, True)
    ins[0].wait()
    scaled, _ = row_scaling(tokens[...].astype(F32))
    held[pl.ds(pl.multiple_of(z * rows, rows), rows)] = (scaled * gain1[...]).astype(BF)

    def project(d):
        at = pl.ds(pl.multiple_of(d * rows, rows), rows)
        normed = held[at]
        queries[at] = mm(normed, w_query[...]).astype(BF)
        pairs[at] = mm(normed, w_pair[...]).astype(BF)

    pl.semaphore_wait(barrier, peers)
    line = LineGather(e, z, n, rows, held, (ag_rs, ag_rr), (ag_ls, ag_lr))
    line.begin()
    plane = PlaneGather(
        e,
        z,
        n_exp,
        cot,
        lambda b: cot_plane.at[b],
        [lambda k, s=s: s.at[k] for s in (push_s, push_r, pass_s, pass_r)],
    )
    plane.begin()
    ins[1].wait()
    ins[2].wait()
    line.work(0, project)

    def gather_step(step):
        line.step(step)
        line.work(step, project)

    each(n, gather_step, 1)
    for copy in outs[:3]:
        copy.start()

    def part(d):
        at = pl.ds(pl.multiple_of(d * rows, rows), rows)
        seen = visible_mask(d, rows, length, prefix[0])
        lane = lax.broadcasted_iota(jnp.int32, (rows, LANES), 1)
        stats = jnp.zeros((rows, LANES), F32)
        for kv in range(kv_local):
            span = slice(kv * LANES, (kv + 1) * LANES)
            pair = pairs[:, span]
            outs = []
            for h, head in enumerate(halves(queries[at, span], low)):
                scores = mm_nt((head * HD**-0.5).astype(BF), pair)
                scores = jnp.where(seen, scores, MASKED)
                top = jnp.max(scores, axis=-1, keepdims=True)
                grown = jnp.exp(scores - top)
                total = jnp.sum(grown, axis=-1, keepdims=True)
                probs = (grown / total).astype(BF)
                outs.append(mm(probs, pair))
                stats = jnp.where(lane == 2 * kv + h, top + jnp.log(total), stats)
            both = jnp.where(low, pltpu.roll(outs[0], HD, 1), outs[1])
            mixed[at, span] = both.astype(BF)
        totals[at] = stats
        return mm(mixed[at], w_out[...])

    scatter = LineScatter(e, z, n, sent, landed, (rs_s, rs_r), part)
    each(n - 1, scatter.step)
    plane.turn()
    plane.turn_across()
    scatter.finish(hidden)
    for copy in outs[3:5]:
        copy.start()
    hid = tokens[...].astype(F32) + hidden[...]
    hidden[...] = hid
    scaled2, _ = row_scaling(hid)
    normed2 = (scaled2 * gain2[...]).astype(BF)
    ext[:, :D] = normed2
    experts = w_router.shape[0]
    logits = mm_nt(normed2, w_router[...])
    lane = lax.broadcasted_iota(jnp.int32, (rows, experts), 1)
    chosen = lane == routes[:, 0:1]
    for k in range(1, routes.shape[1]):
        chosen = chosen | (lane == routes[:, k : k + 1])
    logits = jnp.where(chosen, logits, MASKED)
    grown = jnp.exp(logits - jnp.max(logits, axis=-1, keepdims=True))
    grown = jnp.where(chosen, grown, 0.0)
    gates = grown / jnp.sum(grown, axis=-1, keepdims=True)
    high = gates.astype(BF)
    low_part = (gates - high.astype(F32)).astype(BF)
    mask = jnp.where(chosen, 1.0, 0.0).astype(BF)
    pad = jnp.zeros((rows, LANES - 3 * experts), BF)
    ext[:, D:] = jnp.concatenate([high, low_part, mask, pad], axis=1)
    for copy in outs[5:]:
        copy.start()
    each(n_exp // 2, plane.arrive)
    plane.drain()
    line.drain()
    scatter.drain()
    for copy in outs:
        copy.wait()


def attention_forward(n, n_exp, in_hbm, in_vmem, prefix):
    tokens, w_query, w_pair, w_out, cot = in_hbm
    rows = tokens.shape[0]
    length = rows * n
    qw, pw = w_query.shape[1], w_pair.shape[1]
    v = pl.BlockSpec(memory_space=VMEM)
    hbm = pl.BlockSpec(memory_space=pl.ANY)
    sem = pltpu.SemaphoreType.DMA
    made = (
        ((rows, D), F32),
        ((rows, XW), BF),
        ((length, D), BF),
        ((length, qw), BF),
        ((length, pw), BF),
        ((length, qw), BF),
        ((length, LANES), F32),
    )
    shapes = [jax.ShapeDtypeStruct(*m) for m in made]
    shapes.insert(2, jax.ShapeDtypeStruct((n_exp, rows, D), BF))
    return pl.pallas_call(
        functools.partial(attention_forward_kernel, n, n_exp),
        out_shape=tuple(shapes),
        in_specs=[hbm, hbm, v, hbm, hbm]
        + [v] * len(in_vmem)
        + [pl.BlockSpec(memory_space=pltpu.SMEM)],
        out_specs=[hbm] * 8,
        scratch_shapes=[
            pltpu.VMEM(tokens.shape, BF),
            pltpu.VMEM(w_query.shape, BF),
            pltpu.VMEM(w_out.shape, BF),
        ]
        + [pltpu.VMEM(*m) for m in made]
        + [
            pltpu.VMEM((n, rows, D), BF),
            pltpu.VMEM((n + 1, rows, D), BF),
            sem((n,)),
            sem((n,)),
            sem((n,)),
            sem((n,)),
            sem((n,)),
            sem((n + 1,)),
        ]
        + [sem((n_exp // 2,))] * 4
        + [sem, sem((3,)), sem((7,))],
        compiler_params=pltpu.CompilerParams(
            collective_id=1, has_side_effects=True, vmem_limit_bytes=60 * MIB
        ),
        cost_estimate=pl.CostEstimate(
            flops=2 * length * D * 4 * qw, bytes_accessed=300 * MIB, transcendentals=0
        ),
    )(*in_hbm, *in_vmem, prefix)


def slot_rows(rows, top_k, experts):
    capacity = rows * top_k * 5 // (experts * 4)
    return -(-capacity // 16) * 16


def selection(extra, first, local_experts, slots):
    rows = extra.shape[0]
    pick = lax.broadcasted_iota(jnp.int32, (8, LANES), 1) == (
        64 + first + lax.broadcasted_iota(jnp.int32, (8, LANES), 0)
    )
    named = mm_nt(jnp.where(pick, 1.0, 0.0).astype(BF), extra)
    earlier = lax.broadcasted_iota(jnp.int32, (rows, rows), 0) < lax.broadcasted_iota(
        jnp.int32, (rows, rows), 1
    )
    place = mm(named.astype(BF), jnp.where(earlier, 1.0, 0.0).astype(BF))
    place = jnp.where(named > 0.5, place, -1.0).astype(jnp.int32)
    slot = lax.broadcasted_iota(jnp.int32, (slots, rows), 0)
    parts = [
        jnp.where(slot == place[k : k + 1, :], 1.0, 0.0) for k in range(local_experts)
    ]
    return jnp.concatenate(parts, axis=0).astype(BF)


def own_gate(extra, expert):
    lane = lax.broadcasted_iota(jnp.int32, extra.shape, 1)
    mine = (lane == expert) | (lane == 32 + expert)
    return jnp.sum(jnp.where(mine, extra.astype(F32), 0.0), axis=-1, keepdims=True)


def folded(row):
    return jnp.concatenate(
        [row[:, k * LANES : (k + 1) * LANES] for k in range(D // LANES)], axis=0
    )


def sigmoid(v):
    return 1.0 / (1.0 + jnp.exp(-v))


def own_experts_kernel(
    n,
    n_exp,
    local_experts,
    ext,
    cot,
    cot_plane,
    w_gate_up,
    w_down,
    hidden,
    w_router,
    gain2,
    layer_out,
    dhidden,
    dhidden_low,
    router_part,
    norm2_part,
    all_rows,
    xg,
    cg,
    wgu,
    wd,
    sel,
    xs,
    cs,
    core_in,
    chip_out,
    chip_in,
    mix_core_in,
    mix_out,
    mix_in,
    total,
    joined,
    cot_sem,
    w_sem,
    out_sem,
    column_s,
    column_r,
    ag_s,
    ag_r,
    fw_s,
    fw_r,
    core_s,
    core_r,
    chip_s,
    chip_r,
    mcore_s,
    mcore_r,
    mchip_s,
    mchip_r,
):
    e, z = lax.axis_index("exp"), lax.axis_index("tp")
    rows = ext.shape[0]
    chips = n_exp // 2
    chip, core = e // 2, lax.rem(e, 2)
    partner = 2 * chip + 1 - core
    slots = sel.shape[1] // local_experts
    first = e * local_experts
    experts = w_router.shape[0]

    loads = [
        pltpu.make_async_copy(w_gate_up, wgu, w_sem.at[0]),
        pltpu.make_async_copy(w_down, wd, w_sem.at[1]),
    ]
    for load in loads:
        load.start()

    def cot_load(k):
        return pltpu.make_async_copy(cot_plane.at[e ^ k], cg.at[e ^ k], cot_sem.at[k])

    each(n_exp, lambda k: cot_load(k).start(), 1)
    cg[e] = cot[...]

    barrier, peers = greet(e, z, n, n_exp, False, True)
    for k in range(1, n):
        pl.semaphore_signal(barrier, inc=1, device_id=(e, z ^ k), device_id_type=MESH)
    xg[e] = ext[...]
    joined[:, :XW] = ext[...]
    joined[:, XW:] = cot[...]
    pl.semaphore_wait(barrier, peers + n - 1)
    plane = PlaneGather(
        e,
        z,
        n_exp,
        xg.at[e],
        lambda b: xg.at[b],
        [lambda k, s=s: s.at[k] for s in (ag_s, ag_r, fw_s, fw_r)],
    )
    there, other = plane.mine, plane.other

    def place(p):
        if chips != 4:
            return p
        return jnp.where(p == 0, 0, jnp.where(p == 1, 3, p - 1))

    pair = GROUP // 2
    each(pair, lambda p: plane.push(place(p)).start(), 1)
    plane.hand(0, True).start()

    def up_column(k, landed=False):
        return pltpu.make_async_remote_copy(
            src_ref=joined,
            dst_ref=all_rows.at[(z ^ k) if landed else z, e],
            send_sem=column_s.at[k],
            recv_sem=column_r.at[k],
            device_id=(e, z ^ k),
            device_id_type=MESH,
        )

    relayed = n == 4
    inner = (z == 1) | (z == 2)
    far = n - 1

    def column_on():
        at = all_rows.at[z ^ 2, e]
        return pltpu.make_async_remote_copy(
            src_ref=at,
            dst_ref=at,
            send_sem=column_s.at[0],
            recv_sem=column_r.at[far],
            device_id=(e, z ^ 1),
            device_id_type=MESH,
        )

    for k in range(1, n):
        if k == far and relayed:

            @pl.when(inner)
            def _():
                up_column(far).start()
        else:
            up_column(k).start()
    each(n_exp, lambda k: cot_load(k).wait(), 1)

    def gather(b):
        s = selection(xg[b, :, D:], first, local_experts, slots)
        sel[b] = s
        xs[b] = mm(s, xg[b]).astype(BF)
        cs[b] = mm(s, cg[b]).astype(BF)

    def save(b):
        return (
            pltpu.make_async_copy(xg.at[b], all_rows.at[z, b, :, pl.ds(0, XW)], out_sem.at[0, b]),
            pltpu.make_async_copy(cg.at[b], all_rows.at[z, b, :, pl.ds(XW, D)], out_sem.at[1, b]),
        )

    def save(b):
        return (
            pltpu.make_async_copy(
                xg.at[b], all_rows.at[z, b, :, pl.ds(0, XW)], out_sem.at[0, b]
            ),
            pltpu.make_async_copy(
                cg.at[b], all_rows.at[z, b, :, pl.ds(XW, D)], out_sem.at[1, b]
            ),
        )

    def members(g):
        return [f(place(pair * g + i)) for i in range(pair) for f in (there, other)]

    def expert_step(g, k):
        blocks = members(g)
        at = pl.ds(pl.multiple_of(k * slots, slots), slots)
        wide = jnp.concatenate([xs[b, at] for b in blocks], axis=0)
        gate_value = own_gate(wide[:, D:], first + k)
        units = mm(wide[:, :D], wgu[k])
        gate, up = units[:, :FF], units[:, FF:]
        sig = sigmoid(gate)
        silu = gate * sig
        active = (silu * up).astype(BF)
        made = mm(active, wd[k]).astype(BF).astype(F32)
        upstream = jnp.concatenate([cs[b, at] for b in blocks], axis=0).astype(F32)
        dgate_value = jnp.sum(upstream * made, axis=-1, keepdims=True)
        share = (gate_value * made).astype(BF)
        dmade = (gate_value * upstream).astype(BF)
        dactive = mm_nt(dmade, wd[k])
        dgate = dactive * up * sig * (1.0 + gate * (1.0 - sig))
        dunits = jnp.concatenate([dgate, dactive * silu], axis=1).astype(BF)
        dx = mm_nt(dunits, wgu[k]).astype(BF)
        lane = lax.broadcasted_iota(jnp.int32, (GROUP * slots, LANES), 1)
        high = dgate_value.astype(BF).astype(F32)
        packed = jnp.where(lane == first + k, high, 0.0)
        packed = jnp.where(lane == 32 + first + k, dgate_value - high, packed).astype(BF)
        for i, b in enumerate(blocks):
            here = slice(i * slots, (i + 1) * slots)
            xs[b, at, :D] = share[here]
            xs[b, at, D:] = packed[here]
            cs[b, at] = dx[here]

    def core_copy(k, src, dst, s, r):
        return pltpu.make_async_remote_copy(
            src_ref=src.at[other(k)],
            dst_ref=dst.at[k],
            send_sem=s.at[k],
            recv_sem=r.at[k],
            device_id=(partner, z),
            device_id_type=MESH,
        )

    def chip_copy(k, src, dst, s, r):
        return pltpu.make_async_remote_copy(
            src_ref=src.at[k],
            dst_ref=dst.at[k],
            send_sem=s.at[k],
            recv_sem=r.at[k],
            device_id=(there(k), z),
            device_id_type=MESH,
        )

    def grads_of(b):
        s = sel[b]
        return jnp.concatenate([mm_tn(s, cs[b]), mm_tn(s, xs[b, :, D:])], axis=1)

    def mix_of(b):
        return mm_tn(sel[b], xs[b, :, :D])

    def pass_on(g, of, kept, came, out, into, sems):
        core_sems, chip_sems = sems

        def give(i):
            k = place(pair * g + i)
            kept[other(k)] = of(other(k)).astype(BF)
            core_copy(k, kept, came, *core_sems).start()

        def send(i):
            k = place(pair * g + i)

            @pl.when(k > 0)
            def _():
                mine = of(there(k))
                core_copy(k, kept, came, *core_sems).wait_recv()
                out[k] = (mine + came[k].astype(F32)).astype(BF)
                chip_copy(k, out, into, *chip_sems).start()

        each(pair, give)
        each(pair, send)

    def group_step(g):
        @pl.when(g == 0)
        def _():
            gather(e)

        def turn(i):
            k = place(pair * g + i)

            @pl.when(k > 0)
            def _():
                plane.push(k, True).wait_recv()
                plane.hand(k).start()

        each(pair, turn)

        @pl.when(g == 0)
        def _():
            each(chips, lambda p: plane.push(place(p)).start(), pair)

        def pick(i):
            k = place(pair * g + i)

            @pl.when(k > 0)
            def _():
                gather(there(k))

        def pick_other(i):
            k = place(pair * g + i)
            plane.arrive(k)
            gather(other(k))

        each(pair, pick)
        each(pair, pick_other)

        def start_save(i):
            for b in (there(place(pair * g + i)), other(place(pair * g + i))):
                for copy in save(b):
                    copy.start()

        def end_save(i):
            for b in (there(place(pair * g + i)), other(place(pair * g + i))):
                for copy in save(b):
                    copy.wait()

        each(pair, start_save)

        @pl.when(g == 0)
        def _():
            for load in loads[:2]:
                load.wait()

        def column_step(k):
            if relayed:

                @pl.when((g == 1) & (k == local_experts // 2))
                def _():
                    up_column(2, True).wait_recv()

                    @pl.when(inner)
                    def _():
                        column_on().start()

            expert_step(g, k)

        each(local_experts, column_step)
        each(pair, end_save)
        grad_sems = ((core_s, core_r), (chip_s, chip_r))
        mix_sems = ((mcore_s, mcore_r), (mchip_s, mchip_r))
        pass_on(g, grads_of, xg, core_in, chip_out, chip_in, grad_sems)
        pass_on(g, mix_of, cg, mix_core_in, mix_out, mix_in, mix_sems)

    each(n_exp // GROUP, group_step)
    plane.hand(0, True).wait_send()
    each(chips, lambda k: plane.push(k).wait_send(), 1)
    each(chips, lambda k: plane.hand(k).wait_send(), 1)
    total[...] = grads_of(e)
    core_copy(0, xg, core_in, core_s, core_r).wait_recv()
    total[...] += core_in[0].astype(F32)

    def take_grads(i):
        k = chips - 1 - i
        chip_copy(k, chip_out, chip_in, chip_s, chip_r).wait_recv()
        total[...] += chip_in[k].astype(F32)

    each(chips - 1, take_grads)
    extra = ext[:, D:].astype(F32)
    gates = extra[:, :experts] + extra[:, experts : 2 * experts]
    dgates = total[:, D : D + experts] + total[:, D + experts : D + 2 * experts]
    dlogits = gates * (dgates - jnp.sum(gates * dgates, axis=-1, keepdims=True))
    dlogits = dlogits.astype(BF)
    normed2 = ext[:, :D]
    routed = mm_tn(dlogits, normed2)
    for k in range(D // LANES):
        router_part[k * experts : (k + 1) * experts] = routed[:, k * LANES : (k + 1) * LANES]
    dnormed2 = total[:, :D] + mm(dlogits, w_router[...])
    scaled2, inverse2 = row_scaling(hidden[...])
    norm2_part[...] = folded(jnp.sum(dnormed2 * scaled2, axis=0, keepdims=True))
    back = cot[...].astype(F32) + norm_backward(dnormed2, scaled2, inverse2, gain2[...])
    dhidden[...] = back
    dhidden_low[...] = back.astype(BF)

    total[:, :D] = hidden[...] + mix_of(e)
    core_copy(0, cg, mix_core_in, mcore_s, mcore_r).wait_recv()
    total[:, :D] += mix_core_in[0].astype(F32)

    def take_mix(i):
        k = chips - 1 - i
        chip_copy(k, mix_out, mix_in, mchip_s, mchip_r).wait_recv()
        total[:, :D] += mix_in[k].astype(F32)

    each(chips - 1, take_mix)
    layer_out[...] = total[:, :D].astype(BF)

    def sent_to_core(k):
        core_copy(k, xg, core_in, core_s, core_r).wait_send()
        core_copy(k, cg, mix_core_in, mcore_s, mcore_r).wait_send()

    def sent_to_chip(i):
        chip_copy(i + 1, chip_out, chip_in, chip_s, chip_r).wait_send()
        chip_copy(i + 1, mix_out, mix_in, mchip_s, mchip_r).wait_send()

    each(chips, sent_to_core)
    each(chips - 1, sent_to_chip)
    for k in range(1, n):
        if not (relayed and k == 2):
            up_column(k, True).wait_recv()
        if relayed and k == far:

            @pl.when(inner)
            def _():
                up_column(far).wait_send()
                column_on().wait_send()
        else:
            up_column(k).wait_send()


def own_experts(n, n_exp, ext, cot, cot_plane, w_gate_up, w_down, hidden, w_router, gain2, slots):
    rows = ext.shape[0]
    local_experts = w_gate_up.shape[0]
    experts = w_router.shape[0]
    chips = n_exp // 2
    v = pl.BlockSpec(memory_space=VMEM)
    hbm = pl.BlockSpec(memory_space=pl.ANY)
    sem = pltpu.SemaphoreType.DMA
    taken = n_exp * local_experts * slots
    return pl.pallas_call(
        functools.partial(own_experts_kernel, n, n_exp, local_experts),
        out_shape=(
            jax.ShapeDtypeStruct((rows, D), BF),
            jax.ShapeDtypeStruct((rows, D), F32),
            jax.ShapeDtypeStruct((rows, D), BF),
            jax.ShapeDtypeStruct((experts * (D // LANES), LANES), F32),
            jax.ShapeDtypeStruct((D // LANES, LANES), F32),
            jax.ShapeDtypeStruct((n, n_exp, rows, RW), BF),
        ),
        in_specs=[v, v, hbm, hbm, hbm, v, v, v],
        out_specs=[v] * 5 + [hbm],
        scratch_shapes=[
            pltpu.VMEM((n_exp, rows, XW), BF),
            pltpu.VMEM((n_exp, rows, D), BF),
            pltpu.VMEM(w_gate_up.shape, BF),
            pltpu.VMEM(w_down.shape, BF),
            pltpu.VMEM((n_exp, local_experts * slots, rows), BF),
            pltpu.VMEM((n_exp, local_experts * slots, XW), BF),
            pltpu.VMEM((n_exp, local_experts * slots, D), BF),
            pltpu.VMEM((chips, rows, XW), BF),
            pltpu.VMEM((chips, rows, XW), BF),
            pltpu.VMEM((chips, rows, XW), BF),
            pltpu.VMEM((chips, rows, D), BF),
            pltpu.VMEM((chips, rows, D), BF),
            pltpu.VMEM((chips, rows, D), BF),
            pltpu.VMEM((rows, XW), F32),
            pltpu.VMEM((rows, RW), BF),
            sem((n_exp,)),
            sem((2,)),
            sem((2, n_exp)),
            sem((n,)),
            sem((n,)),
        ]
        + [sem((chips,))] * 12,
        compiler_params=pltpu.CompilerParams(
            collective_id=2, has_side_effects=True, vmem_limit_bytes=63 * MIB
        ),
        cost_estimate=pl.CostEstimate(
            flops=2 * taken * 6 * D * FF, bytes_accessed=300 * MIB, transcendentals=0
        ),
    )(ext, cot, cot_plane, w_gate_up, w_down, hidden, w_router, gain2)


def expert_middle(x, gate_value, upstream, w_gate_up, w_down):
    units = mm(x, w_gate_up)
    gate, up = units[:, :FF], units[:, FF:]
    sig = sigmoid(gate)
    silu = gate * sig
    dmade = (gate_value * upstream.astype(F32)).astype(BF)
    dactive = mm_nt(dmade, w_down)
    dgate = dactive * up * sig * (1.0 + gate * (1.0 - sig))
    return dmade, (silu * up).astype(BF), dgate.astype(BF), (dactive * silu).astype(BF)


def expert_grads_kernel(
    blocks,
    groups,
    early,
    local_experts,
    rows_all,
    *refs,
):
    first = lax.axis_index("exp") * local_experts + early
    k, g = pl.program_id(0), pl.program_id(1)
    refs = list(refs)
    w_gate_up, w_down = refs.pop(0), refs.pop(0)
    done = (refs.pop(0), refs.pop(0)) if early else None
    summed, routed, got, layer, gate_up_grad, down_grad = refs[:6]
    query_grad, pair_grad, out_grad, router_grad, input_grad, layer_out = refs[6:12]
    refs = refs[12:]
    rbuf, kept_x, kept_dy, kept_active, kept_dunits = refs[:5]
    acc_up, acc_down, sems, out_sems, copy_sems = refs[5:]
    slots = kept_x.shape[0] // blocks
    chunks = blocks // GROUP
    size = GROUP * slots
    last = local_experts - early - 1

    def brought():
        return (
            pltpu.make_async_copy(done[0], acc_up.at[pl.ds(0, early)], copy_sems.at[0]),
            pltpu.make_async_copy(done[1], acc_down.at[pl.ds(0, early)], copy_sems.at[1]),
        )

    def taken():
        return (
            pltpu.make_async_copy(
                acc_up.at[pl.ds(0, early)], gate_up_grad.at[pl.ds(0, early)], copy_sems.at[0]
            ),
            pltpu.make_async_copy(
                acc_down.at[pl.ds(0, early)], down_grad.at[pl.ds(0, early)], copy_sems.at[1]
            ),
        )

    opening = (k == 0) & (g == 0)
    if early:

        @pl.when(opening)
        def _():
            for copy in brought():
                copy.start()

    def load(c, slot):
        at = pl.ds(g * blocks + c * GROUP, GROUP)
        return pltpu.make_async_copy(rows_all.at[at], rbuf.at[slot], sems.at[slot])

    load(0, 0).start()

    def chunk(c, carry):
        slot = lax.rem(c, 2)

        @pl.when(c + 1 < chunks)
        def _():
            load(c + 1, 1 - slot).start()

        load(c, slot).wait()
        if early:

            @pl.when(opening & (c == 2))
            def _():
                for copy in brought():
                    copy.wait()
                for copy in taken():
                    copy.start()

        wide = []
        for i in range(GROUP):
            s = selection(rbuf[slot, i, :, D:XW], first + k, 1, slots)
            wide.append(mm(s, rbuf[slot, i]))
        wide = jnp.concatenate(wide, axis=0)
        x = wide[:, :D].astype(BF)
        made = expert_middle(
            x, own_gate(wide[:, D:XW], first + k), wide[:, XW:], w_gate_up[0], w_down[0]
        )
        at = pl.ds(pl.multiple_of(c * size, size), size)
        kept_x[at] = x
        kept_dy[at] = made[0]
        kept_active[at] = made[1]
        kept_dunits[at, :FF] = made[2]
        kept_dunits[at, FF:] = made[3]
        return carry

    lax.fori_loop(0, chunks, chunk, 0)
    bank = lax.rem(k, 2)
    if early:

        @pl.when(opening)
        def _():
            for copy in taken():
                copy.wait()

    def store(kk):
        b = lax.rem(kk, 2)
        return (
            pltpu.make_async_copy(acc_up.at[b], gate_up_grad.at[early + kk], out_sems.at[0, b]),
            pltpu.make_async_copy(acc_down.at[b], down_grad.at[early + kk], out_sems.at[1, b]),
        )

    @pl.when((g == 0) & (k >= 2))
    def _():
        for copy in store(k - 2):
            copy.wait()

    def add(out, at, value):
        if groups == 1:
            out[bank, at] = value
        else:

            @pl.when(g == 0)
            def _():
                out[bank, at] = value

            @pl.when(g > 0)
            def _():
                out[bank, at] += value

    tile = 256

    def up_tile(m, carry):
        at = pl.ds(pl.multiple_of(m * tile, tile), tile)
        add(acc_up, at, mm_tn(kept_x[:, at], kept_dunits[...]))
        return carry

    lax.fori_loop(0, D // tile, up_tile, 0)

    def down_tile(m, carry):
        at = pl.ds(pl.multiple_of(m * tile, tile), tile)
        add(acc_down, at, mm_tn(kept_active[:, at], kept_dy[...]))
        return carry

    lax.fori_loop(0, FF // tile, down_tile, 0)

    @pl.when(opening)
    def _():
        qw, pw = query_grad.shape[1], LANES
        query_grad[...] = summed[:, :qw].astype(F32)
        for j in range(pair_grad.shape[1]):
            pair_grad[:, j] = summed[:, qw + j * pw : qw + (j + 1) * pw].astype(F32)
        out_grad[...] = summed[:, qw + pair_grad.shape[1] * pw :].astype(F32).T
        experts = router_grad.shape[0]
        for j in range(D // LANES):
            router_grad[:, j * LANES : (j + 1) * LANES] = routed[j * experts : (j + 1) * experts]
        input_grad[...] = got[...]
        layer_out[...] = layer[...]

    @pl.when(g == groups - 1)
    def _():
        for copy in store(k):
            copy.start()

    @pl.when((g == groups - 1) & (k == last))
    def _():
        for copy in store(k):
            copy.wait()
        if last > 0:
            for copy in store(k - 1):
                copy.wait()


def expert_grads(rows_all, w_gate_up, w_down, done, rest, slots, experts):
    total, rows = rows_all.shape[:2]
    local_experts = w_gate_up.shape[0]
    early = done[0].shape[0] if done else 0
    assert early <= 2
    blocks = min(total, 32)
    groups = total // blocks
    kept = blocks * slots
    hbm = pl.BlockSpec(memory_space=pl.ANY)
    v = pl.BlockSpec(memory_space=VMEM)
    sem = pltpu.SemaphoreType.DMA
    width = rest[0].shape[1] // 3
    return pl.pallas_call(
        functools.partial(expert_grads_kernel, blocks, groups, early, local_experts),
        grid=(local_experts - early, groups),
        out_shape=(
            jax.ShapeDtypeStruct((local_experts, D, 2 * FF), F32),
            jax.ShapeDtypeStruct((local_experts, FF, D), F32),
            jax.ShapeDtypeStruct((D, width), F32),
            jax.ShapeDtypeStruct((D, width // LANES, LANES), F32),
            jax.ShapeDtypeStruct((width, D), F32),
            jax.ShapeDtypeStruct((experts, D), F32),
            jax.ShapeDtypeStruct(rest[2].shape, F32),
            jax.ShapeDtypeStruct(rest[3].shape, BF),
        ),
        in_specs=[
            hbm,
            pl.BlockSpec((1, D, 2 * FF), lambda k, g: (k + early, 0, 0)),
            pl.BlockSpec((1, FF, D), lambda k, g: (k + early, 0, 0)),
        ]
        + [hbm] * len(done)
        + [v] * 4,
        out_specs=[hbm, hbm] + [v] * 6,
        scratch_shapes=[
            pltpu.VMEM((2, GROUP, rows, RW), BF),
            pltpu.VMEM((kept, D), BF),
            pltpu.VMEM((kept, D), BF),
            pltpu.VMEM((kept, FF), BF),
            pltpu.VMEM((kept, 2 * FF), BF),
            pltpu.VMEM((2, D, 2 * FF), F32),
            pltpu.VMEM((2, FF, D), F32),
            sem((2,)),
            sem((2, 2)),
            sem((2,)),
        ],
        compiler_params=pltpu.CompilerParams(vmem_limit_bytes=60 * MIB),
        cost_estimate=pl.CostEstimate(
            flops=2 * total * slots * local_experts * 6 * D * FF,
            bytes_accessed=300 * MIB,
            transcendentals=0,
        ),
    )(rows_all, w_gate_up, w_down, *done, *rest)


def backward_kernel(n, n_exp, early, local_experts, *refs):
    refs = list(refs)

    def take(count):
        got = refs[:count]
        del refs[:count]
        return got

    dhidden_low, dhidden, tokens, gain1, held, queries, pairs, mixed, totals = take(9)
    w_query, w_pair, w_out, router_part, norm2_part, prefix, _ = take(7)
    if early:
        w_gate_up, w_down = take(2)
    input_grad, summed, router, norms, all_rows = take(5)
    if early:
        gate_up_grad, down_grad = take(2)
    dfull, dqueries, dpairs, dpairs_low, sent, landed, line_norms, plane_norms = take(8)
    w_sum, w_core, w_chip_out, w_chip_in, r_in, r_line = take(6)
    ag_rs, ag_rr, ag_ls, ag_lr, rs_s, rs_r, push_s, push_r, pass_s, pass_r = take(10)
    nz_s, nz_r, np_s, np_r, r1_s, r1_r, r2_s, r2_r, r3_s, r3_r = take(10)
    wc_s, wc_r, wx_s, wx_r, wg_ps, wg_pr, wg_hs, wg_hr = take(8)
    if early:
        tokens_in, wgu, wd, acc_up, acc_down, kept_x, kept_c, kept_active, kept_dunits = take(9)
        load_s, w_sem, out_sem = take(3)

    e, z = lax.axis_index("exp"), lax.axis_index("tp")
    rows = tokens.shape[0]
    length = rows * n
    kv_local = pairs.shape[1] // LANES
    low = lax.broadcasted_iota(jnp.int32, (rows, LANES), 1) < HD
    scale = HD**-0.5
    first = e * local_experts

    if early:
        weights = [
            pltpu.make_async_copy(w_gate_up.at[pl.ds(0, early)], wgu, w_sem.at[0]),
            pltpu.make_async_copy(w_down.at[pl.ds(0, early)], wd, w_sem.at[1]),
        ]
        for copy in weights:
            copy.start()

    barrier = pltpu.get_barrier_semaphore()

    def greet_plane(k):
        pl.semaphore_signal(barrier, inc=1, device_id=(e ^ k, z), device_id_type=MESH)

    def greet_line(k):
        pl.semaphore_signal(barrier, inc=1, device_id=(e, z ^ k), device_id_type=MESH)

    each(n_exp, greet_plane, 1)
    each(n, greet_line, 1)
    dfull[pl.ds(pl.multiple_of(z * rows, rows), rows)] = dhidden_low[...]
    dpairs[...] = jnp.zeros_like(dpairs)
    pl.semaphore_wait(barrier, n_exp + n - 2)

    line = LineGather(e, z, n, rows, dfull, (ag_rs, ag_rr), (ag_ls, ag_lr))
    line.begin()

    def plane(i):
        return PlaneGather(
            e,
            z,
            n_exp,
            all_rows.at[z ^ i, e],
            lambda b: all_rows.at[z ^ i, b],
            [lambda k, s=s: s.at[i, k] for s in (push_s, push_r, pass_s, pass_r)],
        )

    plane(1).begin()

    part_rows = r_in.shape[1]
    share = D // n_exp

    def routers(b):
        return router.at[pl.ds(pl.multiple_of(b * part_rows, part_rows), part_rows)]

    def router_give(k, landed=False):
        src = router_part.at[pl.ds(pl.multiple_of((e ^ k) * part_rows, part_rows), part_rows)]
        return pltpu.make_async_remote_copy(
            src_ref=src,
            dst_ref=r_in.at[(e ^ k) if landed else e],
            send_sem=r1_s.at[k],
            recv_sem=r1_r.at[k],
            device_id=(e ^ k, z),
            device_id_type=MESH,
        )

    def router_line(k, landed=False):
        return pltpu.make_async_remote_copy(
            src_ref=r_line.at[z],
            dst_ref=r_line.at[(z ^ k) if landed else z],
            send_sem=r2_s.at[k],
            recv_sem=r2_r.at[k],
            device_id=(e, z ^ k),
            device_id_type=MESH,
        )

    def router_gather(k, landed=False):
        return pltpu.make_async_remote_copy(
            src_ref=routers(e),
            dst_ref=routers((e ^ k) if landed else e),
            send_sem=r3_s.at[k],
            recv_sem=r3_r.at[k],
            device_id=(e ^ k, z),
            device_id_type=MESH,
        )

    r_in[e] = router_part[pl.ds(pl.multiple_of(e * part_rows, part_rows), part_rows)]
    each(n_exp, lambda k: router_give(k).start(), 1)

    def shares(ref, b):
        return ref.at[pl.ds(pl.multiple_of(b * share, share), share)]

    w_gather = PlaneGather(
        e,
        z,
        n_exp,
        shares(summed, e),
        lambda b: shares(summed, b),
        [lambda k, s=s: s.at[k] for s in (wg_ps, wg_pr, wg_hs, wg_hr)],
    )
    mine, other = w_gather.mine, w_gather.other

    def w_give(k):
        return pltpu.make_async_remote_copy(
            src_ref=shares(w_sum, other(k)),
            dst_ref=w_core.at[k],
            send_sem=wc_s.at[k],
            recv_sem=wc_r.at[k],
            device_id=(other(0), z),
            device_id_type=MESH,
        )

    def w_cross(k):
        return pltpu.make_async_remote_copy(
            src_ref=w_chip_out.at[k],
            dst_ref=w_chip_in.at[k],
            send_sem=wx_s.at[k],
            recv_sem=wx_r.at[k],
            device_id=(mine(k), z),
            device_id_type=MESH,
        )

    def own_share(b):
        return w_sum[pl.ds(pl.multiple_of(b * share, share), share)].astype(F32)

    def attend(d):
        at = pl.ds(pl.multiple_of(d * rows, rows), rows)
        seen = visible_mask(d, rows, length, prefix[0])
        dmixed = mm_nt(dfull[at], w_out[...]).astype(BF)
        stats = totals[at]
        for kv in range(kv_local):
            span = slice(kv * LANES, (kv + 1) * LANES)
            pair = pairs[:, span]
            outs = []
            added = jnp.zeros((length, LANES), F32)
            heads = halves(queries[at, span], low)
            grads = halves(dmixed[:, span], low)
            for h in range(2):
                head = (heads[h] * scale).astype(BF)
                grad = pltpu.roll(grads[h], HD, 1).astype(BF)
                stat = 2 * kv + h
                scores = mm_nt(head, pair)
                probs = jnp.where(seen, jnp.exp(scores - stats[:, stat : stat + 1]), 0.0)
                dprobs = mm_nt(grad, pair)
                inner = jnp.sum(probs * dprobs, axis=-1, keepdims=True)
                dscores = (probs * (dprobs - inner)).astype(BF)
                outs.append(mm(dscores, pair) * scale)
                added += mm_tn(dscores, head) + mm_tn(probs.astype(BF), grad)
            both = jnp.where(low, outs[0], pltpu.roll(outs[1], HD, 1))
            dqueries[at, span] = both.astype(BF)
            dpairs[:, span] += added

    def part(d):
        at = pl.ds(pl.multiple_of(d * rows, rows), rows)
        return mm_nt(dqueries[at], w_query[...]) + mm_nt(dpairs_low[at], w_pair[...])

    scatter = LineScatter(e, z, n, sent, landed, (rs_s, rs_r), part)

    def line_norm(k, landed=False):
        return pltpu.make_async_remote_copy(
            src_ref=line_norms.at[z],
            dst_ref=line_norms.at[(z ^ k) if landed else z],
            send_sem=nz_s.at[k],
            recv_sem=nz_r.at[k],
            device_id=(e, z ^ k),
            device_id_type=MESH,
        )

    def plane_norm(k, landed=False):
        return pltpu.make_async_remote_copy(
            src_ref=plane_norms.at[e],
            dst_ref=plane_norms.at[(e ^ k) if landed else e],
            send_sem=np_s.at[k],
            recv_sem=np_r.at[k],
            device_id=(e ^ k, z),
            device_id_type=MESH,
        )

    def event(t):
        @pl.when((t > 0) & (t < n))
        def _():
            line.step(t)

        @pl.when(t < n)
        def _():
            line.work(t, attend)

        @pl.when(t == n)
        def _():
            dpairs_low[...] = dpairs[...].astype(BF)

        @pl.when((t >= n) & (t < 2 * n - 1))
        def _():
            scatter.step(t - n)

        @pl.when(t == n)
        def _():
            qw, pw = dqueries.shape[1], dpairs_low.shape[1]
            w_sum[:, :qw] = mm_tn(held[...], dqueries[...]).astype(BF)
            w_sum[:, qw : qw + pw] = mm_tn(held[...], dpairs_low[...]).astype(BF)
            w_sum[:, qw + pw :] = mm_tn(dfull[...], mixed[...]).astype(BF)
            each(n_exp // 2, lambda k: w_give(k).start())
            each(n_exp, lambda k: router_give(k, True).wait_recv(), 1)
            total = r_in[0]
            for k in range(1, n_exp):
                total = total + r_in[k]
            r_line[z] = total
            each(n, lambda k: router_line(k).start(), 1)

        @pl.when(t == n + 1)
        def _():
            def cross(k):
                w_give(k).wait_recv()
                w_chip_out[k] = (own_share(mine(k)) + w_core[k].astype(F32)).astype(BF)
                w_cross(k).start()

            each(n_exp // 2, cross, 1)

        @pl.when(t == n + 2)
        def _():
            w_give(0).wait_recv()
            at = pl.ds(pl.multiple_of(e * share, share), share)
            total = own_share(e) + w_core[0].astype(F32)
            for k in range(1, n_exp // 2):
                w_cross(k).wait_recv()
                total = total + w_chip_in[k].astype(F32)
            summed[at] = total.astype(BF)
            w_gather.begin()
            each(n, lambda k: router_line(k, True).wait_recv(), 1)
            total = r_line[0]
            for k in range(1, n):
                total = total + r_line[k]
            router[pl.ds(pl.multiple_of(e * part_rows, part_rows), part_rows)] = total
            each(n_exp, lambda k: router_gather(k).start(), 1)

        @pl.when(t == 2 * n - 1)
        def _():
            scatter.finish(input_grad)
            dnormed1 = input_grad[...]
            scaled, inverse = row_scaling(tokens[...].astype(F32))
            half = D // LANES
            line_norms[z, :half] = folded(jnp.sum(dnormed1 * scaled, axis=0, keepdims=True))
            line_norms[z, half:] = norm2_part[...]
            each(n, lambda k: line_norm(k).start(), 1)
            back = dhidden[...] + norm_backward(dnormed1, scaled, inverse, gain1[...])
            input_grad[...] = back
            w_gather.turn()

        @pl.when(t == 2 * n)
        def _():
            each(n, lambda k: line_norm(k, True).wait_recv(), 1)
            total = line_norms[0]
            for k in range(1, n):
                total = total + line_norms[k]
            plane_norms[e] = total
            each(n_exp, lambda k: plane_norm(k).start(), 1)
            w_gather.turn_across()

    events = 2 * n + 1
    steps = n * (1 + early) if early else 0

    if n == 4 and early == 2:
        acts = {
            (0, 1): [("begin", 2)],
            (0, 2): [("turn", 1)],
            (0, 4): [("turn_across", 1), ("begin", 3)],
            (1, 0): [("turn", 2)],
            (1, 2): [("turn_across", 2), ("turn", 3)],
            (1, 4): [("turn_across", 3)],
        }
    else:
        acts = {}
        for i in range(1, n):
            acts[i - 1, 2] = [("turn", i)] + ([("begin", i + 1)] if i + 1 < n else [])
            acts[i - 1, 2 * early] = acts.get((i - 1, 2 * early), []) + [("turn_across", i)]

    def act(i, point):
        for (step, at), moves in acts.items():

            @pl.when((i == step) & (point == at))
            def _():
                for name, which in moves:
                    getattr(plane(which), name)()

    if early:
        slots = kept_x.shape[1] // n_exp
        acc_up[...] = jnp.zeros_like(acc_up)
        acc_down[...] = jnp.zeros_like(acc_down)
        for copy in weights:
            copy.wait()

        def one_plane(i, carry):
            @pl.when(i > 0)
            def _():
                each(n_exp // 2, plane(i).arrive)

            def load(b):
                slot = lax.rem(b, GROUP)
                return pltpu.make_async_copy(
                    all_rows.at[z ^ i, b], tokens_in.at[slot], load_s.at[slot]
                )

            each(GROUP, lambda b: load(b).start())

            def pick(b):
                load(b).wait()
                slot = lax.rem(b, GROUP)
                s = selection(tokens_in[slot, :, D:XW], first, early, slots)
                got = mm(s, tokens_in[slot]).astype(BF)
                at = pl.ds(pl.multiple_of(b * slots, slots), slots)
                for k in range(early):
                    here = got[k * slots : (k + 1) * slots]
                    kept_x[k, at] = here[:, :XW]
                    kept_c[k, at] = here[:, XW:]

                @pl.when(b + GROUP < n_exp)
                def _():
                    load(b + GROUP).start()

            each(n_exp, pick)
            event(i * (1 + early))
            act(i, 0)

            def expert(k):
                gate_value = own_gate(kept_x[k, :, D:], first + k)
                x = kept_x[k, :, :D]
                made = expert_middle(x, gate_value, kept_c[k], wgu[k], wd[k])
                kept_c[k] = made[0]
                kept_active[...] = made[1]
                kept_dunits[:, :FF] = made[2]
                kept_dunits[:, FF:] = made[3]
                acc_up[k] += mm_tn(kept_x[k, :, :D], kept_dunits[...])
                acc_down[k] += mm_tn(kept_active[...], kept_c[k])
                act(i, 2 * k + 1)
                event(i * (1 + early) + 1 + k)
                act(i, 2 * k + 2)

            each(early, expert)

            return carry

        lax.fori_loop(0, n, one_plane, 0)
        stores = [
            pltpu.make_async_copy(acc_up, gate_up_grad, out_sem.at[0]),
            pltpu.make_async_copy(acc_down, down_grad, out_sem.at[1]),
        ]
        for copy in stores:
            copy.start()
    each(max(events, steps), event, steps)
    if early:
        for copy in stores:
            copy.wait()
    else:

        def one_plane(i):
            plane(i).turn()

            @pl.when(i + 1 < n)
            def _():
                plane(i + 1).begin()

            plane(i).turn_across()

        each(n, one_plane, 1)
        each(n, lambda i: each(n_exp // 2, plane(i).arrive), 1)
    each(n_exp, lambda k: plane_norm(k, True).wait_recv(), 1)
    total = plane_norms[0]
    for k in range(1, n_exp):
        total = total + plane_norms[k]
    norms[...] = total
    each(n_exp // 2, w_gather.arrive)
    each(n_exp, lambda k: router_gather(k, True).wait_recv(), 1)
    each(n, lambda i: plane(i).drain(), 1)
    each(n, lambda k: line_norm(k).wait_send(), 1)
    each(n_exp, lambda k: plane_norm(k).wait_send(), 1)
    each(n_exp, lambda k: router_give(k).wait_send(), 1)
    each(n, lambda k: router_line(k).wait_send(), 1)
    each(n_exp, lambda k: router_gather(k).wait_send(), 1)
    each(n_exp // 2, lambda k: w_give(k).wait_send())
    each(n_exp // 2, lambda k: w_cross(k).wait_send(), 1)
    w_gather.drain()
    line.drain()
    scatter.drain()


def backward(n, n_exp, slots, whole, prefix, all_rows, weights):
    tokens, held = whole[2], whole[4]
    rows = tokens.shape[0]
    length = rows * n
    qw, pw = whole[9].shape[1], whole[10].shape[1]
    local_experts = weights[0].shape[0]
    early = local_experts // 2
    v = pl.BlockSpec(memory_space=VMEM)
    hbm = pl.BlockSpec(memory_space=pl.ANY)
    sem = pltpu.SemaphoreType.DMA
    chips = n_exp // 2
    width = 2 * qw + pw
    share = D // n_exp
    folds = D // LANES
    routed = whole[12].shape[0]
    outs = [
        (jax.ShapeDtypeStruct((rows, D), F32), v),
        (jax.ShapeDtypeStruct((D, width), BF), v),
        (jax.ShapeDtypeStruct((routed, LANES), F32), v),
        (jax.ShapeDtypeStruct((2 * folds, LANES), F32), v),
        (jax.ShapeDtypeStruct((n, n_exp, rows, RW), BF), hbm),
    ]
    scratch = [
        pltpu.VMEM((length, D), BF),
        pltpu.VMEM((length, qw), BF),
        pltpu.VMEM((length, pw), F32),
        pltpu.VMEM((length, pw), BF),
        pltpu.VMEM((n, rows, D), BF),
        pltpu.VMEM((n + 1, rows, D), BF),
        pltpu.VMEM((n, 2 * folds, LANES), F32),
        pltpu.VMEM((n_exp, 2 * folds, LANES), F32),
        pltpu.VMEM((D, width), BF),
        pltpu.VMEM((chips, share, width), BF),
        pltpu.VMEM((chips, share, width), BF),
        pltpu.VMEM((chips, share, width), BF),
        pltpu.VMEM((n_exp, routed // n_exp, LANES), F32),
        pltpu.VMEM((n, routed // n_exp, LANES), F32),
        sem((n,)),
        sem((n,)),
        sem((n,)),
        sem((n,)),
        sem((n,)),
        sem((n + 1,)),
    ]
    scratch += [sem((n, chips))] * 4
    scratch += [sem((n,))] * 2 + [sem((n_exp,))] * 4 + [sem((n,))] * 2 + [sem((n_exp,))] * 2
    scratch += [sem((chips,))] * 8
    if early:
        kept = n_exp * slots
        outs += [
            (jax.ShapeDtypeStruct((early, D, 2 * FF), F32), hbm),
            (jax.ShapeDtypeStruct((early, FF, D), F32), hbm),
        ]
        scratch += [
            pltpu.VMEM((GROUP, rows, RW), BF),
            pltpu.VMEM((early, D, 2 * FF), BF),
            pltpu.VMEM((early, FF, D), BF),
            pltpu.VMEM((early, D, 2 * FF), F32),
            pltpu.VMEM((early, FF, D), F32),
            pltpu.VMEM((early, kept, XW), BF),
            pltpu.VMEM((early, kept, D), BF),
            pltpu.VMEM((kept, FF), BF),
            pltpu.VMEM((kept, 2 * FF), BF),
            sem((GROUP,)),
            sem((2,)),
            sem((2,)),
        ]
    return pl.pallas_call(
        functools.partial(backward_kernel, n, n_exp, early, local_experts),
        out_shape=tuple(shape for shape, _ in outs),
        in_specs=[v] * len(whole)
        + [pl.BlockSpec(memory_space=pltpu.SMEM)]
        + [hbm] * (1 + (2 if early else 0)),
        out_specs=tuple(spec for _, spec in outs),
        input_output_aliases={len(whole) + 1: 4},
        scratch_shapes=scratch,
        compiler_params=pltpu.CompilerParams(
            collective_id=3, has_side_effects=True, vmem_limit_bytes=62 * MIB
        ),
        cost_estimate=pl.CostEstimate(
            flops=2 * length * D * 8 * qw, bytes_accessed=300 * MIB, transcendentals=0
        ),
    )(*whole, prefix, all_rows, *(weights if early else ()))


def local(
    n_exp,
    n_tp,
    tokens,
    norm1_gain,
    w_query,
    w_key_value,
    w_out,
    norm2_gain,
    w_router,
    w_gate_up,
    w_down,
    routes,
    prefix,
    cotangent,
):
    rows = tokens.shape[0]
    experts = w_router.shape[1]
    slots = slot_rows(rows, routes.shape[1], experts)
    w_pair = w_key_value.reshape(D, -1)
    gain1, gain2 = norm1_gain.reshape(1, D), norm2_gain.reshape(1, D)
    router_t = w_router.T
    hidden, ext, cot_plane, held, queries, pairs, mixed, totals = attention_forward(
        n_tp,
        n_exp,
        (tokens, w_query, w_pair, w_out, cotangent),
        (gain1, gain2, router_t, routes),
        prefix,
    )
    layer, dhidden, dhidden_low, router_part, norm2_part, all_rows = own_experts(
        n_tp,
        n_exp,
        ext,
        cotangent,
        cot_plane,
        w_gate_up,
        w_down,
        hidden,
        router_t,
        gain2,
        slots,
    )
    whole = (dhidden_low, dhidden, tokens, gain1, held, queries, pairs, mixed, totals)
    whole += (w_query, w_pair, w_out, router_part, norm2_part)
    made = backward(n_tp, n_exp, slots, whole, prefix, all_rows, (w_gate_up, w_down))
    got, summed, routed, norms, all_rows = made[:5]
    gate_up_grad, down_grad, query_grad, pair_grad, out_grad, router_grad, input_grad, layer_out = (
        expert_grads(
            all_rows.reshape(n_exp * n_tp, rows, RW),
            w_gate_up,
            w_down,
            made[5:],
            (summed, routed, got, layer),
            slots,
            experts,
        )
    )
    norms = norms.reshape(2, D)
    return (
        layer_out,
        input_grad,
        norms[0],
        query_grad,
        pair_grad,
        out_grad,
        norms[1],
        router_grad.T,
        gate_up_grad,
        down_grad,
    )


def solution(mesh):
    return jax.shard_map(
        functools.partial(local, mesh.shape["exp"], mesh.shape["tp"]),
        mesh=mesh,
        in_specs=(
            P(("exp", "tp"), None),
            P(),
            P(None, "tp"),
            P(None, "tp", None),
            P("tp", None),
            P(),
            P(),
            P("exp", None, None),
            P("exp", None, None),
            P(("exp", "tp"), None),
            P("exp"),
            P(("exp", "tp"), None),
        ),
        out_specs=(
            P(("exp", "tp"), None),
            P(("exp", "tp"), None),
            P(),
            P(None, "tp"),
            P(None, "tp", None),
            P("tp", None),
            P(),
            P(),
            P("exp", None, None),
            P("exp", None, None),
        ),
        check_vma=False,
    )
```

```python
import functools

import jax
import jax.numpy as jnp
from jax import lax
from jax.experimental import pallas as pl
from jax.experimental.pallas import tpu as pltpu
from jax.sharding import PartitionSpec as P

D = 1024
H = 16
KVH = 8
HD = 64
FF = 512
LANES = 128
XW = D + LANES
RW = XW + D
GROUP = 4

EPS = 1e-06
MASKED = -1e30
MESH = pl.DeviceIdType.MESH
BF = jnp.bfloat16
F32 = jnp.float32
VMEM = pltpu.VMEM
MIB = 1 << 20


def mm(a, b):
    return jnp.dot(a, b, preferred_element_type=F32)


def mm_nt(a, b):
    return lax.dot_general(a, b, (((1,), (1,)), ((), ())), preferred_element_type=F32)


def mm_tn(a, b):
    return lax.dot_general(a, b, (((0,), (0,)), ((), ())), preferred_element_type=F32)


def row_scaling(values):
    inverse = lax.rsqrt(jnp.mean(values * values, axis=-1, keepdims=True) + EPS)
    return values * inverse, inverse


def norm_backward(gradient, scaled, inverse, gain):
    weighted = gradient * gain
    inner = jnp.mean(weighted * scaled, axis=-1, keepdims=True)
    return inverse * (weighted - scaled * inner)


def block(ref, index, rows):
    return ref.at[pl.ds(pl.multiple_of(index * rows, rows), rows)]


def line_order(n):
    orders = []
    for z in range(n):
        right = list(range(n - 1, z, -1))
        left = list(range(z))
        first, second = (right, left) if len(right) >= len(left) else (left, right)
        order = []
        while first or second:
            if len(first) >= len(second):
                order.append(first.pop(0))
            else:
                order.append(second.pop(0))
        orders.append(order + [z])
    return orders


def lookup(table, z, j):
    value = jnp.int32(table[0][0])
    for a, row in enumerate(table):
        for b, entry in enumerate(row):
            value = jnp.where((z == a) & (j == b), jnp.int32(entry), value)
    return value


def greet(e, z, n, n_exp, line, plane):
    barrier = pltpu.get_barrier_semaphore()
    peers = jnp.int32(0)
    if line:

        @pl.when(z > 0)
        def _():
            pl.semaphore_signal(barrier, inc=1, device_id=(e, z - 1), device_id_type=MESH)

        @pl.when(z < n - 1)
        def _():
            pl.semaphore_signal(barrier, inc=1, device_id=(e, z + 1), device_id_type=MESH)

        peers += jnp.where(z > 0, 1, 0) + jnp.where(z < n - 1, 1, 0)
    if plane:
        chip, core = e // 2, lax.rem(e, 2)
        pl.semaphore_signal(barrier, inc=1, device_id=(e + 1 - 2 * core, z), device_id_type=MESH)

        def one(k, carry):
            there = 2 * (chip ^ k) + core
            pl.semaphore_signal(barrier, inc=1, device_id=(there, z), device_id_type=MESH)
            return carry

        lax.fori_loop(1, n_exp // 2, one, 0)
        peers += n_exp // 2
    return barrier, peers


def each(count, body, start=0):
    lax.fori_loop(start, count, lambda i, c: (body(i), c)[1], 0)


class PlaneGather:
    def __init__(self, e, z, n_exp, own, view, sems):
        self.e, self.z, self.own, self.view = e, z, own, view
        self.chip, self.core, self.chips = e // 2, lax.rem(e, 2), n_exp // 2
        self.push_s, self.push_r, self.pass_s, self.pass_r = sems
        self.square = self.chips == 4
        self.pushes = 3 if self.square else self.chips

    def mine(self, k):
        return 2 * (self.chip ^ k) + self.core

    def other(self, k):
        return 2 * (self.chip ^ k) + 1 - self.core

    def copy(self, src, dst, sems, at, device):
        return pltpu.make_async_remote_copy(
            src_ref=src,
            dst_ref=dst,
            send_sem=sems[0](at),
            recv_sem=sems[1](at),
            device_id=(device, self.z),
            device_id_type=MESH,
        )

    def push(self, k, landed=False):
        src = self.view(self.mine(k)) if landed else self.own
        dst = src if landed else self.view(self.e)
        return self.copy(src, dst, (self.push_s, self.push_r), k, self.mine(k))

    def hand(self, k, first=False, landed=False):
        there = self.view(self.other(k) if landed else self.mine(k))
        src = self.own if first else there
        return self.copy(src, there, (self.pass_s, self.pass_r), k, self.other(0))

    def across(self, half, landed=False):
        whole = self.view(self.mine(3 if landed else 1 + half))
        rows = whole.shape[0] // 2
        there = whole.at[pl.ds(half * rows, rows)]
        sems = (self.push_s, self.push_r)
        return self.copy(there, there, sems, 3 * half, self.mine(2 - half))

    def begin(self):
        each(self.pushes, lambda k: self.push(k).start(), 1)
        self.hand(0, True).start()

    def begin_part(self, part, parts):
        rows = self.own.shape[0] // parts
        at = pl.ds(part * rows, rows)
        for k in (1, 2):
            sems = (self.push_s, self.push_r)
            own, there = self.own.at[at], self.view(self.e).at[at]
            self.copy(own, there, sems, k, self.mine(k)).start()
        if part == 0:
            self.hand(0, True).start()

    def turn(self):
        def one(k):
            self.push(k, True).wait_recv()
            self.hand(k).start()

        if self.square:
            for half in range(2):
                self.push(1 + half, True).wait_recv()
                self.across(half).start()
                self.hand(1 + half).start()
        else:
            each(self.chips, one, 1)

    def turn_across(self):
        if self.square:
            for half in range(2):
                self.across(half, True).wait_recv()
            self.hand(3).start()

    def arrive(self, k):
        self.hand(k, landed=True).wait_recv()

    def drain(self):
        self.hand(0, True).wait_send()
        each(self.pushes, lambda k: self.push(k).wait_send(), 1)
        each(self.chips, lambda k: self.hand(k).wait_send(), 1)
        if self.square:
            for half in range(2):
                self.across(half).wait_send()


class LineGather:
    def __init__(self, e, z, n, rows, held, right_sems, left_sems):
        self.e, self.z, self.n, self.rows, self.held = e, z, n, rows, held
        self.sems = {1: right_sems, -1: left_sems}
        self.onward = {1: z < n - 1, -1: z > 0}

    def has(self, step, way):
        return self.z >= step if way > 0 else self.z + step < self.n

    def copy(self, step, way, landed=False):
        send, recv = self.sems[way]
        there = block(self.held, self.z - way * step, self.rows)
        return pltpu.make_async_remote_copy(
            src_ref=there,
            dst_ref=there,
            send_sem=send.at[step],
            recv_sem=recv.at[step - 1 if landed else step],
            device_id=(self.e, self.z + way),
            device_id_type=MESH,
        )

    def begin(self):
        for way in (1, -1):

            @pl.when(self.onward[way])
            def _():
                self.copy(0, way).start()

    def step(self, step):
        for way in (1, -1):

            @pl.when(self.has(step, way))
            def _():
                self.copy(step, way, True).wait_recv()

            @pl.when(self.has(step, way) & self.onward[way])
            def _():
                self.copy(step, way).start()

    def work(self, step, body):
        def one(way, carry):
            d = jnp.where(way > 0, self.z - step, self.z + step)

            @pl.when((d >= 0) & (d < self.n) & ((step > 0) | (way > 0)))
            def _():
                body(d)

            return carry

        lax.fori_loop(0, 2, one, 0)

    def drain(self):
        for step in range(self.n - 1):
            for way in (1, -1):

                @pl.when(self.has(step, way) & self.onward[way])
                def _():
                    self.copy(step, way).wait_send()


class LineScatter:
    def __init__(self, e, z, n, sent, landed, sems, part):
        self.e, self.z, self.n, self.sent, self.landed, self.part = e, z, n, sent, landed, part
        self.send, self.recv = sems
        self.table = line_order(n)

    def outgoing(self, d):
        right = d > self.z
        place = jnp.where(right | (d < self.z - 1), d, self.n)
        return pltpu.make_async_remote_copy(
            src_ref=self.sent.at[d],
            dst_ref=self.landed.at[place],
            send_sem=self.send.at[d],
            recv_sem=self.recv.at[place],
            device_id=(self.e, jnp.where(right, self.z + 1, self.z - 1)),
            device_id_type=MESH,
        )

    def incoming(self, place):
        return pltpu.make_async_remote_copy(
            src_ref=self.landed.at[place],
            dst_ref=self.landed.at[place],
            send_sem=self.send.at[0],
            recv_sem=self.recv.at[place],
            device_id=(self.e, jnp.where(self.z > 0, self.z - 1, self.z + 1)),
            device_id_type=MESH,
        )

    def step(self, j):
        d = lookup(self.table, self.z, j)
        value = self.part(d)
        upstream = jnp.where(d > self.z, self.z > 0, self.z < self.n - 1)

        @pl.when(upstream)
        def _():
            self.incoming(d).wait_recv()
            self.sent[d] = (value + self.landed[d].astype(F32)).astype(BF)

        @pl.when(jnp.logical_not(upstream))
        def _():
            self.sent[d] = value.astype(BF)

        self.outgoing(d).start()

    def finish(self, total):
        total[...] = self.part(self.z)

        @pl.when(self.z > 0)
        def _():
            self.incoming(self.z).wait_recv()
            total[...] += self.landed[self.z].astype(F32)

        @pl.when(self.z < self.n - 1)
        def _():
            self.incoming(self.n).wait_recv()
            total[...] += self.landed[self.n].astype(F32)

    def drain(self):
        for d in range(self.n):

            @pl.when(self.z != d)
            def _():
                self.outgoing(d).wait_send()


def visible_mask(d, rows, length, prefix):
    row_ids = d * rows + lax.broadcasted_iota(jnp.int32, (rows, length), 0)
    col_ids = lax.broadcasted_iota(jnp.int32, (rows, length), 1)
    return (col_ids <= row_ids) | (col_ids < prefix)


def halves(pair, low):
    pair = pair.astype(F32)
    zero = jnp.zeros_like(pair)
    return jnp.where(low, pair, zero), jnp.where(low, pltpu.roll(pair, HD, 1), zero)


def attention_forward_kernel(n, n_exp, *refs):
    tokens_in, w_query_in, w_pair, w_out_in, cot, gain1, gain2, w_router, routes, prefix = refs[:10]
    hidden_out, ext_out, cot_plane, held_out, queries_out, pairs_out, mixed_out, totals_out = refs[
        10:18
    ]
    tokens, w_query, w_out, hidden, ext, held, queries, pairs, mixed, totals = refs[18:28]
    sent, landed, ag_rs, ag_rr, ag_ls, ag_lr, rs_s, rs_r = refs[28:36]
    push_s, push_r, pass_s, pass_r, local_sem, in_sem, out_sem = refs[36:]
    e, z = lax.axis_index("exp"), lax.axis_index("tp")
    rows = tokens.shape[0]
    length = rows * n
    kv_local = pairs.shape[1] // LANES
    low = lax.broadcasted_iota(jnp.int32, (rows, LANES), 1) < HD
    ins = [
        pltpu.make_async_copy(a, b, in_sem.at[i])
        for i, (a, b) in enumerate(
            ((tokens_in, tokens), (w_query_in, w_query), (w_out_in, w_out))
        )
    ]
    outs = [
        pltpu.make_async_copy(a, b, out_sem.at[i])
        for i, (a, b) in enumerate(
            (
                (held, held_out),
                (queries, queries_out),
                (pairs, pairs_out),
                (mixed, mixed_out),
                (totals, totals_out),
                (hidden, hidden_out),
                (ext, ext_out),
            )
        )
    ]
    for copy in ins:
        copy.start()
    barrier, peers = greet(e, z, n, n_exp, True, True)
    ins[0].wait()
    scaled, _ = row_scaling(tokens[...].astype(F32))
    held[pl.ds(pl.multiple_of(z * rows, rows), rows)] = (scaled * gain1[...]).astype(BF)

    def project(d):
        at = pl.ds(pl.multiple_of(d * rows, rows), rows)
        normed = held[at]
        queries[at] = mm(normed, w_query[...]).astype(BF)
        pairs[at] = mm(normed, w_pair[...]).astype(BF)

    pl.semaphore_wait(barrier, peers)
    line = LineGather(e, z, n, rows, held, (ag_rs, ag_rr), (ag_ls, ag_lr))
    line.begin()
    plane = PlaneGather(
        e,
        z,
        n_exp,
        cot,
        lambda b: cot_plane.at[b],
        [lambda k, s=s: s.at[k] for s in (push_s, push_r, pass_s, pass_r)],
    )
    plane.begin()
    ins[1].wait()
    ins[2].wait()
    line.work(0, project)

    def gather_step(step):
        line.step(step)
        line.work(step, project)

    each(n, gather_step, 1)
    for copy in outs[:3]:
        copy.start()

    def part(d):
        at = pl.ds(pl.multiple_of(d * rows, rows), rows)
        seen = visible_mask(d, rows, length, prefix[0])
        lane = lax.broadcasted_iota(jnp.int32, (rows, LANES), 1)
        stats = jnp.zeros((rows, LANES), F32)
        for kv in range(kv_local):
            span = slice(kv * LANES, (kv + 1) * LANES)
            pair = pairs[:, span]
            outs = []
            for h, head in enumerate(halves(queries[at, span], low)):
                scores = mm_nt((head * HD**-0.5).astype(BF), pair)
                scores = jnp.where(seen, scores, MASKED)
                top = jnp.max(scores, axis=-1, keepdims=True)
                grown = jnp.exp(scores - top)
                total = jnp.sum(grown, axis=-1, keepdims=True)
                probs = (grown / total).astype(BF)
                outs.append(mm(probs, pair))
                stats = jnp.where(lane == 2 * kv + h, top + jnp.log(total), stats)
            both = jnp.where(low, pltpu.roll(outs[0], HD, 1), outs[1])
            mixed[at, span] = both.astype(BF)
        totals[at] = stats
        return mm(mixed[at], w_out[...])

    scatter = LineScatter(e, z, n, sent, landed, (rs_s, rs_r), part)
    each(n - 1, scatter.step)
    plane.turn()
    plane.turn_across()
    scatter.finish(hidden)
    for copy in outs[3:5]:
        copy.start()
    hid = tokens[...].astype(F32) + hidden[...]
    hidden[...] = hid
    scaled2, _ = row_scaling(hid)
    normed2 = (scaled2 * gain2[...]).astype(BF)
    ext[:, :D] = normed2
    experts = w_router.shape[0]
    logits = mm_nt(normed2, w_router[...])
    lane = lax.broadcasted_iota(jnp.int32, (rows, experts), 1)
    chosen = lane == routes[:, 0:1]
    for k in range(1, routes.shape[1]):
        chosen = chosen | (lane == routes[:, k : k + 1])
    logits = jnp.where(chosen, logits, MASKED)
    grown = jnp.exp(logits - jnp.max(logits, axis=-1, keepdims=True))
    grown = jnp.where(chosen, grown, 0.0)
    gates = grown / jnp.sum(grown, axis=-1, keepdims=True)
    high = gates.astype(BF)
    low_part = (gates - high.astype(F32)).astype(BF)
    mask = jnp.where(chosen, 1.0, 0.0).astype(BF)
    pad = jnp.zeros((rows, LANES - 3 * experts), BF)
    ext[:, D:] = jnp.concatenate([high, low_part, mask, pad], axis=1)
    for copy in outs[5:]:
        copy.start()
    each(n_exp // 2, plane.arrive)
    plane.drain()
    line.drain()
    scatter.drain()
    for copy in outs:
        copy.wait()


def attention_forward(n, n_exp, in_hbm, in_vmem, prefix):
    tokens, w_query, w_pair, w_out, cot = in_hbm
    rows = tokens.shape[0]
    length = rows * n
    qw, pw = w_query.shape[1], w_pair.shape[1]
    v = pl.BlockSpec(memory_space=VMEM)
    hbm = pl.BlockSpec(memory_space=pl.ANY)
    sem = pltpu.SemaphoreType.DMA
    made = (
        ((rows, D), F32),
        ((rows, XW), BF),
        ((length, D), BF),
        ((length, qw), BF),
        ((length, pw), BF),
        ((length, qw), BF),
        ((length, LANES), F32),
    )
    shapes = [jax.ShapeDtypeStruct(*m) for m in made]
    shapes.insert(2, jax.ShapeDtypeStruct((n_exp, rows, D), BF))
    return pl.pallas_call(
        functools.partial(attention_forward_kernel, n, n_exp),
        out_shape=tuple(shapes),
        in_specs=[hbm, hbm, v, hbm, hbm]
        + [v] * len(in_vmem)
        + [pl.BlockSpec(memory_space=pltpu.SMEM)],
        out_specs=[hbm] * 8,
        scratch_shapes=[
            pltpu.VMEM(tokens.shape, BF),
            pltpu.VMEM(w_query.shape, BF),
            pltpu.VMEM(w_out.shape, BF),
        ]
        + [pltpu.VMEM(*m) for m in made]
        + [
            pltpu.VMEM((n, rows, D), BF),
            pltpu.VMEM((n + 1, rows, D), BF),
            sem((n,)),
            sem((n,)),
            sem((n,)),
            sem((n,)),
            sem((n,)),
            sem((n + 1,)),
        ]
        + [sem((n_exp // 2,))] * 4
        + [sem, sem((3,)), sem((7,))],
        compiler_params=pltpu.CompilerParams(
            collective_id=1, has_side_effects=True, vmem_limit_bytes=60 * MIB
        ),
        cost_estimate=pl.CostEstimate(
            flops=2 * length * D * 4 * qw, bytes_accessed=300 * MIB, transcendentals=0
        ),
    )(*in_hbm, *in_vmem, prefix)


def slot_rows(rows, top_k, experts):
    capacity = rows * top_k * 5 // (experts * 4)
    return -(-capacity // 16) * 16


def selection(extra, first, local_experts, slots):
    rows = extra.shape[0]
    pick = lax.broadcasted_iota(jnp.int32, (8, LANES), 1) == (
        64 + first + lax.broadcasted_iota(jnp.int32, (8, LANES), 0)
    )
    named = mm_nt(jnp.where(pick, 1.0, 0.0).astype(BF), extra)
    earlier = lax.broadcasted_iota(jnp.int32, (rows, rows), 0) < lax.broadcasted_iota(
        jnp.int32, (rows, rows), 1
    )
    place = mm(named.astype(BF), jnp.where(earlier, 1.0, 0.0).astype(BF))
    place = jnp.where(named > 0.5, place, -1.0).astype(jnp.int32)
    slot = lax.broadcasted_iota(jnp.int32, (slots, rows), 0)
    parts = [
        jnp.where(slot == place[k : k + 1, :], 1.0, 0.0) for k in range(local_experts)
    ]
    return jnp.concatenate(parts, axis=0).astype(BF)


def own_gate(extra, expert):
    lane = lax.broadcasted_iota(jnp.int32, extra.shape, 1)
    mine = (lane == expert) | (lane == 32 + expert)
    return jnp.sum(jnp.where(mine, extra.astype(F32), 0.0), axis=-1, keepdims=True)


def folded(row):
    return jnp.concatenate(
        [row[:, k * LANES : (k + 1) * LANES] for k in range(D // LANES)], axis=0
    )


def sigmoid(v):
    return 1.0 / (1.0 + jnp.exp(-v))


def own_experts_kernel(
    n,
    n_exp,
    local_experts,
    ext,
    cot,
    cot_plane,
    w_gate_up,
    w_down,
    hidden,
    w_router,
    gain2,
    layer_out,
    dhidden,
    dhidden_low,
    router_part,
    norm2_part,
    all_rows,
    xg,
    cg,
    wgu,
    wd,
    sel,
    xs,
    cs,
    core_in,
    chip_out,
    chip_in,
    mix_core_in,
    mix_out,
    mix_in,
    total,
    joined,
    cot_sem,
    w_sem,
    out_sem,
    column_s,
    column_r,
    ag_s,
    ag_r,
    fw_s,
    fw_r,
    core_s,
    core_r,
    chip_s,
    chip_r,
    mcore_s,
    mcore_r,
    mchip_s,
    mchip_r,
):
    e, z = lax.axis_index("exp"), lax.axis_index("tp")
    rows = ext.shape[0]
    chips = n_exp // 2
    chip, core = e // 2, lax.rem(e, 2)
    partner = 2 * chip + 1 - core
    slots = sel.shape[1] // local_experts
    first = e * local_experts
    experts = w_router.shape[0]

    loads = [
        pltpu.make_async_copy(w_gate_up, wgu, w_sem.at[0]),
        pltpu.make_async_copy(w_down, wd, w_sem.at[1]),
    ]
    for load in loads:
        load.start()

    def cot_load(k):
        return pltpu.make_async_copy(cot_plane.at[e ^ k], cg.at[e ^ k], cot_sem.at[k])

    each(n_exp, lambda k: cot_load(k).start(), 1)
    cg[e] = cot[...]

    barrier, peers = greet(e, z, n, n_exp, False, True)
    for k in range(1, n):
        pl.semaphore_signal(barrier, inc=1, device_id=(e, z ^ k), device_id_type=MESH)
    xg[e] = ext[...]
    joined[:, :XW] = ext[...]
    joined[:, XW:] = cot[...]
    pl.semaphore_wait(barrier, peers + n - 1)
    plane = PlaneGather(
        e,
        z,
        n_exp,
        xg.at[e],
        lambda b: xg.at[b],
        [lambda k, s=s: s.at[k] for s in (ag_s, ag_r, fw_s, fw_r)],
    )
    there, other = plane.mine, plane.other

    def place(p):
        if chips != 4:
            return p
        return jnp.where(p == 0, 0, jnp.where(p == 1, 3, p - 1))

    pair = GROUP // 2
    each(pair, lambda p: plane.push(place(p)).start(), 1)
    plane.hand(0, True).start()

    def up_column(k, landed=False):
        return pltpu.make_async_remote_copy(
            src_ref=joined,
            dst_ref=all_rows.at[(z ^ k) if landed else z, e],
            send_sem=column_s.at[k],
            recv_sem=column_r.at[k],
            device_id=(e, z ^ k),
            device_id_type=MESH,
        )

    relayed = n == 4
    inner = (z == 1) | (z == 2)
    far = n - 1

    def column_on():
        at = all_rows.at[z ^ 2, e]
        return pltpu.make_async_remote_copy(
            src_ref=at,
            dst_ref=at,
            send_sem=column_s.at[0],
            recv_sem=column_r.at[far],
            device_id=(e, z ^ 1),
            device_id_type=MESH,
        )

    for k in range(1, n):
        if k == far and relayed:

            @pl.when(inner)
            def _():
                up_column(far).start()
        else:
            up_column(k).start()
    each(n_exp, lambda k: cot_load(k).wait(), 1)

    def gather(b):
        s = selection(xg[b, :, D:], first, local_experts, slots)
        sel[b] = s
        xs[b] = mm(s, xg[b]).astype(BF)
        cs[b] = mm(s, cg[b]).astype(BF)

    def save(b):
        return (
            pltpu.make_async_copy(xg.at[b], all_rows.at[z, b, :, pl.ds(0, XW)], out_sem.at[0, b]),
            pltpu.make_async_copy(cg.at[b], all_rows.at[z, b, :, pl.ds(XW, D)], out_sem.at[1, b]),
        )

    def save(b):
        return (
            pltpu.make_async_copy(
                xg.at[b], all_rows.at[z, b, :, pl.ds(0, XW)], out_sem.at[0, b]
            ),
            pltpu.make_async_copy(
                cg.at[b], all_rows.at[z, b, :, pl.ds(XW, D)], out_sem.at[1, b]
            ),
        )

    def members(g):
        return [f(place(pair * g + i)) for i in range(pair) for f in (there, other)]

    def expert_step(g, k):
        blocks = members(g)
        at = pl.ds(pl.multiple_of(k * slots, slots), slots)
        wide = jnp.concatenate([xs[b, at] for b in blocks], axis=0)
        gate_value = own_gate(wide[:, D:], first + k)
        units = mm(wide[:, :D], wgu[k])
        gate, up = units[:, :FF], units[:, FF:]
        sig = sigmoid(gate)
        silu = gate * sig
        active = (silu * up).astype(BF)
        made = mm(active, wd[k]).astype(BF).astype(F32)
        upstream = jnp.concatenate([cs[b, at] for b in blocks], axis=0).astype(F32)
        dgate_value = jnp.sum(upstream * made, axis=-1, keepdims=True)
        share = (gate_value * made).astype(BF)
        dmade = (gate_value * upstream).astype(BF)
        dactive = mm_nt(dmade, wd[k])
        dgate = dactive * up * sig * (1.0 + gate * (1.0 - sig))
        dunits = jnp.concatenate([dgate, dactive * silu], axis=1).astype(BF)
        dx = mm_nt(dunits, wgu[k]).astype(BF)
        lane = lax.broadcasted_iota(jnp.int32, (GROUP * slots, LANES), 1)
        high = dgate_value.astype(BF).astype(F32)
        packed = jnp.where(lane == first + k, high, 0.0)
        packed = jnp.where(lane == 32 + first + k, dgate_value - high, packed).astype(BF)
        for i, b in enumerate(blocks):
            here = slice(i * slots, (i + 1) * slots)
            xs[b, at, :D] = share[here]
            xs[b, at, D:] = packed[here]
            cs[b, at] = dx[here]

    def core_copy(k, src, dst, s, r):
        return pltpu.make_async_remote_copy(
            src_ref=src.at[other(k)],
            dst_ref=dst.at[k],
            send_sem=s.at[k],
            recv_sem=r.at[k],
            device_id=(partner, z),
            device_id_type=MESH,
        )

    def chip_copy(k, src, dst, s, r):
        return pltpu.make_async_remote_copy(
            src_ref=src.at[k],
            dst_ref=dst.at[k],
            send_sem=s.at[k],
            recv_sem=r.at[k],
            device_id=(there(k), z),
            device_id_type=MESH,
        )

    def grads_of(b):
        s = sel[b]
        return jnp.concatenate([mm_tn(s, cs[b]), mm_tn(s, xs[b, :, D:])], axis=1)

    def mix_of(b):
        return mm_tn(sel[b], xs[b, :, :D])

    def pass_on(g, of, kept, came, out, into, sems):
        core_sems, chip_sems = sems

        def give(i):
            k = place(pair * g + i)
            kept[other(k)] = of(other(k)).astype(BF)
            core_copy(k, kept, came, *core_sems).start()

        def send(i):
            k = place(pair * g + i)

            @pl.when(k > 0)
            def _():
                mine = of(there(k))
                core_copy(k, kept, came, *core_sems).wait_recv()
                out[k] = (mine + came[k].astype(F32)).astype(BF)
                chip_copy(k, out, into, *chip_sems).start()

        each(pair, give)
        each(pair, send)

    def group_step(g):
        @pl.when(g == 0)
        def _():
            gather(e)

        def turn(i):
            k = place(pair * g + i)

            @pl.when(k > 0)
            def _():
                plane.push(k, True).wait_recv()
                plane.hand(k).start()

        each(pair, turn)

        @pl.when(g == 0)
        def _():
            each(chips, lambda p: plane.push(place(p)).start(), pair)

        def pick(i):
            k = place(pair * g + i)

            @pl.when(k > 0)
            def _():
                gather(there(k))

        def pick_other(i):
            k = place(pair * g + i)
            plane.arrive(k)
            gather(other(k))

        each(pair, pick)
        each(pair, pick_other)

        def start_save(i):
            for b in (there(place(pair * g + i)), other(place(pair * g + i))):
                for copy in save(b):
                    copy.start()

        def end_save(i):
            for b in (there(place(pair * g + i)), other(place(pair * g + i))):
                for copy in save(b):
                    copy.wait()

        each(pair, start_save)

        @pl.when(g == 0)
        def _():
            for load in loads[:2]:
                load.wait()

        def column_step(k):
            if relayed:

                @pl.when((g == 1) & (k == local_experts // 2))
                def _():
                    up_column(2, True).wait_recv()

                    @pl.when(inner)
                    def _():
                        column_on().start()

            expert_step(g, k)

        each(local_experts, column_step)
        each(pair, end_save)
        grad_sems = ((core_s, core_r), (chip_s, chip_r))
        mix_sems = ((mcore_s, mcore_r), (mchip_s, mchip_r))
        pass_on(g, grads_of, xg, core_in, chip_out, chip_in, grad_sems)
        pass_on(g, mix_of, cg, mix_core_in, mix_out, mix_in, mix_sems)

    each(n_exp // GROUP, group_step)
    plane.hand(0, True).wait_send()
    each(chips, lambda k: plane.push(k).wait_send(), 1)
    each(chips, lambda k: plane.hand(k).wait_send(), 1)
    total[...] = grads_of(e)
    core_copy(0, xg, core_in, core_s, core_r).wait_recv()
    total[...] += core_in[0].astype(F32)

    def take_grads(i):
        k = chips - 1 - i
        chip_copy(k, chip_out, chip_in, chip_s, chip_r).wait_recv()
        total[...] += chip_in[k].astype(F32)

    each(chips - 1, take_grads)
    extra = ext[:, D:].astype(F32)
    gates = extra[:, :experts] + extra[:, experts : 2 * experts]
    dgates = total[:, D : D + experts] + total[:, D + experts : D + 2 * experts]
    dlogits = gates * (dgates - jnp.sum(gates * dgates, axis=-1, keepdims=True))
    dlogits = dlogits.astype(BF)
    normed2 = ext[:, :D]
    routed = mm_tn(dlogits, normed2)
    for k in range(D // LANES):
        router_part[k * experts : (k + 1) * experts] = routed[:, k * LANES : (k + 1) * LANES]
    dnormed2 = total[:, :D] + mm(dlogits, w_router[...])
    scaled2, inverse2 = row_scaling(hidden[...])
    norm2_part[...] = folded(jnp.sum(dnormed2 * scaled2, axis=0, keepdims=True))
    back = cot[...].astype(F32) + norm_backward(dnormed2, scaled2, inverse2, gain2[...])
    dhidden[...] = back
    dhidden_low[...] = back.astype(BF)

    total[:, :D] = hidden[...] + mix_of(e)
    core_copy(0, cg, mix_core_in, mcore_s, mcore_r).wait_recv()
    total[:, :D] += mix_core_in[0].astype(F32)

    def take_mix(i):
        k = chips - 1 - i
        chip_copy(k, mix_out, mix_in, mchip_s, mchip_r).wait_recv()
        total[:, :D] += mix_in[k].astype(F32)

    each(chips - 1, take_mix)
    layer_out[...] = total[:, :D].astype(BF)

    def sent_to_core(k):
        core_copy(k, xg, core_in, core_s, core_r).wait_send()
        core_copy(k, cg, mix_core_in, mcore_s, mcore_r).wait_send()

    def sent_to_chip(i):
        chip_copy(i + 1, chip_out, chip_in, chip_s, chip_r).wait_send()
        chip_copy(i + 1, mix_out, mix_in, mchip_s, mchip_r).wait_send()

    each(chips, sent_to_core)
    each(chips - 1, sent_to_chip)
    for k in range(1, n):
        if not (relayed and k == 2):
            up_column(k, True).wait_recv()
        if relayed and k == far:

            @pl.when(inner)
            def _():
                up_column(far).wait_send()
                column_on().wait_send()
        else:
            up_column(k).wait_send()


def own_experts(n, n_exp, ext, cot, cot_plane, w_gate_up, w_down, hidden, w_router, gain2, slots):
    rows = ext.shape[0]
    local_experts = w_gate_up.shape[0]
    experts = w_router.shape[0]
    chips = n_exp // 2
    v = pl.BlockSpec(memory_space=VMEM)
    hbm = pl.BlockSpec(memory_space=pl.ANY)
    sem = pltpu.SemaphoreType.DMA
    taken = n_exp * local_experts * slots
    return pl.pallas_call(
        functools.partial(own_experts_kernel, n, n_exp, local_experts),
        out_shape=(
            jax.ShapeDtypeStruct((rows, D), BF),
            jax.ShapeDtypeStruct((rows, D), F32),
            jax.ShapeDtypeStruct((rows, D), BF),
            jax.ShapeDtypeStruct((experts * (D // LANES), LANES), F32),
            jax.ShapeDtypeStruct((D // LANES, LANES), F32),
            jax.ShapeDtypeStruct((n, n_exp, rows, RW), BF),
        ),
        in_specs=[v, v, hbm, hbm, hbm, v, v, v],
        out_specs=[v] * 5 + [hbm],
        scratch_shapes=[
            pltpu.VMEM((n_exp, rows, XW), BF),
            pltpu.VMEM((n_exp, rows, D), BF),
            pltpu.VMEM(w_gate_up.shape, BF),
            pltpu.VMEM(w_down.shape, BF),
            pltpu.VMEM((n_exp, local_experts * slots, rows), BF),
            pltpu.VMEM((n_exp, local_experts * slots, XW), BF),
            pltpu.VMEM((n_exp, local_experts * slots, D), BF),
            pltpu.VMEM((chips, rows, XW), BF),
            pltpu.VMEM((chips, rows, XW), BF),
            pltpu.VMEM((chips, rows, XW), BF),
            pltpu.VMEM((chips, rows, D), BF),
            pltpu.VMEM((chips, rows, D), BF),
            pltpu.VMEM((chips, rows, D), BF),
            pltpu.VMEM((rows, XW), F32),
            pltpu.VMEM((rows, RW), BF),
            sem((n_exp,)),
            sem((2,)),
            sem((2, n_exp)),
            sem((n,)),
            sem((n,)),
        ]
        + [sem((chips,))] * 12,
        compiler_params=pltpu.CompilerParams(
            collective_id=2, has_side_effects=True, vmem_limit_bytes=63 * MIB
        ),
        cost_estimate=pl.CostEstimate(
            flops=2 * taken * 6 * D * FF, bytes_accessed=300 * MIB, transcendentals=0
        ),
    )(ext, cot, cot_plane, w_gate_up, w_down, hidden, w_router, gain2)


def expert_middle(x, gate_value, upstream, w_gate_up, w_down):
    units = mm(x, w_gate_up)
    gate, up = units[:, :FF], units[:, FF:]
    sig = sigmoid(gate)
    silu = gate * sig
    dmade = (gate_value * upstream.astype(F32)).astype(BF)
    dactive = mm_nt(dmade, w_down)
    dgate = dactive * up * sig * (1.0 + gate * (1.0 - sig))
    return dmade, (silu * up).astype(BF), dgate.astype(BF), (dactive * silu).astype(BF)


def expert_grads_kernel(n, n_exp, chunks, groups, early, local_experts, rows_all, *refs):
    z = lax.axis_index("tp")
    first = lax.axis_index("exp") * local_experts + early
    k, g = pl.program_id(0), pl.program_id(1)
    refs = list(refs)

    def take(count):
        got = refs[:count]
        del refs[:count]
        return got

    w_gate_up, w_down = take(2)
    if early:
        up_done, down_done = take(2)
    ends_in = take(4)
    gate_up_grad, down_grad, pair_grad, query_grad, out_grad, router_grad = take(6)
    input_grad, layer_out = take(2)
    rbuf, kept_x, kept_dy, kept_active, kept_dunits, acc_up, acc_down = take(7)
    summed, routed, got, layer, query_v, out_v, router_v = take(7)
    sems, out_sems, copy_sems, end_in_sems, end_out_sems = take(5)
    slots = kept_x.shape[0] // (chunks * GROUP)
    size = GROUP * slots
    last = local_experts - early - 1
    per_plane = n_exp // GROUP
    opening = (k == 0) & (g == 0)

    def brought():
        return (
            pltpu.make_async_copy(up_done, acc_up.at[pl.ds(0, early)], copy_sems.at[0]),
            pltpu.make_async_copy(down_done, acc_down.at[pl.ds(0, early)], copy_sems.at[1]),
        )

    def taken():
        at = pl.ds(0, early)
        return (
            pltpu.make_async_copy(acc_up.at[at], gate_up_grad.at[at], copy_sems.at[0]),
            pltpu.make_async_copy(acc_down.at[at], down_grad.at[at], copy_sems.at[1]),
        )

    def ends_came():
        return [
            pltpu.make_async_copy(a, b, end_in_sems.at[i])
            for i, (a, b) in enumerate(zip(ends_in, (summed, routed, got, layer)))
        ]

    def ends_go():
        pairs = (
            (query_v, query_grad),
            (out_v, out_grad),
            (router_v, router_grad),
            (got, input_grad),
            (layer, layer_out),
        )
        return [
            pltpu.make_async_copy(a, b, end_out_sems.at[i]) for i, (a, b) in enumerate(pairs)
        ]

    @pl.when(opening)
    def _():
        if early:
            for copy in brought():
                copy.start()
        for copy in ends_came():
            copy.start()

    def load(c, slot):
        at = g * chunks + c
        plane = z ^ (at // per_plane)
        b = lax.rem(at, per_plane) * GROUP
        return pltpu.make_async_copy(
            rows_all.at[plane, pl.ds(b, GROUP)], rbuf.at[slot], sems.at[slot]
        )

    load(0, 0).start()

    def chunk(c, carry):
        slot = lax.rem(c, 2)

        @pl.when(c + 1 < chunks)
        def _():
            load(c + 1, 1 - slot).start()

        load(c, slot).wait()
        if early:

            @pl.when(opening & (c == 2))
            def _():
                for copy in brought():
                    copy.wait()
                for copy in taken():
                    copy.start()

        wide = []
        for i in range(GROUP):
            s = selection(rbuf[slot, i, :, D:XW], first + k, 1, slots)
            wide.append(mm(s, rbuf[slot, i]))
        wide = jnp.concatenate(wide, axis=0)
        x = wide[:, :D].astype(BF)
        made = expert_middle(
            x, own_gate(wide[:, D:XW], first + k), wide[:, XW:], w_gate_up[0], w_down[0]
        )
        at = pl.ds(pl.multiple_of(c * size, size), size)
        kept_x[at] = x
        kept_dy[at] = made[0]
        kept_active[at] = made[1]
        kept_dunits[at, :FF] = made[2]
        kept_dunits[at, FF:] = made[3]
        return carry

    lax.fori_loop(0, chunks, chunk, 0)
    bank = lax.rem(k, 2)

    @pl.when(opening)
    def _():
        if early:
            for copy in taken():
                copy.wait()
        for copy in ends_came():
            copy.wait()
        qw, kv = query_v.shape[1], pair_grad.shape[1]
        query_v[...] = summed[:, :qw].astype(F32)
        for j in range(kv):
            at = qw + j * LANES
            pair_grad[:, j] = summed[:, at : at + LANES].astype(F32)
        out_v[...] = summed[:, qw + kv * LANES :].astype(F32).T
        experts = router_v.shape[0]
        for j in range(D // LANES):
            router_v[:, j * LANES : (j + 1) * LANES] = routed[j * experts : (j + 1) * experts]
        for copy in ends_go():
            copy.start()

    def store(kk):
        b = lax.rem(kk, 2)
        return (
            pltpu.make_async_copy(acc_up.at[b], gate_up_grad.at[early + kk], out_sems.at[0, b]),
            pltpu.make_async_copy(acc_down.at[b], down_grad.at[early + kk], out_sems.at[1, b]),
        )

    @pl.when((g == 0) & (k >= 2))
    def _():
        for copy in store(k - 2):
            copy.wait()

    def add(out, at, value):
        if groups == 1:
            out[bank, at] = value
        else:

            @pl.when(g == 0)
            def _():
                out[bank, at] = value

            @pl.when(g > 0)
            def _():
                out[bank, at] += value

    tile = 256

    def up_tile(m):
        at = pl.ds(pl.multiple_of(m * tile, tile), tile)
        add(acc_up, at, mm_tn(kept_x[:, at], kept_dunits[...]))

    each(D // tile, up_tile)

    def down_tile(m):
        at = pl.ds(pl.multiple_of(m * tile, tile), tile)
        add(acc_down, at, mm_tn(kept_active[:, at], kept_dy[...]))

    each(FF // tile, down_tile)

    @pl.when(g == groups - 1)
    def _():
        for copy in store(k):
            copy.start()

    @pl.when((g == groups - 1) & (k == last))
    def _():
        for copy in store(k):
            copy.wait()
        if last > 0:
            for copy in store(k - 1):
                copy.wait()
        for copy in ends_go():
            copy.wait()


def expert_grads(rows_all, w_gate_up, w_down, done, rest, slots, experts):
    n, n_exp, rows = rows_all.shape[:3]
    local_experts = w_gate_up.shape[0]
    early = done[0].shape[0] if done else 0
    assert early <= 2
    total = n * n_exp // GROUP
    chunks = min(total, 8)
    groups = total // chunks
    kept = chunks * GROUP * slots
    hbm = pl.BlockSpec(memory_space=pl.ANY)
    v = pl.BlockSpec(memory_space=VMEM)
    sem = pltpu.SemaphoreType.DMA
    width = rest[0].shape[1] // 3
    return pl.pallas_call(
        functools.partial(
            expert_grads_kernel, n, n_exp, chunks, groups, early, local_experts
        ),
        grid=(local_experts - early, groups),
        out_shape=(
            jax.ShapeDtypeStruct((local_experts, D, 2 * FF), F32),
            jax.ShapeDtypeStruct((local_experts, FF, D), F32),
            jax.ShapeDtypeStruct((D, width // LANES, LANES), F32),
            jax.ShapeDtypeStruct((D, width), F32),
            jax.ShapeDtypeStruct((width, D), F32),
            jax.ShapeDtypeStruct((experts, D), F32),
            jax.ShapeDtypeStruct(rest[2].shape, F32),
            jax.ShapeDtypeStruct(rest[3].shape, BF),
        ),
        in_specs=[
            hbm,
            pl.BlockSpec((1, D, 2 * FF), lambda k, g: (k + early, 0, 0)),
            pl.BlockSpec((1, FF, D), lambda k, g: (k + early, 0, 0)),
        ]
        + [hbm] * (len(done) + 4),
        out_specs=[hbm, hbm, v] + [hbm] * 5,
        scratch_shapes=[
            pltpu.VMEM((2, GROUP, rows, RW), BF),
            pltpu.VMEM((kept, D), BF),
            pltpu.VMEM((kept, D), BF),
            pltpu.VMEM((kept, FF), BF),
            pltpu.VMEM((kept, 2 * FF), BF),
            pltpu.VMEM((2, D, 2 * FF), F32),
            pltpu.VMEM((2, FF, D), F32),
        ]
        + [pltpu.VMEM(a.shape, a.dtype) for a in rest]
        + [
            pltpu.VMEM((D, width), F32),
            pltpu.VMEM((width, D), F32),
            pltpu.VMEM((experts, D), F32),
            sem((2,)),
            sem((2, 2)),
            sem((2,)),
            sem((4,)),
            sem((5,)),
        ],
        compiler_params=pltpu.CompilerParams(vmem_limit_bytes=60 * MIB),
        cost_estimate=pl.CostEstimate(
            flops=2 * total * GROUP * slots * local_experts * 6 * D * FF,
            bytes_accessed=300 * MIB,
            transcendentals=0,
        ),
    )(rows_all, w_gate_up, w_down, *done, *rest)


def backward_kernel(n, n_exp, early, local_experts, *refs):
    refs = list(refs)

    def take(count):
        got = refs[:count]
        del refs[:count]
        return got

    dhidden_low, dhidden, tokens, gain1, held, queries, pairs, mixed, totals = take(9)
    w_query, w_pair, w_out, router_part, norm2_part, prefix, _ = take(7)
    if early:
        w_gate_up, w_down = take(2)
    input_grad, summed, router, norms, all_rows = take(5)
    if early:
        gate_up_grad, down_grad = take(2)
    dfull, dqueries, dpairs, dpairs_low, sent, landed, line_norms, plane_norms = take(8)
    w_sum, w_core, w_chip_out, w_chip_in, r_in, r_line = take(6)
    ag_rs, ag_rr, ag_ls, ag_lr, rs_s, rs_r, push_s, push_r, pass_s, pass_r = take(10)
    nz_s, nz_r, np_s, np_r, r1_s, r1_r, r2_s, r2_r, r3_s, r3_r = take(10)
    wc_s, wc_r, wx_s, wx_r, wg_ps, wg_pr, wg_hs, wg_hr = take(8)
    if early:
        tokens_in, wgu, wd, acc_up, acc_down, kept_x, kept_c, kept_active, kept_dunits = take(9)
        load_s, w_sem, out_sem = take(3)

    e, z = lax.axis_index("exp"), lax.axis_index("tp")
    rows = tokens.shape[0]
    length = rows * n
    kv_local = pairs.shape[1] // LANES
    low = lax.broadcasted_iota(jnp.int32, (rows, LANES), 1) < HD
    scale = HD**-0.5
    first = e * local_experts

    if early:
        weights = [
            pltpu.make_async_copy(w_gate_up.at[pl.ds(0, early)], wgu, w_sem.at[0]),
            pltpu.make_async_copy(w_down.at[pl.ds(0, early)], wd, w_sem.at[1]),
        ]
        for copy in weights:
            copy.start()

    barrier = pltpu.get_barrier_semaphore()

    def greet_plane(k):
        pl.semaphore_signal(barrier, inc=1, device_id=(e ^ k, z), device_id_type=MESH)

    def greet_line(k):
        pl.semaphore_signal(barrier, inc=1, device_id=(e, z ^ k), device_id_type=MESH)

    each(n_exp, greet_plane, 1)
    each(n, greet_line, 1)
    dfull[pl.ds(pl.multiple_of(z * rows, rows), rows)] = dhidden_low[...]
    dpairs[...] = jnp.zeros_like(dpairs)
    if early:
        acc_up[...] = jnp.zeros_like(acc_up)
        acc_down[...] = jnp.zeros_like(acc_down)
    pl.semaphore_wait(barrier, n_exp + n - 2)

    line = LineGather(e, z, n, rows, dfull, (ag_rs, ag_rr), (ag_ls, ag_lr))
    line.begin()

    def plane(i):
        return PlaneGather(
            e,
            z,
            n_exp,
            all_rows.at[z ^ i, e],
            lambda b: all_rows.at[z ^ i, b],
            [lambda k, s=s: s.at[i, k] for s in (push_s, push_r, pass_s, pass_r)],
        )

    if n == 4 and early == 2:
        plane(1).begin_part(0, 4)
        plane(1).begin_part(1, 4)
    else:
        plane(1).begin()

    part_rows = r_in.shape[1]
    share = D // n_exp

    def routers(b):
        return router.at[pl.ds(pl.multiple_of(b * part_rows, part_rows), part_rows)]

    def router_give(k, landed=False):
        src = router_part.at[pl.ds(pl.multiple_of((e ^ k) * part_rows, part_rows), part_rows)]
        return pltpu.make_async_remote_copy(
            src_ref=src,
            dst_ref=r_in.at[(e ^ k) if landed else e],
            send_sem=r1_s.at[k],
            recv_sem=r1_r.at[k],
            device_id=(e ^ k, z),
            device_id_type=MESH,
        )

    def router_line(k, landed=False):
        return pltpu.make_async_remote_copy(
            src_ref=r_line.at[z],
            dst_ref=r_line.at[(z ^ k) if landed else z],
            send_sem=r2_s.at[k],
            recv_sem=r2_r.at[k],
            device_id=(e, z ^ k),
            device_id_type=MESH,
        )

    def router_gather(k, landed=False):
        return pltpu.make_async_remote_copy(
            src_ref=routers(e),
            dst_ref=routers((e ^ k) if landed else e),
            send_sem=r3_s.at[k],
            recv_sem=r3_r.at[k],
            device_id=(e ^ k, z),
            device_id_type=MESH,
        )

    r_in[e] = router_part[pl.ds(pl.multiple_of(e * part_rows, part_rows), part_rows)]
    each(n_exp, lambda k: router_give(k).start(), 1)

    def shares(ref, b):
        return ref.at[pl.ds(pl.multiple_of(b * share, share), share)]

    w_gather = PlaneGather(
        e,
        z,
        n_exp,
        shares(summed, e),
        lambda b: shares(summed, b),
        [lambda k, s=s: s.at[k] for s in (wg_ps, wg_pr, wg_hs, wg_hr)],
    )
    mine, other = w_gather.mine, w_gather.other

    def w_give(k):
        return pltpu.make_async_remote_copy(
            src_ref=shares(w_sum, other(k)),
            dst_ref=w_core.at[k],
            send_sem=wc_s.at[k],
            recv_sem=wc_r.at[k],
            device_id=(other(0), z),
            device_id_type=MESH,
        )

    def w_cross(k):
        return pltpu.make_async_remote_copy(
            src_ref=w_chip_out.at[k],
            dst_ref=w_chip_in.at[k],
            send_sem=wx_s.at[k],
            recv_sem=wx_r.at[k],
            device_id=(mine(k), z),
            device_id_type=MESH,
        )

    def own_share(b):
        return w_sum[pl.ds(pl.multiple_of(b * share, share), share)].astype(F32)

    def attend(d):
        at = pl.ds(pl.multiple_of(d * rows, rows), rows)
        seen = visible_mask(d, rows, length, prefix[0])
        dmixed = mm_nt(dfull[at], w_out[...]).astype(BF)
        stats = totals[at]
        for kv in range(kv_local):
            span = slice(kv * LANES, (kv + 1) * LANES)
            pair = pairs[:, span]
            outs = []
            added = jnp.zeros((length, LANES), F32)
            heads = halves(queries[at, span], low)
            grads = halves(dmixed[:, span], low)
            for h in range(2):
                head = (heads[h] * scale).astype(BF)
                grad = pltpu.roll(grads[h], HD, 1).astype(BF)
                stat = 2 * kv + h
                scores = mm_nt(head, pair)
                probs = jnp.where(seen, jnp.exp(scores - stats[:, stat : stat + 1]), 0.0)
                dprobs = mm_nt(grad, pair)
                inner = jnp.sum(probs * dprobs, axis=-1, keepdims=True)
                dscores = (probs * (dprobs - inner)).astype(BF)
                outs.append(mm(dscores, pair) * scale)
                added += mm_tn(dscores, head) + mm_tn(probs.astype(BF), grad)
            both = jnp.where(low, outs[0], pltpu.roll(outs[1], HD, 1))
            dqueries[at, span] = both.astype(BF)
            dpairs[:, span] += added

    def part(d):
        at = pl.ds(pl.multiple_of(d * rows, rows), rows)
        return mm_nt(dqueries[at], w_query[...]) + mm_nt(dpairs_low[at], w_pair[...])

    scatter = LineScatter(e, z, n, sent, landed, (rs_s, rs_r), part)

    def line_norm(k, landed=False):
        return pltpu.make_async_remote_copy(
            src_ref=line_norms.at[z],
            dst_ref=line_norms.at[(z ^ k) if landed else z],
            send_sem=nz_s.at[k],
            recv_sem=nz_r.at[k],
            device_id=(e, z ^ k),
            device_id_type=MESH,
        )

    def plane_norm(k, landed=False):
        return pltpu.make_async_remote_copy(
            src_ref=plane_norms.at[e],
            dst_ref=plane_norms.at[(e ^ k) if landed else e],
            send_sem=np_s.at[k],
            recv_sem=np_r.at[k],
            device_id=(e ^ k, z),
            device_id_type=MESH,
        )

    def event(t):
        @pl.when((t > 0) & (t < n))
        def _():
            line.step(t)

        @pl.when(t < n)
        def _():
            line.work(t, attend)

        @pl.when(t == n)
        def _():
            dpairs_low[...] = dpairs[...].astype(BF)

        @pl.when((t >= n) & (t < 2 * n - 1))
        def _():
            scatter.step(t - n)

        @pl.when(t == n)
        def _():
            qw, pw = dqueries.shape[1], dpairs_low.shape[1]
            w_sum[:, :qw] = mm_tn(held[...], dqueries[...]).astype(BF)
            w_sum[:, qw : qw + pw] = mm_tn(held[...], dpairs_low[...]).astype(BF)
            w_sum[:, qw + pw :] = mm_tn(dfull[...], mixed[...]).astype(BF)
            each(n_exp // 2, lambda k: w_give(k).start())
            each(n_exp, lambda k: router_give(k, True).wait_recv(), 1)
            total = r_in[0]
            for k in range(1, n_exp):
                total = total + r_in[k]
            r_line[z] = total
            each(n, lambda k: router_line(k).start(), 1)

        @pl.when(t == n + 1)
        def _():
            def cross(k):
                w_give(k).wait_recv()
                w_chip_out[k] = (own_share(mine(k)) + w_core[k].astype(F32)).astype(BF)
                w_cross(k).start()

            each(n_exp // 2, cross, 1)

        @pl.when(t == n + 2)
        def _():
            w_give(0).wait_recv()
            at = pl.ds(pl.multiple_of(e * share, share), share)
            total = own_share(e) + w_core[0].astype(F32)
            for k in range(1, n_exp // 2):
                w_cross(k).wait_recv()
                total = total + w_chip_in[k].astype(F32)
            summed[at] = total.astype(BF)
            w_gather.begin()
            each(n, lambda k: router_line(k, True).wait_recv(), 1)
            total = r_line[0]
            for k in range(1, n):
                total = total + r_line[k]
            router[pl.ds(pl.multiple_of(e * part_rows, part_rows), part_rows)] = total
            each(n_exp, lambda k: router_gather(k).start(), 1)

        @pl.when(t == 2 * n - 1)
        def _():
            scatter.finish(input_grad)
            dnormed1 = input_grad[...]
            scaled, inverse = row_scaling(tokens[...].astype(F32))
            half = D // LANES
            line_norms[z, :half] = folded(jnp.sum(dnormed1 * scaled, axis=0, keepdims=True))
            line_norms[z, half:] = norm2_part[...]
            each(n, lambda k: line_norm(k).start(), 1)
            back = dhidden[...] + norm_backward(dnormed1, scaled, inverse, gain1[...])
            input_grad[...] = back
            w_gather.turn()

        @pl.when(t == 2 * n)
        def _():
            each(n, lambda k: line_norm(k, True).wait_recv(), 1)
            total = line_norms[0]
            for k in range(1, n):
                total = total + line_norms[k]
            plane_norms[e] = total
            each(n_exp, lambda k: plane_norm(k).start(), 1)
            w_gather.turn_across()

    events = 2 * n + 1
    steps = n * (1 + early) if early else 0

    if n == 4 and early == 2:
        acts = {
            (0, 0): [("begin_part", 1, 2, 4)],
            (0, 1): [("begin_part", 1, 3, 4)],
            (0, 2): [("begin_part", 2, 0, 4)],
            (0, 3): [("turn", 1), ("begin_part", 2, 1, 4)],
            (0, 4): [("begin_part", 2, 2, 4), ("turn_across", 1)],
            (1, 0): [("begin_part", 2, 3, 4)],
            (1, 1): [("begin_part", 3, 0, 4)],
            (1, 2): [("begin_part", 3, 1, 4)],
            (1, 3): [("turn", 2), ("begin_part", 3, 2, 4)],
            (1, 4): [("begin_part", 3, 3, 4), ("turn_across", 2)],
            (2, 2): [("turn", 3)],
            (2, 4): [("turn_across", 3)],
        }
    else:
        acts = {}
        for i in range(1, n):
            acts[i - 1, 2] = [("turn", i)] + ([("begin", i + 1)] if i + 1 < n else [])
            acts[i - 1, 2 * early] = acts.get((i - 1, 2 * early), []) + [("turn_across", i)]

    def act(i, point):
        for (step, at), moves in acts.items():

            @pl.when((i == step) & (point == at))
            def _():
                for name, which, *more in moves:
                    getattr(plane(which), name)(*more)

    if early:
        slots = kept_x.shape[1] // n_exp
        for copy in weights:
            copy.wait()

        def one_plane(i, carry):
            @pl.when(i > 0)
            def _():
                each(n_exp // 2, plane(i).arrive)

            def load(b):
                slot = lax.rem(b, GROUP)
                return pltpu.make_async_copy(
                    all_rows.at[z ^ i, b], tokens_in.at[slot], load_s.at[slot]
                )

            each(GROUP, lambda b: load(b).start())

            def pick(b):
                load(b).wait()
                slot = lax.rem(b, GROUP)
                s = selection(tokens_in[slot, :, D:XW], first, early, slots)
                got = mm(s, tokens_in[slot]).astype(BF)
                at = pl.ds(pl.multiple_of(b * slots, slots), slots)
                for k in range(early):
                    here = got[k * slots : (k + 1) * slots]
                    kept_x[k, at] = here[:, :XW]
                    kept_c[k, at] = here[:, XW:]

                @pl.when(b + GROUP < n_exp)
                def _():
                    load(b + GROUP).start()

            each(n_exp, pick)
            event(i * (1 + early))
            act(i, 0)

            def expert(k):
                gate_value = own_gate(kept_x[k, :, D:], first + k)
                x = kept_x[k, :, :D]
                made = expert_middle(x, gate_value, kept_c[k], wgu[k], wd[k])
                kept_c[k] = made[0]
                kept_active[...] = made[1]
                kept_dunits[:, :FF] = made[2]
                kept_dunits[:, FF:] = made[3]
                acc_up[k] += mm_tn(kept_x[k, :, :D], kept_dunits[...])
                acc_down[k] += mm_tn(kept_active[...], kept_c[k])
                act(i, 2 * k + 1)
                event(i * (1 + early) + 1 + k)
                act(i, 2 * k + 2)

            each(early, expert)

            return carry

        lax.fori_loop(0, n, one_plane, 0)
        stores = [
            pltpu.make_async_copy(acc_up, gate_up_grad, out_sem.at[0]),
            pltpu.make_async_copy(acc_down, down_grad, out_sem.at[1]),
        ]
        for copy in stores:
            copy.start()
    each(max(events, steps), event, steps)
    if early:
        for copy in stores:
            copy.wait()
    else:

        def one_plane(i):
            plane(i).turn()

            @pl.when(i + 1 < n)
            def _():
                plane(i + 1).begin()

            plane(i).turn_across()

        each(n, one_plane, 1)
        each(n, lambda i: each(n_exp // 2, plane(i).arrive), 1)
    each(n_exp, lambda k: plane_norm(k, True).wait_recv(), 1)
    total = plane_norms[0]
    for k in range(1, n_exp):
        total = total + plane_norms[k]
    norms[...] = total
    each(n_exp // 2, w_gather.arrive)
    each(n_exp, lambda k: router_gather(k, True).wait_recv(), 1)
    each(n, lambda i: plane(i).drain(), 1)
    each(n, lambda k: line_norm(k).wait_send(), 1)
    each(n_exp, lambda k: plane_norm(k).wait_send(), 1)
    each(n_exp, lambda k: router_give(k).wait_send(), 1)
    each(n, lambda k: router_line(k).wait_send(), 1)
    each(n_exp, lambda k: router_gather(k).wait_send(), 1)
    each(n_exp // 2, lambda k: w_give(k).wait_send())
    each(n_exp // 2, lambda k: w_cross(k).wait_send(), 1)
    w_gather.drain()
    line.drain()
    scatter.drain()


def backward(n, n_exp, slots, whole, prefix, all_rows, weights):
    tokens, held = whole[2], whole[4]
    rows = tokens.shape[0]
    length = rows * n
    qw, pw = whole[9].shape[1], whole[10].shape[1]
    local_experts = weights[0].shape[0]
    early = local_experts // 2
    v = pl.BlockSpec(memory_space=VMEM)
    hbm = pl.BlockSpec(memory_space=pl.ANY)
    sem = pltpu.SemaphoreType.DMA
    chips = n_exp // 2
    width = 2 * qw + pw
    share = D // n_exp
    folds = D // LANES
    routed = whole[12].shape[0]
    outs = [
        (jax.ShapeDtypeStruct((rows, D), F32), v),
        (jax.ShapeDtypeStruct((D, width), BF), v),
        (jax.ShapeDtypeStruct((routed, LANES), F32), v),
        (jax.ShapeDtypeStruct((2 * folds, LANES), F32), v),
        (jax.ShapeDtypeStruct((n, n_exp, rows, RW), BF), hbm),
    ]
    scratch = [
        pltpu.VMEM((length, D), BF),
        pltpu.VMEM((length, qw), BF),
        pltpu.VMEM((length, pw), F32),
        pltpu.VMEM((length, pw), BF),
        pltpu.VMEM((n, rows, D), BF),
        pltpu.VMEM((n + 1, rows, D), BF),
        pltpu.VMEM((n, 2 * folds, LANES), F32),
        pltpu.VMEM((n_exp, 2 * folds, LANES), F32),
        pltpu.VMEM((D, width), BF),
        pltpu.VMEM((chips, share, width), BF),
        pltpu.VMEM((chips, share, width), BF),
        pltpu.VMEM((chips, share, width), BF),
        pltpu.VMEM((n_exp, routed // n_exp, LANES), F32),
        pltpu.VMEM((n, routed // n_exp, LANES), F32),
        sem((n,)),
        sem((n,)),
        sem((n,)),
        sem((n,)),
        sem((n,)),
        sem((n + 1,)),
    ]
    scratch += [sem((n, chips))] * 4
    scratch += [sem((n,))] * 2 + [sem((n_exp,))] * 4 + [sem((n,))] * 2 + [sem((n_exp,))] * 2
    scratch += [sem((chips,))] * 8
    if early:
        kept = n_exp * slots
        outs += [
            (jax.ShapeDtypeStruct((early, D, 2 * FF), F32), hbm),
            (jax.ShapeDtypeStruct((early, FF, D), F32), hbm),
        ]
        scratch += [
            pltpu.VMEM((GROUP, rows, RW), BF),
            pltpu.VMEM((early, D, 2 * FF), BF),
            pltpu.VMEM((early, FF, D), BF),
            pltpu.VMEM((early, D, 2 * FF), F32),
            pltpu.VMEM((early, FF, D), F32),
            pltpu.VMEM((early, kept, XW), BF),
            pltpu.VMEM((early, kept, D), BF),
            pltpu.VMEM((kept, FF), BF),
            pltpu.VMEM((kept, 2 * FF), BF),
            sem((GROUP,)),
            sem((2,)),
            sem((2,)),
        ]
    return pl.pallas_call(
        functools.partial(backward_kernel, n, n_exp, early, local_experts),
        out_shape=tuple(shape for shape, _ in outs),
        in_specs=[v] * len(whole)
        + [pl.BlockSpec(memory_space=pltpu.SMEM)]
        + [hbm] * (1 + (2 if early else 0)),
        out_specs=tuple(spec for _, spec in outs),
        input_output_aliases={len(whole) + 1: 4},
        scratch_shapes=scratch,
        compiler_params=pltpu.CompilerParams(
            collective_id=3, has_side_effects=True, vmem_limit_bytes=62 * MIB
        ),
        cost_estimate=pl.CostEstimate(
            flops=2 * length * D * 8 * qw, bytes_accessed=300 * MIB, transcendentals=0
        ),
    )(*whole, prefix, all_rows, *(weights if early else ()))


def local(
    n_exp,
    n_tp,
    tokens,
    norm1_gain,
    w_query,
    w_key_value,
    w_out,
    norm2_gain,
    w_router,
    w_gate_up,
    w_down,
    routes,
    prefix,
    cotangent,
):
    rows = tokens.shape[0]
    experts = w_router.shape[1]
    slots = slot_rows(rows, routes.shape[1], experts)
    w_pair = w_key_value.reshape(D, -1)
    gain1, gain2 = norm1_gain.reshape(1, D), norm2_gain.reshape(1, D)
    router_t = w_router.T
    hidden, ext, cot_plane, held, queries, pairs, mixed, totals = attention_forward(
        n_tp,
        n_exp,
        (tokens, w_query, w_pair, w_out, cotangent),
        (gain1, gain2, router_t, routes),
        prefix,
    )
    layer, dhidden, dhidden_low, router_part, norm2_part, all_rows = own_experts(
        n_tp,
        n_exp,
        ext,
        cotangent,
        cot_plane,
        w_gate_up,
        w_down,
        hidden,
        router_t,
        gain2,
        slots,
    )
    whole = (dhidden_low, dhidden, tokens, gain1, held, queries, pairs, mixed, totals)
    whole += (w_query, w_pair, w_out, router_part, norm2_part)
    made = backward(n_tp, n_exp, slots, whole, prefix, all_rows, (w_gate_up, w_down))
    got, summed, routed, norms, all_rows = made[:5]
    gate_up_grad, down_grad, pair_grad, query_grad, out_grad, router_grad, input_grad, layer_out = (
        expert_grads(
            all_rows,
            w_gate_up,
            w_down,
            made[5:],
            (summed, routed, got, layer),
            slots,
            experts,
        )
    )
    norms = norms.reshape(2, D)
    return (
        layer_out,
        input_grad,
        norms[0],
        query_grad,
        pair_grad,
        out_grad,
        norms[1],
        router_grad.T,
        gate_up_grad,
        down_grad,
    )


def solution(mesh):
    return jax.shard_map(
        functools.partial(local, mesh.shape["exp"], mesh.shape["tp"]),
        mesh=mesh,
        in_specs=(
            P(("exp", "tp"), None),
            P(),
            P(None, "tp"),
            P(None, "tp", None),
            P("tp", None),
            P(),
            P(),
            P("exp", None, None),
            P("exp", None, None),
            P(("exp", "tp"), None),
            P("exp"),
            P(("exp", "tp"), None),
        ),
        out_specs=(
            P(("exp", "tp"), None),
            P(("exp", "tp"), None),
            P(),
            P(None, "tp"),
            P(None, "tp", None),
            P("tp", None),
            P(),
            P(),
            P("exp", None, None),
            P("exp", None, None),
        ),
        check_vma=False,
    )
```

```python
import functools

import jax
import jax.numpy as jnp
from jax import lax
from jax.experimental import pallas as pl
from jax.experimental.pallas import tpu as pltpu
from jax.sharding import PartitionSpec as P

D = 1024
H = 16
KVH = 8
HD = 64
FF = 512
LANES = 128
XW = D + LANES
RW = XW + D
GROUP = 4

EPS = 1e-06
MASKED = -1e30
MESH = pl.DeviceIdType.MESH
BF = jnp.bfloat16
F32 = jnp.float32
VMEM = pltpu.VMEM
MIB = 1 << 20


def mm(a, b):
    return jnp.dot(a, b, preferred_element_type=F32)


def mm_nt(a, b):
    return lax.dot_general(a, b, (((1,), (1,)), ((), ())), preferred_element_type=F32)


def mm_tn(a, b):
    return lax.dot_general(a, b, (((0,), (0,)), ((), ())), preferred_element_type=F32)


def row_scaling(values):
    inverse = lax.rsqrt(jnp.mean(values * values, axis=-1, keepdims=True) + EPS)
    return values * inverse, inverse


def norm_backward(gradient, scaled, inverse, gain):
    weighted = gradient * gain
    inner = jnp.mean(weighted * scaled, axis=-1, keepdims=True)
    return inverse * (weighted - scaled * inner)


def block(ref, index, rows):
    return ref.at[pl.ds(pl.multiple_of(index * rows, rows), rows)]


def line_order(n):
    orders = []
    for z in range(n):
        right = list(range(n - 1, z, -1))
        left = list(range(z))
        first, second = (right, left) if len(right) >= len(left) else (left, right)
        order = []
        while first or second:
            if len(first) >= len(second):
                order.append(first.pop(0))
            else:
                order.append(second.pop(0))
        orders.append(order + [z])
    return orders


def lookup(table, z, j):
    value = jnp.int32(table[0][0])
    for a, row in enumerate(table):
        for b, entry in enumerate(row):
            value = jnp.where((z == a) & (j == b), jnp.int32(entry), value)
    return value


def greet(e, z, n, n_exp, line, plane):
    barrier = pltpu.get_barrier_semaphore()
    peers = jnp.int32(0)
    if line:

        @pl.when(z > 0)
        def _():
            pl.semaphore_signal(barrier, inc=1, device_id=(e, z - 1), device_id_type=MESH)

        @pl.when(z < n - 1)
        def _():
            pl.semaphore_signal(barrier, inc=1, device_id=(e, z + 1), device_id_type=MESH)

        peers += jnp.where(z > 0, 1, 0) + jnp.where(z < n - 1, 1, 0)
    if plane:
        chip, core = e // 2, lax.rem(e, 2)
        pl.semaphore_signal(barrier, inc=1, device_id=(e + 1 - 2 * core, z), device_id_type=MESH)

        def one(k, carry):
            there = 2 * (chip ^ k) + core
            pl.semaphore_signal(barrier, inc=1, device_id=(there, z), device_id_type=MESH)
            return carry

        lax.fori_loop(1, n_exp // 2, one, 0)
        peers += n_exp // 2
    return barrier, peers


def each(count, body, start=0):
    lax.fori_loop(start, count, lambda i, c: (body(i), c)[1], 0)


class PlaneGather:
    def __init__(self, e, z, n_exp, own, view, sems):
        self.e, self.z, self.own, self.view = e, z, own, view
        self.chip, self.core, self.chips = e // 2, lax.rem(e, 2), n_exp // 2
        self.push_s, self.push_r, self.pass_s, self.pass_r = sems
        self.square = self.chips == 4
        self.pushes = 3 if self.square else self.chips

    def mine(self, k):
        return 2 * (self.chip ^ k) + self.core

    def other(self, k):
        return 2 * (self.chip ^ k) + 1 - self.core

    def copy(self, src, dst, sems, at, device):
        return pltpu.make_async_remote_copy(
            src_ref=src,
            dst_ref=dst,
            send_sem=sems[0](at),
            recv_sem=sems[1](at),
            device_id=(device, self.z),
            device_id_type=MESH,
        )

    def push(self, k, landed=False):
        src = self.view(self.mine(k)) if landed else self.own
        dst = src if landed else self.view(self.e)
        return self.copy(src, dst, (self.push_s, self.push_r), k, self.mine(k))

    def hand(self, k, first=False, landed=False):
        there = self.view(self.other(k) if landed else self.mine(k))
        src = self.own if first else there
        return self.copy(src, there, (self.pass_s, self.pass_r), k, self.other(0))

    def across(self, half, landed=False):
        whole = self.view(self.mine(3 if landed else 1 + half))
        rows = whole.shape[0] // 2
        there = whole.at[pl.ds(half * rows, rows)]
        sems = (self.push_s, self.push_r)
        return self.copy(there, there, sems, 3 * half, self.mine(2 - half))

    def begin(self):
        each(self.pushes, lambda k: self.push(k).start(), 1)
        self.hand(0, True).start()

    def begin_part(self, part, parts):
        rows = self.own.shape[0] // parts
        at = pl.ds(part * rows, rows)
        for k in (1, 2):
            sems = (self.push_s, self.push_r)
            own, there = self.own.at[at], self.view(self.e).at[at]
            self.copy(own, there, sems, k, self.mine(k)).start()
        if part == 0:
            self.hand(0, True).start()

    def turn(self):
        def one(k):
            self.push(k, True).wait_recv()
            self.hand(k).start()

        if self.square:
            for half in range(2):
                self.push(1 + half, True).wait_recv()
                self.across(half).start()
                self.hand(1 + half).start()
        else:
            each(self.chips, one, 1)

    def turn_across(self):
        if self.square:
            for half in range(2):
                self.across(half, True).wait_recv()
            self.hand(3).start()

    def arrive(self, k):
        self.hand(k, landed=True).wait_recv()

    def drain(self):
        self.hand(0, True).wait_send()
        each(self.pushes, lambda k: self.push(k).wait_send(), 1)
        each(self.chips, lambda k: self.hand(k).wait_send(), 1)
        if self.square:
            for half in range(2):
                self.across(half).wait_send()


class LineGather:
    def __init__(self, e, z, n, rows, held, right_sems, left_sems):
        self.e, self.z, self.n, self.rows, self.held = e, z, n, rows, held
        self.sems = {1: right_sems, -1: left_sems}
        self.onward = {1: z < n - 1, -1: z > 0}

    def has(self, step, way):
        return self.z >= step if way > 0 else self.z + step < self.n

    def copy(self, step, way, landed=False):
        send, recv = self.sems[way]
        there = block(self.held, self.z - way * step, self.rows)
        return pltpu.make_async_remote_copy(
            src_ref=there,
            dst_ref=there,
            send_sem=send.at[step],
            recv_sem=recv.at[step - 1 if landed else step],
            device_id=(self.e, self.z + way),
            device_id_type=MESH,
        )

    def begin(self):
        for way in (1, -1):

            @pl.when(self.onward[way])
            def _():
                self.copy(0, way).start()

    def step(self, step):
        for way in (1, -1):

            @pl.when(self.has(step, way))
            def _():
                self.copy(step, way, True).wait_recv()

            @pl.when(self.has(step, way) & self.onward[way])
            def _():
                self.copy(step, way).start()

    def work(self, step, body):
        def one(way, carry):
            d = jnp.where(way > 0, self.z - step, self.z + step)

            @pl.when((d >= 0) & (d < self.n) & ((step > 0) | (way > 0)))
            def _():
                body(d)

            return carry

        lax.fori_loop(0, 2, one, 0)

    def drain(self):
        for step in range(self.n - 1):
            for way in (1, -1):

                @pl.when(self.has(step, way) & self.onward[way])
                def _():
                    self.copy(step, way).wait_send()


class LineScatter:
    def __init__(self, e, z, n, sent, landed, sems, part):
        self.e, self.z, self.n, self.sent, self.landed, self.part = e, z, n, sent, landed, part
        self.send, self.recv = sems
        self.table = line_order(n)

    def outgoing(self, d):
        right = d > self.z
        place = jnp.where(right | (d < self.z - 1), d, self.n)
        return pltpu.make_async_remote_copy(
            src_ref=self.sent.at[d],
            dst_ref=self.landed.at[place],
            send_sem=self.send.at[d],
            recv_sem=self.recv.at[place],
            device_id=(self.e, jnp.where(right, self.z + 1, self.z - 1)),
            device_id_type=MESH,
        )

    def incoming(self, place):
        return pltpu.make_async_remote_copy(
            src_ref=self.landed.at[place],
            dst_ref=self.landed.at[place],
            send_sem=self.send.at[0],
            recv_sem=self.recv.at[place],
            device_id=(self.e, jnp.where(self.z > 0, self.z - 1, self.z + 1)),
            device_id_type=MESH,
        )

    def step(self, j):
        d = lookup(self.table, self.z, j)
        value = self.part(d)
        upstream = jnp.where(d > self.z, self.z > 0, self.z < self.n - 1)

        @pl.when(upstream)
        def _():
            self.incoming(d).wait_recv()
            self.sent[d] = (value + self.landed[d].astype(F32)).astype(BF)

        @pl.when(jnp.logical_not(upstream))
        def _():
            self.sent[d] = value.astype(BF)

        self.outgoing(d).start()

    def finish(self, total):
        total[...] = self.part(self.z)

        @pl.when(self.z > 0)
        def _():
            self.incoming(self.z).wait_recv()
            total[...] += self.landed[self.z].astype(F32)

        @pl.when(self.z < self.n - 1)
        def _():
            self.incoming(self.n).wait_recv()
            total[...] += self.landed[self.n].astype(F32)

    def drain(self):
        for d in range(self.n):

            @pl.when(self.z != d)
            def _():
                self.outgoing(d).wait_send()


def visible_mask(d, rows, length, prefix):
    row_ids = d * rows + lax.broadcasted_iota(jnp.int32, (rows, length), 0)
    col_ids = lax.broadcasted_iota(jnp.int32, (rows, length), 1)
    return (col_ids <= row_ids) | (col_ids < prefix)


def halves(pair, low):
    pair = pair.astype(F32)
    zero = jnp.zeros_like(pair)
    return jnp.where(low, pair, zero), jnp.where(low, pltpu.roll(pair, HD, 1), zero)


def attention_forward_kernel(n, n_exp, *refs):
    tokens_in, w_query_in, w_pair, w_out_in, cot, gain1, gain2, w_router, routes, prefix = refs[:10]
    hidden_out, ext_out, cot_plane, held_out, queries_out, pairs_out, mixed_out, totals_out = refs[
        10:18
    ]
    tokens, w_query, w_out, hidden, ext, held, queries, pairs, mixed, totals = refs[18:28]
    sent, landed, ag_rs, ag_rr, ag_ls, ag_lr, rs_s, rs_r = refs[28:36]
    push_s, push_r, pass_s, pass_r, local_sem, in_sem, out_sem = refs[36:]
    e, z = lax.axis_index("exp"), lax.axis_index("tp")
    rows = tokens.shape[0]
    length = rows * n
    kv_local = pairs.shape[1] // LANES
    low = lax.broadcasted_iota(jnp.int32, (rows, LANES), 1) < HD
    ins = [
        pltpu.make_async_copy(a, b, in_sem.at[i])
        for i, (a, b) in enumerate(
            ((tokens_in, tokens), (w_query_in, w_query), (w_out_in, w_out))
        )
    ]
    outs = [
        pltpu.make_async_copy(a, b, out_sem.at[i])
        for i, (a, b) in enumerate(
            (
                (held, held_out),
                (queries, queries_out),
                (pairs, pairs_out),
                (mixed, mixed_out),
                (totals, totals_out),
                (hidden, hidden_out),
                (ext, ext_out),
            )
        )
    ]
    for copy in ins:
        copy.start()
    barrier, peers = greet(e, z, n, n_exp, True, True)
    ins[0].wait()
    scaled, _ = row_scaling(tokens[...].astype(F32))
    held[pl.ds(pl.multiple_of(z * rows, rows), rows)] = (scaled * gain1[...]).astype(BF)

    def project(d):
        at = pl.ds(pl.multiple_of(d * rows, rows), rows)
        normed = held[at]
        queries[at] = mm(normed, w_query[...]).astype(BF)
        pairs[at] = mm(normed, w_pair[...]).astype(BF)

    pl.semaphore_wait(barrier, peers)
    line = LineGather(e, z, n, rows, held, (ag_rs, ag_rr), (ag_ls, ag_lr))
    line.begin()
    plane = PlaneGather(
        e,
        z,
        n_exp,
        cot,
        lambda b: cot_plane.at[b],
        [lambda k, s=s: s.at[k] for s in (push_s, push_r, pass_s, pass_r)],
    )
    plane.begin()
    ins[1].wait()
    ins[2].wait()
    line.work(0, project)

    def gather_step(step):
        line.step(step)
        line.work(step, project)

    each(n, gather_step, 1)
    for copy in outs[:3]:
        copy.start()

    def part(d):
        at = pl.ds(pl.multiple_of(d * rows, rows), rows)
        seen = visible_mask(d, rows, length, prefix[0])
        lane = lax.broadcasted_iota(jnp.int32, (rows, LANES), 1)
        stats = jnp.zeros((rows, LANES), F32)
        for kv in range(kv_local):
            span = slice(kv * LANES, (kv + 1) * LANES)
            pair = pairs[:, span]
            outs = []
            for h, head in enumerate(halves(queries[at, span], low)):
                scores = mm_nt((head * HD**-0.5).astype(BF), pair)
                scores = jnp.where(seen, scores, MASKED)
                top = jnp.max(scores, axis=-1, keepdims=True)
                grown = jnp.exp(scores - top)
                total = jnp.sum(grown, axis=-1, keepdims=True)
                probs = (grown / total).astype(BF)
                outs.append(mm(probs, pair))
                stats = jnp.where(lane == 2 * kv + h, top + jnp.log(total), stats)
            both = jnp.where(low, pltpu.roll(outs[0], HD, 1), outs[1])
            mixed[at, span] = both.astype(BF)
        totals[at] = stats
        return mm(mixed[at], w_out[...])

    scatter = LineScatter(e, z, n, sent, landed, (rs_s, rs_r), part)
    each(n - 1, scatter.step)
    plane.turn()
    plane.turn_across()
    scatter.finish(hidden)
    for copy in outs[3:5]:
        copy.start()
    hid = tokens[...].astype(F32) + hidden[...]
    hidden[...] = hid
    scaled2, _ = row_scaling(hid)
    normed2 = (scaled2 * gain2[...]).astype(BF)
    ext[:, :D] = normed2
    experts = w_router.shape[0]
    logits = mm_nt(normed2, w_router[...])
    place = lax.broadcasted_iota(jnp.int32, (experts, rows), 0)
    named = place == routes[0:1, :]
    for k in range(1, routes.shape[0]):
        named = named | (place == routes[k : k + 1, :])
    square = (experts, experts)
    same = lax.broadcasted_iota(jnp.int32, square, 0) == lax.broadcasted_iota(jnp.int32, square, 1)
    named = jnp.where(named, 1.0, 0.0).astype(BF)
    chosen = mm_tn(named, jnp.where(same, 1.0, 0.0).astype(BF)) > 0.5
    logits = jnp.where(chosen, logits, MASKED)
    grown = jnp.exp(logits - jnp.max(logits, axis=-1, keepdims=True))
    grown = jnp.where(chosen, grown, 0.0)
    gates = grown / jnp.sum(grown, axis=-1, keepdims=True)
    high = gates.astype(BF)
    low_part = (gates - high.astype(F32)).astype(BF)
    mask = jnp.where(chosen, 1.0, 0.0).astype(BF)
    pad = jnp.zeros((rows, LANES - 3 * experts), BF)
    ext[:, D:] = jnp.concatenate([high, low_part, mask, pad], axis=1)
    for copy in outs[5:]:
        copy.start()
    each(n_exp // 2, plane.arrive)
    plane.drain()
    line.drain()
    scatter.drain()
    for copy in outs:
        copy.wait()


def attention_forward(n, n_exp, in_hbm, in_vmem, prefix):
    tokens, w_query, w_pair, w_out, cot = in_hbm
    rows = tokens.shape[0]
    length = rows * n
    qw, pw = w_query.shape[1], w_pair.shape[1]
    v = pl.BlockSpec(memory_space=VMEM)
    hbm = pl.BlockSpec(memory_space=pl.ANY)
    sem = pltpu.SemaphoreType.DMA
    made = (
        ((rows, D), F32),
        ((rows, XW), BF),
        ((length, D), BF),
        ((length, qw), BF),
        ((length, pw), BF),
        ((length, qw), BF),
        ((length, LANES), F32),
    )
    shapes = [jax.ShapeDtypeStruct(*m) for m in made]
    shapes.insert(2, jax.ShapeDtypeStruct((n_exp, rows, D), BF))
    return pl.pallas_call(
        functools.partial(attention_forward_kernel, n, n_exp),
        out_shape=tuple(shapes),
        in_specs=[hbm, hbm, v, hbm, hbm]
        + [v] * len(in_vmem)
        + [pl.BlockSpec(memory_space=pltpu.SMEM)],
        out_specs=[hbm] * 8,
        scratch_shapes=[
            pltpu.VMEM(tokens.shape, BF),
            pltpu.VMEM(w_query.shape, BF),
            pltpu.VMEM(w_out.shape, BF),
        ]
        + [pltpu.VMEM(*m) for m in made]
        + [
            pltpu.VMEM((n, rows, D), BF),
            pltpu.VMEM((n + 1, rows, D), BF),
            sem((n,)),
            sem((n,)),
            sem((n,)),
            sem((n,)),
            sem((n,)),
            sem((n + 1,)),
        ]
        + [sem((n_exp // 2,))] * 4
        + [sem, sem((3,)), sem((7,))],
        compiler_params=pltpu.CompilerParams(
            collective_id=1, has_side_effects=True, vmem_limit_bytes=60 * MIB
        ),
        cost_estimate=pl.CostEstimate(
            flops=2 * length * D * 4 * qw, bytes_accessed=300 * MIB, transcendentals=0
        ),
    )(*in_hbm, *in_vmem, prefix)


def slot_rows(rows, top_k, experts):
    capacity = rows * top_k * 5 // (experts * 4)
    return -(-capacity // 16) * 16


def selection(extra, first, local_experts, slots):
    rows = extra.shape[0]
    pick = lax.broadcasted_iota(jnp.int32, (8, LANES), 1) == (
        64 + first + lax.broadcasted_iota(jnp.int32, (8, LANES), 0)
    )
    named = mm_nt(jnp.where(pick, 1.0, 0.0).astype(BF), extra)
    earlier = lax.broadcasted_iota(jnp.int32, (rows, rows), 0) < lax.broadcasted_iota(
        jnp.int32, (rows, rows), 1
    )
    place = mm(named.astype(BF), jnp.where(earlier, 1.0, 0.0).astype(BF))
    place = jnp.where(named > 0.5, place, -1.0).astype(jnp.int32)
    slot = lax.broadcasted_iota(jnp.int32, (slots, rows), 0)
    parts = [
        jnp.where(slot == place[k : k + 1, :], 1.0, 0.0) for k in range(local_experts)
    ]
    return jnp.concatenate(parts, axis=0).astype(BF)


def own_gate(extra, expert):
    lane = lax.broadcasted_iota(jnp.int32, extra.shape, 1)
    mine = (lane == expert) | (lane == 32 + expert)
    return jnp.sum(jnp.where(mine, extra.astype(F32), 0.0), axis=-1, keepdims=True)


def folded(row):
    return jnp.concatenate(
        [row[:, k * LANES : (k + 1) * LANES] for k in range(D // LANES)], axis=0
    )


def sigmoid(v):
    return 1.0 / (1.0 + jnp.exp(-v))


def own_experts_kernel(
    n,
    n_exp,
    local_experts,
    ext,
    cot,
    cot_plane,
    w_gate_up,
    w_down,
    hidden,
    w_router,
    gain2,
    layer_out,
    dhidden,
    dhidden_low,
    router_part,
    norm2_part,
    all_rows,
    xg,
    cg,
    wgu,
    wd,
    sel,
    xs,
    cs,
    core_in,
    chip_out,
    chip_in,
    mix_core_in,
    mix_out,
    mix_in,
    total,
    joined,
    cot_sem,
    w_sem,
    out_sem,
    column_s,
    column_r,
    ag_s,
    ag_r,
    fw_s,
    fw_r,
    core_s,
    core_r,
    chip_s,
    chip_r,
    mcore_s,
    mcore_r,
    mchip_s,
    mchip_r,
):
    e, z = lax.axis_index("exp"), lax.axis_index("tp")
    rows = ext.shape[0]
    chips = n_exp // 2
    chip, core = e // 2, lax.rem(e, 2)
    partner = 2 * chip + 1 - core
    slots = sel.shape[1] // local_experts
    first = e * local_experts
    experts = w_router.shape[0]

    loads = [
        pltpu.make_async_copy(w_gate_up, wgu, w_sem.at[0]),
        pltpu.make_async_copy(w_down, wd, w_sem.at[1]),
    ]
    for load in loads:
        load.start()

    def cot_load(k):
        return pltpu.make_async_copy(cot_plane.at[e ^ k], cg.at[e ^ k], cot_sem.at[k])

    each(n_exp, lambda k: cot_load(k).start(), 1)
    cg[e] = cot[...]

    barrier, peers = greet(e, z, n, n_exp, False, True)
    for k in range(1, n):
        pl.semaphore_signal(barrier, inc=1, device_id=(e, z ^ k), device_id_type=MESH)
    xg[e] = ext[...]
    joined[:, :XW] = ext[...]
    joined[:, XW:] = cot[...]
    pl.semaphore_wait(barrier, peers + n - 1)
    plane = PlaneGather(
        e,
        z,
        n_exp,
        xg.at[e],
        lambda b: xg.at[b],
        [lambda k, s=s: s.at[k] for s in (ag_s, ag_r, fw_s, fw_r)],
    )
    there, other = plane.mine, plane.other

    def place(p):
        if chips != 4:
            return p
        return jnp.where(p == 0, 0, jnp.where(p == 1, 3, p - 1))

    pair = GROUP // 2
    each(pair, lambda p: plane.push(place(p)).start(), 1)
    plane.hand(0, True).start()

    def up_column(k, landed=False):
        return pltpu.make_async_remote_copy(
            src_ref=joined,
            dst_ref=all_rows.at[(z ^ k) if landed else z, e],
            send_sem=column_s.at[k],
            recv_sem=column_r.at[k],
            device_id=(e, z ^ k),
            device_id_type=MESH,
        )

    relayed = n == 4
    inner = (z == 1) | (z == 2)
    far = n - 1

    def column_on():
        at = all_rows.at[z ^ 2, e]
        return pltpu.make_async_remote_copy(
            src_ref=at,
            dst_ref=at,
            send_sem=column_s.at[0],
            recv_sem=column_r.at[far],
            device_id=(e, z ^ 1),
            device_id_type=MESH,
        )

    for k in range(1, n):
        if k == far and relayed:

            @pl.when(inner)
            def _():
                up_column(far).start()
        else:
            up_column(k).start()
    each(n_exp, lambda k: cot_load(k).wait(), 1)

    def gather(b):
        s = selection(xg[b, :, D:], first, local_experts, slots)
        sel[b] = s
        xs[b] = mm(s, xg[b]).astype(BF)
        cs[b] = mm(s, cg[b]).astype(BF)

    def save(b):
        return (
            pltpu.make_async_copy(xg.at[b], all_rows.at[z, b, :, pl.ds(0, XW)], out_sem.at[0, b]),
            pltpu.make_async_copy(cg.at[b], all_rows.at[z, b, :, pl.ds(XW, D)], out_sem.at[1, b]),
        )

    def save(b):
        return (
            pltpu.make_async_copy(
                xg.at[b], all_rows.at[z, b, :, pl.ds(0, XW)], out_sem.at[0, b]
            ),
            pltpu.make_async_copy(
                cg.at[b], all_rows.at[z, b, :, pl.ds(XW, D)], out_sem.at[1, b]
            ),
        )

    def members(g):
        return [f(place(pair * g + i)) for i in range(pair) for f in (there, other)]

    def expert_step(g, k):
        blocks = members(g)
        at = pl.ds(pl.multiple_of(k * slots, slots), slots)
        wide = jnp.concatenate([xs[b, at] for b in blocks], axis=0)
        gate_value = own_gate(wide[:, D:], first + k)
        units = mm(wide[:, :D], wgu[k])
        gate, up = units[:, :FF], units[:, FF:]
        sig = sigmoid(gate)
        silu = gate * sig
        active = (silu * up).astype(BF)
        made = mm(active, wd[k]).astype(BF).astype(F32)
        upstream = jnp.concatenate([cs[b, at] for b in blocks], axis=0).astype(F32)
        dgate_value = jnp.sum(upstream * made, axis=-1, keepdims=True)
        share = (gate_value * made).astype(BF)
        dmade = (gate_value * upstream).astype(BF)
        dactive = mm_nt(dmade, wd[k])
        dgate = dactive * up * sig * (1.0 + gate * (1.0 - sig))
        dunits = jnp.concatenate([dgate, dactive * silu], axis=1).astype(BF)
        dx = mm_nt(dunits, wgu[k]).astype(BF)
        lane = lax.broadcasted_iota(jnp.int32, (GROUP * slots, LANES), 1)
        high = dgate_value.astype(BF).astype(F32)
        packed = jnp.where(lane == first + k, high, 0.0)
        packed = jnp.where(lane == 32 + first + k, dgate_value - high, packed).astype(BF)
        for i, b in enumerate(blocks):
            here = slice(i * slots, (i + 1) * slots)
            xs[b, at, :D] = share[here]
            xs[b, at, D:] = packed[here]
            cs[b, at] = dx[here]

    def core_copy(k, src, dst, s, r):
        return pltpu.make_async_remote_copy(
            src_ref=src.at[other(k)],
            dst_ref=dst.at[k],
            send_sem=s.at[k],
            recv_sem=r.at[k],
            device_id=(partner, z),
            device_id_type=MESH,
        )

    def chip_copy(k, src, dst, s, r):
        return pltpu.make_async_remote_copy(
            src_ref=src.at[k],
            dst_ref=dst.at[k],
            send_sem=s.at[k],
            recv_sem=r.at[k],
            device_id=(there(k), z),
            device_id_type=MESH,
        )

    def grads_of(b):
        s = sel[b]
        return jnp.concatenate([mm_tn(s, cs[b]), mm_tn(s, xs[b, :, D:])], axis=1)

    def mix_of(b):
        return mm_tn(sel[b], xs[b, :, :D])

    def pass_on(g, of, kept, came, out, into, sems):
        core_sems, chip_sems = sems

        def give(i):
            k = place(pair * g + i)
            kept[other(k)] = of(other(k)).astype(BF)
            core_copy(k, kept, came, *core_sems).start()

        def send(i):
            k = place(pair * g + i)

            @pl.when(k > 0)
            def _():
                mine = of(there(k))
                core_copy(k, kept, came, *core_sems).wait_recv()
                out[k] = (mine + came[k].astype(F32)).astype(BF)
                chip_copy(k, out, into, *chip_sems).start()

        each(pair, give)
        each(pair, send)

    def group_step(g):
        @pl.when(g == 0)
        def _():
            gather(e)

        def turn(i):
            k = place(pair * g + i)

            @pl.when(k > 0)
            def _():
                plane.push(k, True).wait_recv()
                plane.hand(k).start()

        each(pair, turn)

        @pl.when(g == 0)
        def _():
            each(chips, lambda p: plane.push(place(p)).start(), pair)

        def pick(i):
            k = place(pair * g + i)

            @pl.when(k > 0)
            def _():
                gather(there(k))

        def pick_other(i):
            k = place(pair * g + i)
            plane.arrive(k)
            gather(other(k))

        each(pair, pick)
        each(pair, pick_other)

        def start_save(i):
            for b in (there(place(pair * g + i)), other(place(pair * g + i))):
                for copy in save(b):
                    copy.start()

        def end_save(i):
            for b in (there(place(pair * g + i)), other(place(pair * g + i))):
                for copy in save(b):
                    copy.wait()

        each(pair, start_save)

        @pl.when(g == 0)
        def _():
            for load in loads[:2]:
                load.wait()

        def column_step(k):
            if relayed:

                @pl.when((g == 1) & (k == local_experts // 2))
                def _():
                    up_column(2, True).wait_recv()

                    @pl.when(inner)
                    def _():
                        column_on().start()

            expert_step(g, k)

        each(local_experts, column_step)
        each(pair, end_save)
        grad_sems = ((core_s, core_r), (chip_s, chip_r))
        mix_sems = ((mcore_s, mcore_r), (mchip_s, mchip_r))
        pass_on(g, grads_of, xg, core_in, chip_out, chip_in, grad_sems)
        pass_on(g, mix_of, cg, mix_core_in, mix_out, mix_in, mix_sems)

    each(n_exp // GROUP, group_step)
    plane.hand(0, True).wait_send()
    each(chips, lambda k: plane.push(k).wait_send(), 1)
    each(chips, lambda k: plane.hand(k).wait_send(), 1)
    total[...] = grads_of(e)
    core_copy(0, xg, core_in, core_s, core_r).wait_recv()
    total[...] += core_in[0].astype(F32)

    def take_grads(i):
        k = chips - 1 - i
        chip_copy(k, chip_out, chip_in, chip_s, chip_r).wait_recv()
        total[...] += chip_in[k].astype(F32)

    each(chips - 1, take_grads)
    extra = ext[:, D:].astype(F32)
    gates = extra[:, :experts] + extra[:, experts : 2 * experts]
    dgates = total[:, D : D + experts] + total[:, D + experts : D + 2 * experts]
    dlogits = gates * (dgates - jnp.sum(gates * dgates, axis=-1, keepdims=True))
    dlogits = dlogits.astype(BF)
    normed2 = ext[:, :D]
    routed = mm_tn(dlogits, normed2)
    for k in range(D // LANES):
        router_part[k * experts : (k + 1) * experts] = routed[:, k * LANES : (k + 1) * LANES]
    dnormed2 = total[:, :D] + mm(dlogits, w_router[...])
    scaled2, inverse2 = row_scaling(hidden[...])
    norm2_part[...] = folded(jnp.sum(dnormed2 * scaled2, axis=0, keepdims=True))
    back = cot[...].astype(F32) + norm_backward(dnormed2, scaled2, inverse2, gain2[...])
    dhidden[...] = back
    dhidden_low[...] = back.astype(BF)

    total[:, :D] = hidden[...] + mix_of(e)
    core_copy(0, cg, mix_core_in, mcore_s, mcore_r).wait_recv()
    total[:, :D] += mix_core_in[0].astype(F32)

    def take_mix(i):
        k = chips - 1 - i
        chip_copy(k, mix_out, mix_in, mchip_s, mchip_r).wait_recv()
        total[:, :D] += mix_in[k].astype(F32)

    each(chips - 1, take_mix)
    layer_out[...] = total[:, :D].astype(BF)

    def sent_to_core(k):
        core_copy(k, xg, core_in, core_s, core_r).wait_send()
        core_copy(k, cg, mix_core_in, mcore_s, mcore_r).wait_send()

    def sent_to_chip(i):
        chip_copy(i + 1, chip_out, chip_in, chip_s, chip_r).wait_send()
        chip_copy(i + 1, mix_out, mix_in, mchip_s, mchip_r).wait_send()

    each(chips, sent_to_core)
    each(chips - 1, sent_to_chip)
    for k in range(1, n):
        if not (relayed and k == 2):
            up_column(k, True).wait_recv()
        if relayed and k == far:

            @pl.when(inner)
            def _():
                up_column(far).wait_send()
                column_on().wait_send()
        else:
            up_column(k).wait_send()


def own_experts(n, n_exp, ext, cot, cot_plane, w_gate_up, w_down, hidden, w_router, gain2, slots):
    rows = ext.shape[0]
    local_experts = w_gate_up.shape[0]
    experts = w_router.shape[0]
    chips = n_exp // 2
    v = pl.BlockSpec(memory_space=VMEM)
    hbm = pl.BlockSpec(memory_space=pl.ANY)
    sem = pltpu.SemaphoreType.DMA
    taken = n_exp * local_experts * slots
    return pl.pallas_call(
        functools.partial(own_experts_kernel, n, n_exp, local_experts),
        out_shape=(
            jax.ShapeDtypeStruct((rows, D), BF),
            jax.ShapeDtypeStruct((rows, D), F32),
            jax.ShapeDtypeStruct((rows, D), BF),
            jax.ShapeDtypeStruct((experts * (D // LANES), LANES), F32),
            jax.ShapeDtypeStruct((D // LANES, LANES), F32),
            jax.ShapeDtypeStruct((n, n_exp, rows, RW), BF),
        ),
        in_specs=[v, v, hbm, hbm, hbm, v, v, v],
        out_specs=[v] * 5 + [hbm],
        scratch_shapes=[
            pltpu.VMEM((n_exp, rows, XW), BF),
            pltpu.VMEM((n_exp, rows, D), BF),
            pltpu.VMEM(w_gate_up.shape, BF),
            pltpu.VMEM(w_down.shape, BF),
            pltpu.VMEM((n_exp, local_experts * slots, rows), BF),
            pltpu.VMEM((n_exp, local_experts * slots, XW), BF),
            pltpu.VMEM((n_exp, local_experts * slots, D), BF),
            pltpu.VMEM((chips, rows, XW), BF),
            pltpu.VMEM((chips, rows, XW), BF),
            pltpu.VMEM((chips, rows, XW), BF),
            pltpu.VMEM((chips, rows, D), BF),
            pltpu.VMEM((chips, rows, D), BF),
            pltpu.VMEM((chips, rows, D), BF),
            pltpu.VMEM((rows, XW), F32),
            pltpu.VMEM((rows, RW), BF),
            sem((n_exp,)),
            sem((2,)),
            sem((2, n_exp)),
            sem((n,)),
            sem((n,)),
        ]
        + [sem((chips,))] * 12,
        compiler_params=pltpu.CompilerParams(
            collective_id=2, has_side_effects=True, vmem_limit_bytes=63 * MIB
        ),
        cost_estimate=pl.CostEstimate(
            flops=2 * taken * 6 * D * FF, bytes_accessed=300 * MIB, transcendentals=0
        ),
    )(ext, cot, cot_plane, w_gate_up, w_down, hidden, w_router, gain2)


def expert_middle(x, gate_value, upstream, w_gate_up, w_down):
    units = mm(x, w_gate_up)
    gate, up = units[:, :FF], units[:, FF:]
    sig = sigmoid(gate)
    silu = gate * sig
    dmade = (gate_value * upstream.astype(F32)).astype(BF)
    dactive = mm_nt(dmade, w_down)
    dgate = dactive * up * sig * (1.0 + gate * (1.0 - sig))
    return dmade, (silu * up).astype(BF), dgate.astype(BF), (dactive * silu).astype(BF)


def expert_grads_kernel(n, n_exp, chunks, groups, early, local_experts, rows_all, *refs):
    z = lax.axis_index("tp")
    first = lax.axis_index("exp") * local_experts + early
    k, g = pl.program_id(0), pl.program_id(1)
    refs = list(refs)

    def take(count):
        got = refs[:count]
        del refs[:count]
        return got

    w_gate_up, w_down = take(2)
    if early:
        up_done, down_done = take(2)
    ends_in = take(4)
    gate_up_grad, down_grad, pair_grad, query_grad, out_grad, router_grad = take(6)
    input_grad, layer_out = take(2)
    rbuf, kept_x, kept_dy, kept_active, kept_dunits, acc_up, acc_down = take(7)
    summed, routed, got, layer, query_v, out_v, router_v = take(7)
    sems, out_sems, copy_sems, end_in_sems, end_out_sems = take(5)
    slots = kept_x.shape[0] // (chunks * GROUP)
    size = GROUP * slots
    last = local_experts - early - 1
    per_plane = n_exp // GROUP
    opening = (k == 0) & (g == 0)

    def brought():
        return (
            pltpu.make_async_copy(up_done, acc_up.at[pl.ds(0, early)], copy_sems.at[0]),
            pltpu.make_async_copy(down_done, acc_down.at[pl.ds(0, early)], copy_sems.at[1]),
        )

    def taken():
        at = pl.ds(0, early)
        return (
            pltpu.make_async_copy(acc_up.at[at], gate_up_grad.at[at], copy_sems.at[0]),
            pltpu.make_async_copy(acc_down.at[at], down_grad.at[at], copy_sems.at[1]),
        )

    def ends_came():
        return [
            pltpu.make_async_copy(a, b, end_in_sems.at[i])
            for i, (a, b) in enumerate(zip(ends_in, (summed, routed, got, layer)))
        ]

    def ends_go():
        pairs = (
            (query_v, query_grad),
            (out_v, out_grad),
            (router_v, router_grad),
            (got, input_grad),
            (layer, layer_out),
        )
        return [
            pltpu.make_async_copy(a, b, end_out_sems.at[i]) for i, (a, b) in enumerate(pairs)
        ]

    @pl.when(opening)
    def _():
        if early:
            for copy in brought():
                copy.start()
        for copy in ends_came():
            copy.start()

    def load(c, slot):
        at = g * chunks + c
        plane = z ^ (at // per_plane)
        b = lax.rem(at, per_plane) * GROUP
        return pltpu.make_async_copy(
            rows_all.at[plane, pl.ds(b, GROUP)], rbuf.at[slot], sems.at[slot]
        )

    load(0, 0).start()

    def chunk(c, carry):
        slot = lax.rem(c, 2)

        @pl.when(c + 1 < chunks)
        def _():
            load(c + 1, 1 - slot).start()

        load(c, slot).wait()
        if early:

            @pl.when(opening & (c == 2))
            def _():
                for copy in brought():
                    copy.wait()
                for copy in taken():
                    copy.start()

        wide = []
        for i in range(GROUP):
            s = selection(rbuf[slot, i, :, D:XW], first + k, 1, slots)
            wide.append(mm(s, rbuf[slot, i]))
        wide = jnp.concatenate(wide, axis=0)
        x = wide[:, :D].astype(BF)
        made = expert_middle(
            x, own_gate(wide[:, D:XW], first + k), wide[:, XW:], w_gate_up[0], w_down[0]
        )
        at = pl.ds(pl.multiple_of(c * size, size), size)
        kept_x[at] = x
        kept_dy[at] = made[0]
        kept_active[at] = made[1]
        kept_dunits[at, :FF] = made[2]
        kept_dunits[at, FF:] = made[3]
        return carry

    lax.fori_loop(0, chunks, chunk, 0)
    bank = lax.rem(k, 2)

    @pl.when(opening)
    def _():
        if early:
            for copy in taken():
                copy.wait()
        for copy in ends_came():
            copy.wait()
        qw, kv = query_v.shape[1], pair_grad.shape[1]
        query_v[...] = summed[:, :qw].astype(F32)
        for j in range(kv):
            at = qw + j * LANES
            pair_grad[:, j] = summed[:, at : at + LANES].astype(F32)
        out_v[...] = summed[:, qw + kv * LANES :].astype(F32).T
        experts = router_v.shape[0]
        for j in range(D // LANES):
            router_v[:, j * LANES : (j + 1) * LANES] = routed[j * experts : (j + 1) * experts]
        for copy in ends_go():
            copy.start()

    def store(kk):
        b = lax.rem(kk, 2)
        return (
            pltpu.make_async_copy(acc_up.at[b], gate_up_grad.at[early + kk], out_sems.at[0, b]),
            pltpu.make_async_copy(acc_down.at[b], down_grad.at[early + kk], out_sems.at[1, b]),
        )

    @pl.when((g == 0) & (k >= 2))
    def _():
        for copy in store(k - 2):
            copy.wait()

    def add(out, at, value):
        if groups == 1:
            out[bank, at] = value
        else:

            @pl.when(g == 0)
            def _():
                out[bank, at] = value

            @pl.when(g > 0)
            def _():
                out[bank, at] += value

    tile = 256

    def up_tile(m):
        at = pl.ds(pl.multiple_of(m * tile, tile), tile)
        add(acc_up, at, mm_tn(kept_x[:, at], kept_dunits[...]))

    each(D // tile, up_tile)

    def down_tile(m):
        at = pl.ds(pl.multiple_of(m * tile, tile), tile)
        add(acc_down, at, mm_tn(kept_active[:, at], kept_dy[...]))

    each(FF // tile, down_tile)

    @pl.when(g == groups - 1)
    def _():
        for copy in store(k):
            copy.start()

    @pl.when((g == groups - 1) & (k == last))
    def _():
        for copy in store(k):
            copy.wait()
        if last > 0:
            for copy in store(k - 1):
                copy.wait()
        for copy in ends_go():
            copy.wait()


def expert_grads(rows_all, w_gate_up, w_down, done, rest, slots, experts):
    n, n_exp, rows = rows_all.shape[:3]
    local_experts = w_gate_up.shape[0]
    early = done[0].shape[0] if done else 0
    assert early <= 2
    total = n * n_exp // GROUP
    chunks = min(total, 8)
    groups = total // chunks
    kept = chunks * GROUP * slots
    hbm = pl.BlockSpec(memory_space=pl.ANY)
    v = pl.BlockSpec(memory_space=VMEM)
    sem = pltpu.SemaphoreType.DMA
    width = rest[0].shape[1] // 3
    return pl.pallas_call(
        functools.partial(
            expert_grads_kernel, n, n_exp, chunks, groups, early, local_experts
        ),
        grid=(local_experts - early, groups),
        out_shape=(
            jax.ShapeDtypeStruct((local_experts, D, 2 * FF), F32),
            jax.ShapeDtypeStruct((local_experts, FF, D), F32),
            jax.ShapeDtypeStruct((D, width // LANES, LANES), F32),
            jax.ShapeDtypeStruct((D, width), F32),
            jax.ShapeDtypeStruct((width, D), F32),
            jax.ShapeDtypeStruct((experts, D), F32),
            jax.ShapeDtypeStruct(rest[2].shape, F32),
            jax.ShapeDtypeStruct(rest[3].shape, BF),
        ),
        in_specs=[
            hbm,
            pl.BlockSpec((1, D, 2 * FF), lambda k, g: (k + early, 0, 0)),
            pl.BlockSpec((1, FF, D), lambda k, g: (k + early, 0, 0)),
        ]
        + [hbm] * (len(done) + 4),
        out_specs=[hbm, hbm, v] + [hbm] * 5,
        scratch_shapes=[
            pltpu.VMEM((2, GROUP, rows, RW), BF),
            pltpu.VMEM((kept, D), BF),
            pltpu.VMEM((kept, D), BF),
            pltpu.VMEM((kept, FF), BF),
            pltpu.VMEM((kept, 2 * FF), BF),
            pltpu.VMEM((2, D, 2 * FF), F32),
            pltpu.VMEM((2, FF, D), F32),
        ]
        + [pltpu.VMEM(a.shape, a.dtype) for a in rest]
        + [
            pltpu.VMEM((D, width), F32),
            pltpu.VMEM((width, D), F32),
            pltpu.VMEM((experts, D), F32),
            sem((2,)),
            sem((2, 2)),
            sem((2,)),
            sem((4,)),
            sem((5,)),
        ],
        compiler_params=pltpu.CompilerParams(vmem_limit_bytes=60 * MIB),
        cost_estimate=pl.CostEstimate(
            flops=2 * total * GROUP * slots * local_experts * 6 * D * FF,
            bytes_accessed=300 * MIB,
            transcendentals=0,
        ),
    )(rows_all, w_gate_up, w_down, *done, *rest)


def backward_kernel(n, n_exp, early, local_experts, *refs):
    refs = list(refs)

    def take(count):
        got = refs[:count]
        del refs[:count]
        return got

    dhidden_low, dhidden, tokens, gain1, held, queries, pairs, mixed, totals = take(9)
    w_query, w_pair, w_out, router_part, norm2_part, prefix, _ = take(7)
    if early:
        w_gate_up, w_down = take(2)
    input_grad, summed, router, norms, all_rows = take(5)
    if early:
        gate_up_grad, down_grad = take(2)
    dfull, dqueries, dpairs, dpairs_low, sent, landed, line_norms, plane_norms = take(8)
    w_sum, w_core, w_chip_out, w_chip_in, r_in, r_line = take(6)
    ag_rs, ag_rr, ag_ls, ag_lr, rs_s, rs_r, push_s, push_r, pass_s, pass_r = take(10)
    nz_s, nz_r, np_s, np_r, r1_s, r1_r, r2_s, r2_r, r3_s, r3_r = take(10)
    wc_s, wc_r, wx_s, wx_r, wg_ps, wg_pr, wg_hs, wg_hr = take(8)
    if early:
        tokens_in, wgu, wd, acc_up, acc_down, kept_x, kept_c, kept_active, kept_dunits = take(9)
        load_s, w_sem, out_sem = take(3)

    e, z = lax.axis_index("exp"), lax.axis_index("tp")
    rows = tokens.shape[0]
    length = rows * n
    kv_local = pairs.shape[1] // LANES
    low = lax.broadcasted_iota(jnp.int32, (rows, LANES), 1) < HD
    scale = HD**-0.5
    first = e * local_experts

    if early:
        weights = [
            pltpu.make_async_copy(w_gate_up.at[pl.ds(0, early)], wgu, w_sem.at[0]),
            pltpu.make_async_copy(w_down.at[pl.ds(0, early)], wd, w_sem.at[1]),
        ]
        for copy in weights:
            copy.start()

    barrier = pltpu.get_barrier_semaphore()

    def greet_plane(k):
        pl.semaphore_signal(barrier, inc=1, device_id=(e ^ k, z), device_id_type=MESH)

    def greet_line(k):
        pl.semaphore_signal(barrier, inc=1, device_id=(e, z ^ k), device_id_type=MESH)

    each(n_exp, greet_plane, 1)
    each(n, greet_line, 1)
    dfull[pl.ds(pl.multiple_of(z * rows, rows), rows)] = dhidden_low[...]
    dpairs[...] = jnp.zeros_like(dpairs)
    if early:
        acc_up[...] = jnp.zeros_like(acc_up)
        acc_down[...] = jnp.zeros_like(acc_down)
    pl.semaphore_wait(barrier, n_exp + n - 2)

    line = LineGather(e, z, n, rows, dfull, (ag_rs, ag_rr), (ag_ls, ag_lr))
    line.begin()

    def plane(i):
        return PlaneGather(
            e,
            z,
            n_exp,
            all_rows.at[z ^ i, e],
            lambda b: all_rows.at[z ^ i, b],
            [lambda k, s=s: s.at[i, k] for s in (push_s, push_r, pass_s, pass_r)],
        )

    if n == 4 and early == 2:
        plane(1).begin_part(0, 4)
        plane(1).begin_part(1, 4)
    else:
        plane(1).begin()

    part_rows = r_in.shape[1]
    share = D // n_exp

    def routers(b):
        return router.at[pl.ds(pl.multiple_of(b * part_rows, part_rows), part_rows)]

    def router_give(k, landed=False):
        src = router_part.at[pl.ds(pl.multiple_of((e ^ k) * part_rows, part_rows), part_rows)]
        return pltpu.make_async_remote_copy(
            src_ref=src,
            dst_ref=r_in.at[(e ^ k) if landed else e],
            send_sem=r1_s.at[k],
            recv_sem=r1_r.at[k],
            device_id=(e ^ k, z),
            device_id_type=MESH,
        )

    def router_line(k, landed=False):
        return pltpu.make_async_remote_copy(
            src_ref=r_line.at[z],
            dst_ref=r_line.at[(z ^ k) if landed else z],
            send_sem=r2_s.at[k],
            recv_sem=r2_r.at[k],
            device_id=(e, z ^ k),
            device_id_type=MESH,
        )

    def router_gather(k, landed=False):
        return pltpu.make_async_remote_copy(
            src_ref=routers(e),
            dst_ref=routers((e ^ k) if landed else e),
            send_sem=r3_s.at[k],
            recv_sem=r3_r.at[k],
            device_id=(e ^ k, z),
            device_id_type=MESH,
        )

    r_in[e] = router_part[pl.ds(pl.multiple_of(e * part_rows, part_rows), part_rows)]
    each(n_exp, lambda k: router_give(k).start(), 1)

    def shares(ref, b):
        return ref.at[pl.ds(pl.multiple_of(b * share, share), share)]

    w_gather = PlaneGather(
        e,
        z,
        n_exp,
        shares(summed, e),
        lambda b: shares(summed, b),
        [lambda k, s=s: s.at[k] for s in (wg_ps, wg_pr, wg_hs, wg_hr)],
    )
    mine, other = w_gather.mine, w_gather.other

    def w_give(k):
        return pltpu.make_async_remote_copy(
            src_ref=shares(w_sum, other(k)),
            dst_ref=w_core.at[k],
            send_sem=wc_s.at[k],
            recv_sem=wc_r.at[k],
            device_id=(other(0), z),
            device_id_type=MESH,
        )

    def w_cross(k):
        return pltpu.make_async_remote_copy(
            src_ref=w_chip_out.at[k],
            dst_ref=w_chip_in.at[k],
            send_sem=wx_s.at[k],
            recv_sem=wx_r.at[k],
            device_id=(mine(k), z),
            device_id_type=MESH,
        )

    def own_share(b):
        return w_sum[pl.ds(pl.multiple_of(b * share, share), share)].astype(F32)

    def attend(d):
        at = pl.ds(pl.multiple_of(d * rows, rows), rows)
        seen = visible_mask(d, rows, length, prefix[0])
        dmixed = mm_nt(dfull[at], w_out[...]).astype(BF)
        stats = totals[at]
        for kv in range(kv_local):
            span = slice(kv * LANES, (kv + 1) * LANES)
            pair = pairs[:, span]
            outs = []
            added = jnp.zeros((length, LANES), F32)
            heads = halves(queries[at, span], low)
            grads = halves(dmixed[:, span], low)
            for h in range(2):
                head = (heads[h] * scale).astype(BF)
                grad = pltpu.roll(grads[h], HD, 1).astype(BF)
                stat = 2 * kv + h
                scores = mm_nt(head, pair)
                probs = jnp.where(seen, jnp.exp(scores - stats[:, stat : stat + 1]), 0.0)
                dprobs = mm_nt(grad, pair)
                inner = jnp.sum(probs * dprobs, axis=-1, keepdims=True)
                dscores = (probs * (dprobs - inner)).astype(BF)
                outs.append(mm(dscores, pair) * scale)
                added += mm_tn(dscores, head) + mm_tn(probs.astype(BF), grad)
            both = jnp.where(low, outs[0], pltpu.roll(outs[1], HD, 1))
            dqueries[at, span] = both.astype(BF)
            dpairs[:, span] += added

    def part(d):
        at = pl.ds(pl.multiple_of(d * rows, rows), rows)
        return mm_nt(dqueries[at], w_query[...]) + mm_nt(dpairs_low[at], w_pair[...])

    scatter = LineScatter(e, z, n, sent, landed, (rs_s, rs_r), part)

    def line_norm(k, landed=False):
        return pltpu.make_async_remote_copy(
            src_ref=line_norms.at[z],
            dst_ref=line_norms.at[(z ^ k) if landed else z],
            send_sem=nz_s.at[k],
            recv_sem=nz_r.at[k],
            device_id=(e, z ^ k),
            device_id_type=MESH,
        )

    def plane_norm(k, landed=False):
        return pltpu.make_async_remote_copy(
            src_ref=plane_norms.at[e],
            dst_ref=plane_norms.at[(e ^ k) if landed else e],
            send_sem=np_s.at[k],
            recv_sem=np_r.at[k],
            device_id=(e ^ k, z),
            device_id_type=MESH,
        )

    def event(t):
        @pl.when((t > 0) & (t < n))
        def _():
            line.step(t)

        @pl.when(t < n)
        def _():
            line.work(t, attend)

        @pl.when(t == n)
        def _():
            dpairs_low[...] = dpairs[...].astype(BF)

        @pl.when((t >= n) & (t < 2 * n - 1))
        def _():
            scatter.step(t - n)

        @pl.when(t == n)
        def _():
            qw, pw = dqueries.shape[1], dpairs_low.shape[1]
            w_sum[:, :qw] = mm_tn(held[...], dqueries[...]).astype(BF)
            w_sum[:, qw : qw + pw] = mm_tn(held[...], dpairs_low[...]).astype(BF)
            w_sum[:, qw + pw :] = mm_tn(dfull[...], mixed[...]).astype(BF)
            each(n_exp // 2, lambda k: w_give(k).start())
            each(n_exp, lambda k: router_give(k, True).wait_recv(), 1)
            total = r_in[0]
            for k in range(1, n_exp):
                total = total + r_in[k]
            r_line[z] = total
            each(n, lambda k: router_line(k).start(), 1)

        @pl.when(t == n + 1)
        def _():
            def cross(k):
                w_give(k).wait_recv()
                w_chip_out[k] = (own_share(mine(k)) + w_core[k].astype(F32)).astype(BF)
                w_cross(k).start()

            each(n_exp // 2, cross, 1)

        @pl.when(t == n + 2)
        def _():
            w_give(0).wait_recv()
            at = pl.ds(pl.multiple_of(e * share, share), share)
            total = own_share(e) + w_core[0].astype(F32)
            for k in range(1, n_exp // 2):
                w_cross(k).wait_recv()
                total = total + w_chip_in[k].astype(F32)
            summed[at] = total.astype(BF)
            w_gather.begin()
            each(n, lambda k: router_line(k, True).wait_recv(), 1)
            total = r_line[0]
            for k in range(1, n):
                total = total + r_line[k]
            router[pl.ds(pl.multiple_of(e * part_rows, part_rows), part_rows)] = total
            each(n_exp, lambda k: router_gather(k).start(), 1)

        @pl.when(t == 2 * n - 1)
        def _():
            scatter.finish(input_grad)
            dnormed1 = input_grad[...]
            scaled, inverse = row_scaling(tokens[...].astype(F32))
            half = D // LANES
            line_norms[z, :half] = folded(jnp.sum(dnormed1 * scaled, axis=0, keepdims=True))
            line_norms[z, half:] = norm2_part[...]
            each(n, lambda k: line_norm(k).start(), 1)
            back = dhidden[...] + norm_backward(dnormed1, scaled, inverse, gain1[...])
            input_grad[...] = back
            w_gather.turn()

        @pl.when(t == 2 * n)
        def _():
            each(n, lambda k: line_norm(k, True).wait_recv(), 1)
            total = line_norms[0]
            for k in range(1, n):
                total = total + line_norms[k]
            plane_norms[e] = total
            each(n_exp, lambda k: plane_norm(k).start(), 1)
            w_gather.turn_across()

    events = 2 * n + 1
    steps = n * (1 + early) if early else 0

    if n == 4 and early == 2:
        acts = {
            0: [("begin_part", 1, 2, 4), ("begin_part", 1, 3, 4)],
            1: [("begin_part", 2, 0, 4), ("turn", 1), ("begin_part", 2, 1, 4)],
            2: [("begin_part", 2, 2, 4), ("turn_across", 1)],
            3: [("begin_part", 2, 3, 4), ("begin_part", 3, 0, 4)],
            4: [("begin_part", 3, 1, 4), ("turn", 2), ("begin_part", 3, 2, 4)],
            5: [("begin_part", 3, 3, 4), ("turn_across", 2)],
            7: [("turn", 3)],
            8: [("turn_across", 3)],
        }
    else:
        acts = {}
        for i in range(1, n):
            at = (i - 1) * (1 + early) + 1
            acts[at] = [("turn", i)] + ([("begin", i + 1)] if i + 1 < n else [])
            acts[at + early - 1] = acts.get(at + early - 1, []) + [("turn_across", i)]

    def act(t):
        for at, moves in acts.items():

            @pl.when(t == at)
            def _():
                for name, which, *more in moves:
                    getattr(plane(which), name)(*more)

    if early:
        slots = kept_x.shape[1] // n_exp
        for copy in weights:
            copy.wait()

        def pick_plane(i):
            @pl.when(i > 0)
            def _():
                each(n_exp // 2, plane(i).arrive)

            def load(b):
                slot = lax.rem(b, GROUP)
                return pltpu.make_async_copy(
                    all_rows.at[z ^ i, b], tokens_in.at[slot], load_s.at[slot]
                )

            each(GROUP, lambda b: load(b).start())

            def pick(b):
                load(b).wait()
                slot = lax.rem(b, GROUP)
                s = selection(tokens_in[slot, :, D:XW], first, early, slots)
                got = mm(s, tokens_in[slot]).astype(BF)
                at = pl.ds(pl.multiple_of(b * slots, slots), slots)
                for k in range(early):
                    here = got[k * slots : (k + 1) * slots]
                    kept_x[k, at] = here[:, :XW]
                    kept_c[k, at] = here[:, XW:]

                @pl.when(b + GROUP < n_exp)
                def _():
                    load(b + GROUP).start()

            each(n_exp, pick)

        def expert(k):
            gate_value = own_gate(kept_x[k, :, D:], first + k)
            x = kept_x[k, :, :D]
            made = expert_middle(x, gate_value, kept_c[k], wgu[k], wd[k])
            kept_c[k] = made[0]
            kept_active[...] = made[1]
            kept_dunits[:, :FF] = made[2]
            kept_dunits[:, FF:] = made[3]
            acc_up[k] += mm_tn(kept_x[k, :, :D], kept_dunits[...])
            acc_down[k] += mm_tn(kept_active[...], kept_c[k])

        def one_step(t):
            i, r = t // (1 + early), lax.rem(t, 1 + early)

            @pl.when(r == 0)
            def _():
                pick_plane(i)

            @pl.when(r > 0)
            def _():
                expert(r - 1)

            event(t)
            act(t)

        each(steps, one_step)
        stores = [
            pltpu.make_async_copy(acc_up, gate_up_grad, out_sem.at[0]),
            pltpu.make_async_copy(acc_down, down_grad, out_sem.at[1]),
        ]
        for copy in stores:
            copy.start()
    if steps < events:
        each(events, event, steps)
    if early:
        for copy in stores:
            copy.wait()
    else:

        def one_plane(i):
            plane(i).turn()

            @pl.when(i + 1 < n)
            def _():
                plane(i + 1).begin()

            plane(i).turn_across()

        each(n, one_plane, 1)
        each(n, lambda i: each(n_exp // 2, plane(i).arrive), 1)
    each(n_exp, lambda k: plane_norm(k, True).wait_recv(), 1)
    total = plane_norms[0]
    for k in range(1, n_exp):
        total = total + plane_norms[k]
    norms[...] = total
    each(n_exp // 2, w_gather.arrive)
    each(n_exp, lambda k: router_gather(k, True).wait_recv(), 1)
    each(n, lambda i: plane(i).drain(), 1)
    each(n, lambda k: line_norm(k).wait_send(), 1)
    each(n_exp, lambda k: plane_norm(k).wait_send(), 1)
    each(n_exp, lambda k: router_give(k).wait_send(), 1)
    each(n, lambda k: router_line(k).wait_send(), 1)
    each(n_exp, lambda k: router_gather(k).wait_send(), 1)
    each(n_exp // 2, lambda k: w_give(k).wait_send())
    each(n_exp // 2, lambda k: w_cross(k).wait_send(), 1)
    w_gather.drain()
    line.drain()
    scatter.drain()


def backward(n, n_exp, slots, whole, prefix, all_rows, weights):
    tokens, held = whole[2], whole[4]
    rows = tokens.shape[0]
    length = rows * n
    qw, pw = whole[9].shape[1], whole[10].shape[1]
    local_experts = weights[0].shape[0]
    early = local_experts // 2
    v = pl.BlockSpec(memory_space=VMEM)
    hbm = pl.BlockSpec(memory_space=pl.ANY)
    sem = pltpu.SemaphoreType.DMA
    chips = n_exp // 2
    width = 2 * qw + pw
    share = D // n_exp
    folds = D // LANES
    routed = whole[12].shape[0]
    outs = [
        (jax.ShapeDtypeStruct((rows, D), F32), v),
        (jax.ShapeDtypeStruct((D, width), BF), v),
        (jax.ShapeDtypeStruct((routed, LANES), F32), v),
        (jax.ShapeDtypeStruct((2 * folds, LANES), F32), v),
        (jax.ShapeDtypeStruct((n, n_exp, rows, RW), BF), hbm),
    ]
    scratch = [
        pltpu.VMEM((length, D), BF),
        pltpu.VMEM((length, qw), BF),
        pltpu.VMEM((length, pw), F32),
        pltpu.VMEM((length, pw), BF),
        pltpu.VMEM((n, rows, D), BF),
        pltpu.VMEM((n + 1, rows, D), BF),
        pltpu.VMEM((n, 2 * folds, LANES), F32),
        pltpu.VMEM((n_exp, 2 * folds, LANES), F32),
        pltpu.VMEM((D, width), BF),
        pltpu.VMEM((chips, share, width), BF),
        pltpu.VMEM((chips, share, width), BF),
        pltpu.VMEM((chips, share, width), BF),
        pltpu.VMEM((n_exp, routed // n_exp, LANES), F32),
        pltpu.VMEM((n, routed // n_exp, LANES), F32),
        sem((n,)),
        sem((n,)),
        sem((n,)),
        sem((n,)),
        sem((n,)),
        sem((n + 1,)),
    ]
    scratch += [sem((n, chips))] * 4
    scratch += [sem((n,))] * 2 + [sem((n_exp,))] * 4 + [sem((n,))] * 2 + [sem((n_exp,))] * 2
    scratch += [sem((chips,))] * 8
    if early:
        kept = n_exp * slots
        outs += [
            (jax.ShapeDtypeStruct((early, D, 2 * FF), F32), hbm),
            (jax.ShapeDtypeStruct((early, FF, D), F32), hbm),
        ]
        scratch += [
            pltpu.VMEM((GROUP, rows, RW), BF),
            pltpu.VMEM((early, D, 2 * FF), BF),
            pltpu.VMEM((early, FF, D), BF),
            pltpu.VMEM((early, D, 2 * FF), F32),
            pltpu.VMEM((early, FF, D), F32),
            pltpu.VMEM((early, kept, XW), BF),
            pltpu.VMEM((early, kept, D), BF),
            pltpu.VMEM((kept, FF), BF),
            pltpu.VMEM((kept, 2 * FF), BF),
            sem((GROUP,)),
            sem((2,)),
            sem((2,)),
        ]
    return pl.pallas_call(
        functools.partial(backward_kernel, n, n_exp, early, local_experts),
        out_shape=tuple(shape for shape, _ in outs),
        in_specs=[v] * len(whole)
        + [pl.BlockSpec(memory_space=pltpu.SMEM)]
        + [hbm] * (1 + (2 if early else 0)),
        out_specs=tuple(spec for _, spec in outs),
        input_output_aliases={len(whole) + 1: 4},
        scratch_shapes=scratch,
        compiler_params=pltpu.CompilerParams(
            collective_id=3, has_side_effects=True, vmem_limit_bytes=62 * MIB
        ),
        cost_estimate=pl.CostEstimate(
            flops=2 * length * D * 8 * qw, bytes_accessed=300 * MIB, transcendentals=0
        ),
    )(*whole, prefix, all_rows, *(weights if early else ()))


def local(
    n_exp,
    n_tp,
    tokens,
    norm1_gain,
    w_query,
    w_key_value,
    w_out,
    norm2_gain,
    w_router,
    w_gate_up,
    w_down,
    routes,
    prefix,
    cotangent,
):
    rows = tokens.shape[0]
    experts = w_router.shape[1]
    slots = slot_rows(rows, routes.shape[1], experts)
    w_pair = w_key_value.reshape(D, -1)
    gain1, gain2 = norm1_gain.reshape(1, D), norm2_gain.reshape(1, D)
    router_t = w_router.T
    hidden, ext, cot_plane, held, queries, pairs, mixed, totals = attention_forward(
        n_tp,
        n_exp,
        (tokens, w_query, w_pair, w_out, cotangent),
        (gain1, gain2, router_t, routes.T),
        prefix,
    )
    layer, dhidden, dhidden_low, router_part, norm2_part, all_rows = own_experts(
        n_tp,
        n_exp,
        ext,
        cotangent,
        cot_plane,
        w_gate_up,
        w_down,
        hidden,
        router_t,
        gain2,
        slots,
    )
    whole = (dhidden_low, dhidden, tokens, gain1, held, queries, pairs, mixed, totals)
    whole += (w_query, w_pair, w_out, router_part, norm2_part)
    made = backward(n_tp, n_exp, slots, whole, prefix, all_rows, (w_gate_up, w_down))
    got, summed, routed, norms, all_rows = made[:5]
    gate_up_grad, down_grad, pair_grad, query_grad, out_grad, router_grad, input_grad, layer_out = (
        expert_grads(
            all_rows,
            w_gate_up,
            w_down,
            made[5:],
            (summed, routed, got, layer),
            slots,
            experts,
        )
    )
    norms = norms.reshape(2, D)
    return (
        layer_out,
        input_grad,
        norms[0],
        query_grad,
        pair_grad,
        out_grad,
        norms[1],
        router_grad.T,
        gate_up_grad,
        down_grad,
    )


def solution(mesh):
    return jax.shard_map(
        functools.partial(local, mesh.shape["exp"], mesh.shape["tp"]),
        mesh=mesh,
        in_specs=(
            P(("exp", "tp"), None),
            P(),
            P(None, "tp"),
            P(None, "tp", None),
            P("tp", None),
            P(),
            P(),
            P("exp", None, None),
            P("exp", None, None),
            P(("exp", "tp"), None),
            P("exp"),
            P(("exp", "tp"), None),
        ),
        out_specs=(
            P(("exp", "tp"), None),
            P(("exp", "tp"), None),
            P(),
            P(None, "tp"),
            P(None, "tp", None),
            P("tp", None),
            P(),
            P(),
            P("exp", None, None),
            P("exp", None, None),
        ),
        check_vma=False,
    )
```
